32 devices in a mesh: shard: 4 (over y, core), ctx: 2 (over x), tp: 4 (over z).
Axes of the slice: x: 2, y: 2, z: 4, core: 2. Of those that a mesh axis runs over, the one named last changes fastest.
Arguments:
- inputs: bfloat16 [4, 768, 1024], P('shard', ('ctx', 'tp')), may hold values from -6 to 6
- cotangent: bfloat16 [4, 768, 1024], P('shard', ('ctx', 'tp')), may hold values from -6 to 6
- lengths: int32 [4], P('shard'), may hold values from 576 to 768, as said below
- buckets: int32 [73], replicated, may hold values from 0 to 72, each once
- ffn1_in: bfloat16 [1024, 4096], P(('shard', 'ctx'), 'tp'), may hold values from -0.1875 to 0.1875
- ffn1_out: bfloat16 [1024, 4096], P(('shard', 'ctx'), 'tp'), may hold values from -0.25 to 0.25
- norm_gains: bfloat16 [1024, 5], P(('shard', 'ctx')), may hold values from 0.5 to 1.5
- norm_biases: bfloat16 [1024, 5], P(('shard', 'ctx')), may hold values from -1.5 to 1.5
- qkv_weight: bfloat16 [1024, 3, 1024], P(('shard', 'ctx'), None, 'tp'), may hold values from -0.1875 to 0.1875
- attn_out: bfloat16 [1024, 1024], P(('shard', 'ctx'), 'tp'), may hold values from -0.5 to 0.5
- distance: bfloat16 [64, 73], P(('shard', 'ctx')), may hold values from -6 to 6
- glu_in: bfloat16 [1024, 2, 1024], P(('shard', 'ctx'), None, 'tp'), may hold values from -0.1875 to 0.1875
- depthwise: bfloat16 [1024, 31], P(('tp', 'shard', 'ctx')), may hold values from -1 to 1
- conv_gain: bfloat16 [1024], P(('tp', 'shard', 'ctx')), may hold values from 0.5 to 1.5
- conv_bias: bfloat16 [1024], P(('tp', 'shard', 'ctx')), may hold values from -1.5 to 1.5
- conv_out: bfloat16 [1024, 1024], P(('shard', 'ctx'), 'tp'), may hold values from -0.25 to 0.25
- ffn2_in: bfloat16 [1024, 4096], P(('shard', 'ctx'), 'tp'), may hold values from -0.1875 to 0.1875
- ffn2_out: bfloat16 [1024, 4096], P(('shard', 'ctx'), 'tp'), may hold values from -0.25 to 0.25
Outputs:
- activations: bfloat16 [4, 768, 1024], P('shard', ('ctx', 'tp'))
- input_grad: float32 [4, 768, 1024], P('shard', ('ctx', 'tp'))
- grad_ffn1_in: float32 [1024, 4096], P(('shard', 'ctx'), 'tp')
- grad_ffn1_out: float32 [1024, 4096], P(('shard', 'ctx'), 'tp')
- grad_norm_gains: float32 [1024, 5], P(('shard', 'ctx'))
- grad_norm_biases: float32 [1024, 5], P(('shard', 'ctx'))
- grad_qkv_weight: float32 [1024, 3, 1024], P(('shard', 'ctx'), None, 'tp')
- grad_attn_out: float32 [1024, 1024], P(('shard', 'ctx'), 'tp')
- grad_distance: float32 [64, 73], P(('shard', 'ctx'))
- grad_glu_in: float32 [1024, 2, 1024], P(('shard', 'ctx'), None, 'tp')
- grad_depthwise: float32 [1024, 31], P(('tp', 'shard', 'ctx'))
- grad_conv_gain: float32 [1024], P(('tp', 'shard', 'ctx'))
- grad_conv_bias: float32 [1024], P(('tp', 'shard', 'ctx'))
- grad_conv_out: float32 [1024, 1024], P(('shard', 'ctx'), 'tp')
- grad_ffn2_in: float32 [1024, 4096], P(('shard', 'ctx'), 'tp')
- grad_ffn2_out: float32 [1024, 4096], P(('shard', 'ctx'), 'tp')
The draws below stay inside these ranges and needn't reach their ends.
Inputs may be any that keep to these rules, and one draw needn't show every extreme that they name: `lengths`: one clip has all 768 frames valid and one clip has exactly 576. `buckets`: each row of the distance table serves exactly one offset.
All inputs are finite; a program needn't handle non-finite values.
Results may differ from the reference program's by a relative error of at most 0.034.
Values may be sent and summed in bfloat16 or wider, within the bound.
No kernel may reach another device: no remote copies, remote signals or barrier semaphores. Data moves between devices by JAX's collectives and lax.ppermute only.
A program may use at most 128 MiB of HBM per device.

```python
import jax
import jax.numpy as jnp
from jax import lax

D = 1024
FF = 4096
HEADS = 16
HD = 64
KERNEL = 31
LEFT = 64
SPAN = 73
FRAME_DEV = 384
FRAMES = 768
CLIPS = 4


def draw_lengths(key, part):
    key = jax.random.fold_in(key, 11)
    fewest = FRAMES - FRAME_DEV // 2
    key_values, key_places = jax.random.split(key)
    values = jax.random.randint(key_values, (CLIPS,), fewest, FRAMES + 1)
    places = jax.random.permutation(key_places, CLIPS)
    values = values.at[places[0]].set(FRAMES)
    values = values.at[places[1]].set(fewest)
    return values.astype(jnp.int32)


def with_spikes(values, rng, source, target, parts, factor):
    owner, partner = [(jnp.arange(values.shape[axis_at]) // (values.shape[axis_at] // parts)).reshape([-1 if axis == axis_at else 1 for axis in range(values.ndim)]) for axis_at in (source, target)]
    chosen = jax.random.permutation(rng, parts)[partner]
    strong = (owner == chosen) | (owner == (partner + parts // 2) % parts)
    return jnp.where(strong, factor * values, values)


def shard_levels(own_key, shape, cuts, smallest, largest):
    factor_of = 1.0
    for position, parts in cuts:
        draws = jax.random.uniform(jax.random.fold_in(jax.random.fold_in(own_key, 6), position), (parts,), jnp.float32, smallest / len(cuts), largest / len(cuts))
        factor_of = factor_of * jnp.repeat(jnp.exp(draws), shape[position] // parts).reshape((-1,) + (1,) * (len(shape) - 1 - position))
    return factor_of


def scatter_about(key, shape, width, most, pieces=(), kind=jnp.bfloat16):
    level = shard_levels(key, shape, pieces, -0.22, 0.18) if pieces else 1.0
    drawn = jax.random.normal(key, shape, jnp.float32) * width * level
    return jnp.minimum(jnp.maximum(drawn, -most), most).astype(kind)


def noise_with(rng, shape, scale, limit, cuts, heavy, kind=jnp.bfloat16):
    drawn = scale * jax.random.normal(rng, shape, jnp.float32)
    if cuts:
        drawn = drawn * shard_levels(rng, shape, cuts, -0.22, 0.18)
    return jnp.clip(with_spikes(drawn, jax.random.fold_in(rng, 3), *heavy), -limit, limit).astype(kind)


def setup_inputs(seed: int = 0) -> dict:
    streams_of = jax.random.split(jax.random.key(seed), 19)
    return {
        "inputs": scatter_about(streams_of[0], (CLIPS, FRAMES, D), 1.0, 6.0, ((0, 4), (1, 8))),
        "cotangent": noise_with(streams_of[1], (CLIPS, FRAMES, D), 1.0, 6.0, ((0, 4), (1, 8)), (0, 2, 4, 2.0)),
        "lengths": draw_lengths(jax.random.fold_in(streams_of[18], 71), 0),
        "buckets": jax.random.permutation(streams_of[3], SPAN).astype(jnp.int32),
        "ffn1_in": scatter_about(streams_of[4], (D, FF), D ** -0.5, 0.1875, ((0, 8), (1, 4))),
        "ffn1_out": scatter_about(streams_of[5], (D, FF), (FF // 8) ** -0.5, 0.25, ((0, 8), (1, 4))),
        "norm_gains": jnp.clip(1.0 + 0.1 * jax.random.normal(streams_of[6], (D, 5), jnp.float32), 0.5, 1.5).astype(jnp.bfloat16),
        "norm_biases": scatter_about(streams_of[7], (D, 5), 0.3, 1.5, ((0, 8),)),
        "qkv_weight": scatter_about(streams_of[8], (D, 3, D), D ** -0.5, 0.1875, ((0, 8), (2, 4))),
        "attn_out": scatter_about(streams_of[9], (D, D), (D // 8) ** -0.5, 0.5, ((0, 8), (1, 4))),
        "distance": scatter_about(streams_of[10], (HD, SPAN), 1.0, 6.0, ((0, 8),)),
        "glu_in": scatter_about(streams_of[11], (D, 2, D), D ** -0.5, 0.1875, ((0, 8), (2, 4))),
        "depthwise": scatter_about(streams_of[12], (D, KERNEL), KERNEL ** -0.5, 1.0, ((0, 32),)),
        "conv_gain": jnp.clip(1.0 + 0.1 * jax.random.normal(streams_of[13], (D,), jnp.float32), 0.5, 1.5).astype(jnp.bfloat16),
        "conv_bias": scatter_about(streams_of[14], (D,), 0.3, 1.5, ((0, 32),)),
        "conv_out": scatter_about(streams_of[15], (D, D), (D // 2) ** -0.5, 0.25, ((0, 8), (1, 4))),
        "ffn2_in": scatter_about(streams_of[16], (D, FF), D ** -0.5, 0.1875, ((0, 8), (1, 4))),
        "ffn2_out": scatter_about(streams_of[17], (D, FF), (FF // 8) ** -0.5, 0.25, ((0, 8), (1, 4))),
    }


@jax.custom_vjp
def low(v):
    return lax.optimization_barrier(v.astype(jnp.bfloat16)).astype(jnp.float32)

@jax.custom_vjp
def low_back(v):
    return v

def low_keep(v):
    return (low(v), None)

def low_pass(kept, grad):
    return (grad,)

def back_keep(v):
    return (v, None)

def back_low(kept, grad):
    return (low(grad),)
low.defvjp(low_keep, low_pass)
low_back.defvjp(back_keep, back_low)
EPSILON = 1e-05
MASKED = -1e+30
HIGHEST = lax.Precision.HIGHEST

def matmul(left, right):
    return jnp.dot(left, right, precision=HIGHEST)

def layer_norm(stream, gain, offset):
    centre = stream - lax.optimization_barrier(jnp.mean(stream, axis=-1, keepdims=True))
    spread = lax.optimization_barrier(jnp.mean(centre * centre, axis=-1, keepdims=True))
    return centre * lax.rsqrt(spread + EPSILON) * gain + offset

def skewed(relative, columns):
    height = relative.shape[0]
    padded = jnp.pad(relative, ((0, 0), (0, columns + 1 - relative.shape[1])))
    return padded.reshape(-1)[:height * columns].reshape(height, columns)

def feed_forward(normed, weight_in, weight_out):
    hidden = low(normed)
    before = low_back(matmul(hidden, weight_in))
    active = low(jax.nn.silu(before))
    return low_back(matmul(active, weight_out.T))

def head_attention(query_rows, key_rows, value_rows, rel_table, in_band, allowed):
    columns = key_rows.shape[0]
    scores = (matmul(query_rows, key_rows.T) + skewed(matmul(query_rows, rel_table), columns)) * HD ** (-0.5)
    scores = low_back(scores)
    masked = jnp.where(allowed, scores, MASKED)
    raised = jnp.where(in_band, jnp.exp(masked - lax.optimization_barrier(jnp.max(masked, axis=-1, keepdims=True))), 0.0)
    weights = low(raised / lax.optimization_barrier(jnp.sum(raised, axis=-1, keepdims=True)))
    return matmul(weights, value_rows)

def attention(normed, weight_qkv, weight_out, distance_table, selector, in_band, allowed):
    frame_count = normed.shape[0]
    hidden = low(normed)
    project = low(low_back(jnp.einsum('fd,dkc->fkc', hidden, weight_qkv, precision=HIGHEST)))
    border = ((LEFT, LEFT), (0, 0))
    query_heads = project[:, 0].reshape(frame_count, HEADS, HD).transpose(1, 0, 2)
    key_heads = jnp.pad(project[:, 1], border).reshape(frame_count + 2 * LEFT, HEADS, HD).transpose(1, 0, 2)
    value_heads = jnp.pad(project[:, 2], border).reshape(frame_count + 2 * LEFT, HEADS, HD).transpose(1, 0, 2)
    rel_table = matmul(distance_table, selector)

    def one_head(triple):
        return head_attention(triple[0], triple[1], triple[2], rel_table, in_band, allowed)
    context = lax.map(jax.checkpoint(one_head), (query_heads, key_heads, value_heads))
    context = low(low_back(context.transpose(1, 0, 2).reshape(frame_count, HEADS * HD)))
    return low_back(matmul(context, weight_out.T))

def convolve(normed, weight_glu, weight_depth, conv_scale, conv_shift, weight_out, live_rows):
    frame_count = normed.shape[0]
    hidden = low(normed)
    halves = low_back(jnp.einsum('fd,dkc->kfc', hidden, weight_glu, precision=HIGHEST))
    gated = low(halves[0] * jax.nn.sigmoid(halves[1]) * live_rows)
    padded = jnp.pad(gated, ((KERNEL - 1, 0), (0, 0)))
    mixed = padded[0:frame_count] * weight_depth[:, 0]
    for offset in range(1, KERNEL):
        mixed = mixed + padded[offset:offset + frame_count] * weight_depth[:, offset]
    centre_mean = lax.optimization_barrier(jnp.mean(mixed, axis=-1, keepdims=True))
    square_mean = lax.optimization_barrier(jnp.mean(mixed * mixed, axis=-1, keepdims=True))
    normal = (mixed - centre_mean) * lax.rsqrt(square_mean - centre_mean * centre_mean + EPSILON)
    active = low(jax.nn.silu(normal * conv_scale + conv_shift))
    return low_back(matmul(active, weight_out.T))

def layer(stream, params, live_rows, in_band, allowed, selector):
    ffn1_in, ffn1_out, norm_gains, norm_biases, qkv_weight, attn_out, distance, glu_in, depthwise, conv_gain, conv_bias, conv_out, ffn2_in, ffn2_out = params
    stream_one = stream + 0.5 * feed_forward(layer_norm(stream, norm_gains[:, 0], norm_biases[:, 0]), ffn1_in, ffn1_out)
    stream_two = stream_one + attention(layer_norm(stream_one, norm_gains[:, 1], norm_biases[:, 1]), qkv_weight, attn_out, distance, selector, in_band, allowed)
    stream_three = stream_two + convolve(layer_norm(stream_two, norm_gains[:, 2], norm_biases[:, 2]), glu_in, depthwise, conv_gain, conv_bias, conv_out, live_rows)
    stream_four = stream_three + 0.5 * feed_forward(layer_norm(stream_three, norm_gains[:, 3], norm_biases[:, 3]), ffn2_in, ffn2_out)
    return layer_norm(stream_four, norm_gains[:, 4], norm_biases[:, 4])

def reference(inputs, cotangent, lengths, buckets, ffn1_in, ffn1_out, norm_gains, norm_biases, qkv_weight, attn_out, distance, glu_in, depthwise, conv_gain, conv_bias, conv_out, ffn2_in, ffn2_out):
    weights = tuple((weight.astype(jnp.float32) for weight in (ffn1_in, ffn1_out, norm_gains, norm_biases, qkv_weight, attn_out, distance, glu_in, depthwise, conv_gain, conv_bias, conv_out, ffn2_in, ffn2_out)))
    selector = (jnp.arange(SPAN, dtype=jnp.int32)[:, None] == buckets[None, :]).astype(jnp.float32)
    row_index = jnp.arange(FRAMES, dtype=jnp.int32)[:, None]
    ext_index = jnp.arange(FRAMES + 2 * LEFT, dtype=jnp.int32)[None, :]
    offsets = ext_index - row_index
    in_band = (offsets >= 0) & (offsets < SPAN)
    key_frame = ext_index - LEFT

    def one_clip(totals, clip_item):
        clip_rows, clip_grad, length = clip_item
        live_rows = (row_index < length).astype(jnp.float32)
        allowed = in_band & (key_frame >= 0) & (key_frame < length)
        outputs, pullback = jax.vjp(lambda clip_in, params: layer(clip_in, params, live_rows, in_band, allowed, selector), clip_rows.astype(jnp.float32), weights)
        row_grad, weight_grads = pullback(clip_grad.astype(jnp.float32))
        totals = tuple((summed + fresh for summed, fresh in zip(totals, weight_grads)))
        return (totals, (outputs.astype(jnp.bfloat16), row_grad))
    starting = tuple((jnp.zeros(weight.shape, jnp.float32) for weight in weights))
    totals, (activations, input_grad) = lax.scan(one_clip, starting, (inputs, cotangent, lengths))
    return (activations, input_grad, totals[0], totals[1], totals[2], totals[3], totals[4], totals[5], totals[6], totals[7], totals[8], totals[9], totals[10], totals[11], totals[12], totals[13])
```

```python
import jax
import jax.numpy as jnp
from jax import lax
from jax.sharding import PartitionSpec as P

D = 1024
HD = 64
KERNEL = 31
LEFT = 64
SPAN = 73


EPSILON = 1e-05
MASKED = -1e30


def extended_2(block, sides, width):
    for axis, dim in sides:
        count = lax.axis_size(axis)
        forward = [(i, i + 1) for i in range(count - 1)]
        backward = [(target, source) for source, target in forward]
        low = lax.ppermute(
            lax.slice_in_dim(block, block.shape[dim] - width, None, axis=dim), axis, forward
        )
        high = lax.ppermute(lax.slice_in_dim(block, 0, width, axis=dim), axis, backward)
        block = jnp.concatenate([low, block, high], axis=dim)
    return block


def from_behind(value, axis, steps):
    count = lax.axis_size(axis)
    initial, last = (max(0, -steps), min(count, count - steps))
    return lax.ppermute(value, axis, [(source, source + steps) for source in range(initial, last)])


def product(left, right):
    return jnp.dot(left, right, preferred_element_type=jnp.float32)


def product_nt(left, right):
    return lax.dot_general(
        left, right, (((1,), (1,)), ((), ())), preferred_element_type=jnp.float32
    )


def product_tn(left, right):
    return lax.dot_general(
        left, right, (((0,), (0,)), ((), ())), preferred_element_type=jnp.float32
    )


def silu_slope(values):
    logistic = jax.nn.sigmoid(values)
    return logistic * (1.0 + values * (1.0 - logistic))


def norm_rows(stream, gain, offset):
    centre = stream - jnp.mean(stream, axis=-1, keepdims=True)
    inverse = lax.rsqrt(jnp.mean(centre * centre, axis=-1, keepdims=True) + EPSILON)
    normal = centre * inverse
    return (normal * gain + offset, normal, inverse)


def norm_back(upstream, normal, inverse, gain):
    scaled = upstream * gain
    inward = inverse * (
        scaled
        - jnp.mean(scaled, axis=-1, keepdims=True)
        - normal * jnp.mean(scaled * normal, axis=-1, keepdims=True)
    )
    return (inward, jnp.sum(upstream * normal, axis=0), jnp.sum(upstream, axis=0))


def skewed(relative, columns):
    height = relative.shape[0]
    padded = jnp.pad(relative, ((0, 0), (0, columns + 1 - relative.shape[1])))
    return padded.reshape(-1)[: height * columns].reshape(height, columns)


def unskewed(grid, span_cols):
    height, columns = grid.shape
    flat = jnp.pad(grid.reshape(-1), (0, height))
    return flat.reshape(height, columns + 1)[:, :span_cols]


def gather_pair(couple):
    return (
        lax.all_gather(couple[0], ("shard", "ctx"), axis=0, tiled=True),
        lax.all_gather(couple[1], ("shard", "ctx"), axis=0, tiled=True),
    )


def gather_five(bundle):
    return (
        lax.all_gather(bundle[0], ("shard", "ctx"), axis=0, tiled=True),
        lax.all_gather(bundle[1], ("shard", "ctx"), axis=0, tiled=True),
        lax.all_gather(bundle[2], ("shard", "ctx"), axis=0, tiled=True),
        lax.all_gather(bundle[3], ("shard", "ctx"), axis=0, tiled=True),
        lax.all_gather(bundle[4], ("shard", "ctx"), axis=0, tiled=True),
    )


def settle_wide(value):
    count = lax.axis_size("shard") * lax.axis_size("ctx")
    pieces = value.astype(jnp.bfloat16).reshape((count, value.shape[0] // count) + value.shape[1:])
    pieces = lax.all_to_all(pieces, ("shard", "ctx"), 0, 0)
    return jnp.sum(pieces.astype(jnp.float32), axis=0)


def settle_narrow(values):
    count = lax.axis_size("shard") * lax.axis_size("ctx")
    flat = jnp.concatenate([v.reshape(count, -1) for v in values], axis=1)
    summed = jnp.sum(lax.all_to_all(flat, ("shard", "ctx"), 0, 0), axis=0)
    out, start = [], 0
    for v in values:
        size = v.size // count
        out.append(summed[start : start + size].reshape((v.shape[0] // count,) + v.shape[1:]))
        start += size
    return out


def settle_pair(couple):
    return (settle_wide(couple[0]), settle_wide(couple[1]))


def settle_conv(bundle):
    small = settle_narrow((bundle[1], bundle[2], bundle[3]))
    return (settle_wide(bundle[0]), *small, settle_wide(bundle[4]))


def settle_attn(bundle):
    small = settle_narrow((bundle[0], bundle[1], bundle[4]))
    return (small[0], small[1], settle_wide(bundle[2]), settle_wide(bundle[3]), small[2])


def widen(stream_rows):
    return lax.all_gather(stream_rows, "tp", axis=0, tiled=True)


def narrow(partial_value):
    count = lax.axis_size("tp")
    pieces = partial_value.astype(jnp.bfloat16).reshape(
        count, partial_value.shape[0] // count, partial_value.shape[1]
    )
    return jnp.sum(lax.all_to_all(pieces, "tp", 0, 0).astype(jnp.float32), axis=0)


def widen_grad(stream_rows):
    return lax.all_gather(stream_rows, "tp", axis=0, tiled=True)


def narrow_grad(partial_value):
    count = lax.axis_size("tp")
    pieces = partial_value.astype(jnp.bfloat16).reshape(
        count, partial_value.shape[0] // count, partial_value.shape[1]
    )
    return jnp.sum(lax.all_to_all(pieces, "tp", 0, 0).astype(jnp.float32), axis=0)


def sum_over_tp(couple):
    return lax.psum((couple[0], couple[1]), "tp")


def head_forward(query_rows, key_rows, value_rows, rel_table, setting):
    columns = key_rows.shape[0]
    scores = (
        product_nt(query_rows, key_rows) + skewed(product(query_rows, rel_table), columns)
    ) * setting["scaling"]
    masked = jnp.where(setting["allowed"], scores, MASKED)
    ceiling = jnp.max(masked, axis=-1, keepdims=True)
    raised = jnp.where(setting["in_band"], jnp.exp(masked - ceiling), 0.0)
    denominator = jnp.sum(raised, axis=-1, keepdims=True)
    weights = (raised / denominator).astype(jnp.bfloat16)
    return (product(weights, value_rows), ceiling, denominator)


def head_backward(
    query_rows, key_rows, value_rows, ceiling, denominator, upstream, rel_table, setting
):
    columns = key_rows.shape[0]
    span_cols = rel_table.shape[1]
    scores = (
        product_nt(query_rows, key_rows) + skewed(product(query_rows, rel_table), columns)
    ) * setting["scaling"]
    masked = jnp.where(setting["allowed"], scores, MASKED)
    chance = jnp.where(setting["in_band"], jnp.exp(masked - ceiling), 0.0) / denominator
    weights = chance.astype(jnp.bfloat16)
    d_chance = product_nt(upstream, value_rows)
    d_value = product_tn(weights, upstream)
    inner_sum = jnp.sum(d_chance * chance, axis=-1, keepdims=True)
    d_scores = jnp.where(setting["allowed"], chance * (d_chance - inner_sum), 0.0).astype(
        jnp.bfloat16
    )
    d_relative = unskewed(d_scores, span_cols)
    d_query = (product(d_scores, key_rows) + product_nt(d_relative, rel_table)) * setting["scaling"]
    d_key = product_tn(d_scores, query_rows) * setting["scaling"]
    d_table = product_tn(query_rows, d_relative) * setting["scaling"]
    return (d_query, d_key, d_value, d_table)


def depth_mix(extended, kernel_taps, height):
    mixed = extended[0:height] * kernel_taps[:, 0]
    for offset in range(1, kernel_taps.shape[1]):
        mixed = mixed + extended[offset : offset + height] * kernel_taps[:, offset]
    return mixed


def ffn_forward(stream, gain, offset, weight_in, weight_out):
    normed, normal, inverse = norm_rows(stream, gain, offset)
    hidden = widen(normed.astype(jnp.bfloat16))
    before = product(hidden, weight_in)
    active = jax.nn.silu(before).astype(jnp.bfloat16)
    result = stream + 0.5 * narrow(product_nt(active, weight_out))
    return (result, (normal, inverse, hidden, before, active))


def ffn_backward(d_stream, gain, stored_ffn, weight_in, weight_out):
    normal, inverse, hidden, before, active = stored_ffn
    d_branch = widen_grad((0.5 * d_stream).astype(jnp.bfloat16))
    d_active = product(d_branch, weight_out)
    grad_out = product_tn(d_branch, active)
    d_before = (d_active * silu_slope(before)).astype(jnp.bfloat16)
    grad_in = product_tn(hidden, d_before)
    d_normed = narrow_grad(product_nt(d_before, weight_in))
    d_input, d_gain, d_offset = norm_back(d_normed, normal, inverse, gain)
    return (d_stream + d_input, d_gain, d_offset, grad_in, grad_out)


def attn_forward(stream, gain, offset, qkv_all, attn_all, table_all, setting):
    normed, normal, inverse = norm_rows(stream, gain, offset)
    hidden = widen(normed.astype(jnp.bfloat16))
    height = hidden.shape[0]
    channels = qkv_all.shape[2]
    local_heads = channels // HD
    project = jnp.einsum("fd,dkc->fkc", hidden, qkv_all, preferred_element_type=jnp.float32).astype(
        jnp.bfloat16
    )
    key_value = project[:, 1:].reshape(height, 2 * channels)
    widened = extended_2(key_value, (("ctx", 0),), LEFT)
    columns = widened.shape[0]
    query_heads = project[:, 0].reshape(height, local_heads, HD).transpose(1, 0, 2)
    key_heads = widened[:, :channels].reshape(columns, local_heads, HD).transpose(1, 0, 2)
    value_heads = widened[:, channels:].reshape(columns, local_heads, HD).transpose(1, 0, 2)
    rel_table = product(table_all, setting["selector"]).astype(jnp.bfloat16)

    def one_head(triple):
        return head_forward(triple[0], triple[1], triple[2], rel_table, setting)

    context, ceiling, denominator = lax.map(one_head, (query_heads, key_heads, value_heads))
    context = context.transpose(1, 0, 2).reshape(height, channels).astype(jnp.bfloat16)
    result = stream + narrow(product_nt(context, attn_all))
    return (
        result,
        (
            normal,
            inverse,
            hidden,
            query_heads,
            key_heads,
            value_heads,
            ceiling,
            denominator,
            context,
            rel_table,
        ),
    )


def attn_backward(d_stream, gain, stored_attn, qkv_all, attn_all, setting):
    (
        normal,
        inverse,
        hidden,
        query_heads,
        key_heads,
        value_heads,
        ceiling,
        denominator,
        context,
        rel_table,
    ) = stored_attn
    height = hidden.shape[0]
    channels = context.shape[1]
    local_heads = query_heads.shape[0]
    columns = key_heads.shape[1]
    d_branch = widen_grad(d_stream.astype(jnp.bfloat16))
    grad_out = product_tn(d_branch, context)
    d_context = product(d_branch, attn_all).astype(jnp.bfloat16)
    d_heads = d_context.reshape(height, local_heads, HD).transpose(1, 0, 2)

    def one_head(bundle):
        return head_backward(
            bundle[0], bundle[1], bundle[2], bundle[3], bundle[4], bundle[5], rel_table, setting
        )

    d_query, d_key, d_value, d_table = lax.map(
        one_head, (query_heads, key_heads, value_heads, ceiling, denominator, d_heads)
    )
    d_pairs = jnp.concatenate(
        [
            d_key.transpose(1, 0, 2).reshape(columns, channels),
            d_value.transpose(1, 0, 2).reshape(columns, channels),
        ],
        1,
    )
    outer_rims = jnp.concatenate([d_pairs[:LEFT], d_pairs[LEFT + height :]], 0)
    returned = extended_2(outer_rims.astype(jnp.bfloat16), (("ctx", 0),), LEFT).astype(
        outer_rims.dtype
    )
    d_pairs = d_pairs[LEFT : LEFT + height]
    d_pairs = d_pairs + jnp.pad(returned[:LEFT], ((0, height - LEFT), (0, 0)))
    d_pairs = d_pairs + jnp.pad(returned[3 * LEFT :], ((height - LEFT, 0), (0, 0)))
    d_project = jnp.concatenate([d_query.transpose(1, 0, 2).reshape(height, channels), d_pairs], 1)
    d_project = d_project.reshape(height, 3, channels).astype(jnp.bfloat16)
    grad_qkv = jnp.einsum("fd,fkc->dkc", hidden, d_project, preferred_element_type=jnp.float32)
    d_normed = narrow_grad(
        jnp.einsum("fkc,dkc->fd", d_project, qkv_all, preferred_element_type=jnp.float32)
    )
    d_input, d_gain, d_offset = norm_back(d_normed, normal, inverse, gain)
    d_rel = jnp.sum(d_table, axis=0)
    grad_table = jnp.dot(
        d_rel, setting["selector"].astype(jnp.float32).T, precision=lax.Precision.HIGHEST
    )
    return (d_stream + d_input, d_gain, d_offset, grad_qkv, grad_out, grad_table)


def conv_forward(stream, gain, offset, conv_set, setting):
    glu_all, depth_all, scale_all, shift_all, out_all = conv_set
    normed, normal, inverse = norm_rows(stream, gain, offset)
    hidden = widen(normed.astype(jnp.bfloat16))
    height = hidden.shape[0]
    halves = jnp.einsum("fd,dkc->kfc", hidden, glu_all, preferred_element_type=jnp.float32)
    logistic = jax.nn.sigmoid(halves[1])
    gated = (halves[0] * logistic * setting["live_rows"]).astype(jnp.bfloat16)
    earlier = from_behind(gated[height - (KERNEL - 1) :], "ctx", 1)
    extended = jnp.concatenate([earlier, gated], 0)
    mixed = depth_mix(extended, depth_all.astype(jnp.float32), height)
    row_sum, square_sum = sum_over_tp((jnp.sum(mixed, axis=1), jnp.sum(mixed * mixed, axis=1)))
    centre_mean = (row_sum / D)[:, None]
    inverse_conv = lax.rsqrt((square_sum / D)[:, None] - centre_mean * centre_mean + EPSILON)
    conv_normal = (mixed - centre_mean) * inverse_conv
    levels = conv_normal * scale_all.astype(jnp.float32) + shift_all.astype(jnp.float32)
    active = jax.nn.silu(levels).astype(jnp.bfloat16)
    result = stream + narrow(product_nt(active, out_all))
    return (
        result,
        (
            normal,
            inverse,
            hidden,
            halves,
            logistic,
            extended,
            conv_normal,
            inverse_conv,
            levels,
            active,
        ),
    )


def conv_backward(d_stream, gain, stored_conv, conv_set, setting):
    glu_all, depth_all, scale_all, shift_all, out_all = conv_set
    (
        normal,
        inverse,
        hidden,
        halves,
        logistic,
        extended,
        conv_normal,
        inverse_conv,
        levels,
        active,
    ) = stored_conv
    height = hidden.shape[0]
    d_branch = widen_grad(d_stream.astype(jnp.bfloat16))
    grad_out = product_tn(d_branch, active)
    d_levels = product(d_branch, out_all) * silu_slope(levels)
    grad_scale = jnp.sum(d_levels * conv_normal, axis=0)
    grad_shift = jnp.sum(d_levels, axis=0)
    scaled = d_levels * scale_all.astype(jnp.float32)
    plain_sum, cross_sum = sum_over_tp(
        (jnp.sum(scaled, axis=1), jnp.sum(scaled * conv_normal, axis=1))
    )
    d_mixed = inverse_conv * (
        scaled - (plain_sum / D)[:, None] - conv_normal * (cross_sum / D)[:, None]
    )
    kernel_taps = depth_all.astype(jnp.float32)
    tap_count = kernel_taps.shape[1]
    d_extended = jnp.zeros((height + tap_count - 1, d_mixed.shape[1]), jnp.float32)
    tap_grads = []
    for offset in range(tap_count):
        d_extended = d_extended + jnp.pad(
            d_mixed * kernel_taps[:, offset], ((offset, tap_count - 1 - offset), (0, 0))
        )
        tap_grads.append(jnp.sum(d_mixed * extended[offset : offset + height], axis=0))
    grad_depth = jnp.stack(tap_grads, axis=1)
    later = from_behind(d_extended[: KERNEL - 1], "ctx", -1)
    d_gated = d_extended[KERNEL - 1 :] + jnp.pad(later, ((height - (KERNEL - 1), 0), (0, 0)))
    d_gated = d_gated * setting["live_rows"]
    d_halves = jnp.stack(
        [d_gated * logistic, d_gated * halves[0] * logistic * (1.0 - logistic)], 0
    ).astype(jnp.bfloat16)
    grad_glu = jnp.einsum("fd,kfc->dkc", hidden, d_halves, preferred_element_type=jnp.float32)
    d_normed = narrow_grad(
        jnp.einsum("kfc,dkc->fd", d_halves, glu_all, preferred_element_type=jnp.float32)
    )
    d_input, d_gain, d_offset = norm_back(d_normed, normal, inverse, gain)
    return (
        d_stream + d_input,
        d_gain,
        d_offset,
        (grad_glu, grad_depth, grad_scale, grad_shift, grad_out),
    )


def run_forward(stream, weights, setting):
    (
        ffn1_in,
        ffn1_out,
        norm_gains,
        norm_biases,
        qkv_weight,
        attn_out,
        distance,
        glu_in,
        depthwise,
        conv_gain,
        conv_bias,
        conv_out,
        ffn2_in,
        ffn2_out,
    ) = weights
    stored = {}
    gains_all, biases_all, qkv_all, attn_all, table_all = gather_five(
        (norm_gains, norm_biases, qkv_weight, attn_out, distance)
    )
    gains_all = gains_all.astype(jnp.float32)
    biases_all = biases_all.astype(jnp.float32)
    first_in, first_out = gather_pair((ffn1_in, ffn1_out))
    stream, stored["ffn_one"] = ffn_forward(
        stream, gains_all[:, 0], biases_all[:, 0], first_in, first_out
    )
    stream, stored["attention"] = attn_forward(
        stream, gains_all[:, 1], biases_all[:, 1], qkv_all, attn_all, table_all, setting
    )
    conv_set = gather_five((glu_in, depthwise, conv_gain, conv_bias, conv_out))
    stream, stored["convolution"] = conv_forward(
        stream, gains_all[:, 2], biases_all[:, 2], conv_set, setting
    )
    second_in, second_out = gather_pair((ffn2_in, ffn2_out))
    stream, stored["ffn_two"] = ffn_forward(
        stream, gains_all[:, 3], biases_all[:, 3], second_in, second_out
    )
    result, final_normal, final_inverse = norm_rows(stream, gains_all[:, 4], biases_all[:, 4])
    stored["final_normal"] = final_normal
    stored["final_inverse"] = final_inverse
    stored["gains"] = gains_all
    stored["first_in"] = first_in
    stored["first_out"] = first_out
    stored["qkv_all"] = qkv_all
    stored["attn_all"] = attn_all
    stored["conv_set"] = conv_set
    stored["second_in"] = second_in
    stored["second_out"] = second_out
    return (result, stored)


def body(
    inputs,
    cotangent,
    lengths,
    buckets,
    ffn1_in,
    ffn1_out,
    norm_gains,
    norm_biases,
    qkv_weight,
    attn_out,
    distance,
    glu_in,
    depthwise,
    conv_gain,
    conv_bias,
    conv_out,
    ffn2_in,
    ffn2_out,
):
    stream = inputs[0].astype(jnp.float32)
    height = stream.shape[0] * lax.axis_size("tp")
    first_frame = lax.axis_index("ctx") * height
    length = lengths[0]
    frame_ids = first_frame + jnp.arange(height, dtype=jnp.int32)
    live_rows = (frame_ids < length).astype(jnp.float32)[:, None]
    ext_ids = jnp.arange(height + 2 * LEFT, dtype=jnp.int32)
    offsets = ext_ids[None, :] - jnp.arange(height, dtype=jnp.int32)[:, None]
    key_frames = (first_frame - LEFT + ext_ids)[None, :]
    in_band = (offsets >= 0) & (offsets < SPAN)
    allowed = in_band & (key_frames >= 0) & (key_frames < length)
    selector = (jnp.arange(SPAN, dtype=jnp.int32)[:, None] == buckets[None, :]).astype(jnp.bfloat16)
    setting = {
        "live_rows": live_rows,
        "in_band": in_band,
        "allowed": allowed,
        "selector": selector,
        "scaling": HD ** (-0.5),
    }
    weights = (
        ffn1_in,
        ffn1_out,
        norm_gains,
        norm_biases,
        qkv_weight,
        attn_out,
        distance,
        glu_in,
        depthwise,
        conv_gain,
        conv_bias,
        conv_out,
        ffn2_in,
        ffn2_out,
    )
    result, stored = run_forward(stream, weights, setting)
    gains_all = stored["gains"]
    d_stream, gain_four, bias_four = norm_back(
        cotangent[0].astype(jnp.float32),
        stored["final_normal"],
        stored["final_inverse"],
        gains_all[:, 4],
    )
    d_stream, gain_three, bias_three, grad_in_two, grad_out_two = ffn_backward(
        d_stream, gains_all[:, 3], stored["ffn_two"], stored["second_in"], stored["second_out"]
    )
    ffn_two_grads = settle_pair((grad_in_two, grad_out_two))
    d_stream, gain_two, bias_two, conv_grads = conv_backward(
        d_stream, gains_all[:, 2], stored["convolution"], stored["conv_set"], setting
    )
    conv_settled = settle_conv(conv_grads)
    d_stream, gain_one, bias_one, grad_qkv, grad_attn, grad_table = attn_backward(
        d_stream,
        gains_all[:, 1],
        stored["attention"],
        stored["qkv_all"],
        stored["attn_all"],
        setting,
    )
    d_stream, gain_zero, bias_zero, grad_in_one, grad_out_one = ffn_backward(
        d_stream, gains_all[:, 0], stored["ffn_one"], stored["first_in"], stored["first_out"]
    )
    ffn_one_grads = settle_pair((grad_in_one, grad_out_one))
    grad_gains = jnp.stack([gain_zero, gain_one, gain_two, gain_three, gain_four], axis=1)
    grad_biases = jnp.stack([bias_zero, bias_one, bias_two, bias_three, bias_four], axis=1)
    attn_settled = settle_attn((grad_gains, grad_biases, grad_qkv, grad_attn, grad_table))
    norm_sums, table_sum = sum_over_tp(
        (jnp.stack([attn_settled[0], attn_settled[1]], 0), attn_settled[4])
    )
    return (
        result.astype(jnp.bfloat16)[None],
        d_stream[None],
        ffn_one_grads[0],
        ffn_one_grads[1],
        norm_sums[0],
        norm_sums[1],
        attn_settled[2],
        attn_settled[3],
        table_sum,
        conv_settled[0],
        conv_settled[1],
        conv_settled[2],
        conv_settled[3],
        conv_settled[4],
        ffn_two_grads[0],
        ffn_two_grads[1],
    )


def solution(mesh):
    placed = (
        P("shard", ("ctx", "tp"), None),
        P("shard", ("ctx", "tp"), None),
        P("shard"),
        P(),
        P(("shard", "ctx"), "tp"),
        P(("shard", "ctx"), "tp"),
        P(("shard", "ctx"), None),
        P(("shard", "ctx"), None),
        P(("shard", "ctx"), None, "tp"),
        P(("shard", "ctx"), "tp"),
        P(("shard", "ctx"), None),
        P(("shard", "ctx"), None, "tp"),
        P(("tp", "shard", "ctx"), None),
        P(("tp", "shard", "ctx")),
        P(("tp", "shard", "ctx")),
        P(("shard", "ctx"), "tp"),
        P(("shard", "ctx"), "tp"),
        P(("shard", "ctx"), "tp"),
    )
    return jax.shard_map(
        body,
        mesh=mesh,
        in_specs=placed,
        out_specs=(
            P("shard", ("ctx", "tp"), None),
            P("shard", ("ctx", "tp"), None),
            P(("shard", "ctx"), "tp"),
            P(("shard", "ctx"), "tp"),
            P(("shard", "ctx"), None),
            P(("shard", "ctx"), None),
            P(("shard", "ctx"), None, "tp"),
            P(("shard", "ctx"), "tp"),
            P(("shard", "ctx"), None),
            P(("shard", "ctx"), None, "tp"),
            P(("tp", "shard", "ctx"), None),
            P(("tp", "shard", "ctx")),
            P(("tp", "shard", "ctx")),
            P(("shard", "ctx"), "tp"),
            P(("shard", "ctx"), "tp"),
            P(("shard", "ctx"), "tp"),
        ),
        check_vma=False,
    )
```

```python
import functools

import jax
import jax.numpy as jnp
from jax import lax
from jax.experimental import pallas as pl
from jax.experimental.pallas import tpu as pltpu
from jax.sharding import Mesh
from jax.sharding import PartitionSpec as P

D = 1024
HD = 64
KERNEL = 31
LEFT = 64
RIGHT = 16
SPAN = 73
PAIR = 128
KEYS = 256
EPSILON = 1e-05
MASKED = -1e30
SCALE = HD**-0.5
F32 = jnp.float32
BF16 = jnp.bfloat16


def product(left, right):
    return jnp.dot(left, right, preferred_element_type=F32)


def product_nt(left, right):
    return lax.dot_general(left, right, (((1,), (1,)), ((), ())), preferred_element_type=F32)


def product_tn(left, right):
    return lax.dot_general(left, right, (((0,), (0,)), ((), ())), preferred_element_type=F32)


def silu_slope(values):
    logistic = jax.nn.sigmoid(values)
    return logistic * (1.0 + values * (1.0 - logistic))


def norm_rows(stream, gain, offset):
    centre = stream - jnp.mean(stream, axis=-1, keepdims=True)
    inverse = lax.rsqrt(jnp.mean(centre * centre, axis=-1, keepdims=True) + EPSILON)
    normal = centre * inverse
    return (normal * gain + offset, normal, inverse)


def norm_back(upstream, normal, inverse, gain):
    scaled = upstream * gain
    inward = inverse * (
        scaled
        - jnp.mean(scaled, axis=-1, keepdims=True)
        - normal * jnp.mean(scaled * normal, axis=-1, keepdims=True)
    )
    return (inward, jnp.sum(upstream * normal, axis=0), jnp.sum(upstream, axis=0))


def bits_of(axis):
    count = lax.axis_size(axis)
    return [1 << k for k in range(count.bit_length() - 1)]


def partner(value, axis, mask):
    count = lax.axis_size(axis)
    return lax.ppermute(value, axis, [(i, i ^ mask) for i in range(count)])


def cube_gather(value, axes):
    value = value[None]
    for axis in axes:
        for mask in bits_of(axis):
            value = jnp.concatenate([value, partner(value, axis, mask)], 0)
    return value


def cube_settle(value, axes):
    for axis in reversed(axes):
        for mask in reversed(bits_of(axis)):
            half = value.shape[0] // 2
            arrived = partner(value[half:].astype(BF16), axis, mask)
            value = value[:half].astype(F32) + arrived.astype(F32)
    return value[0]


def cube_flags(axes):
    return [(lax.axis_index(axis) & mask) != 0 for axis in axes for mask in bits_of(axis)]


def crossed(blocks, axes):
    for k, flag in enumerate(cube_flags(axes)):
        blocks = [jnp.where(flag, blocks[i ^ (1 << k)], blocks[i]) for i in range(len(blocks))]
    return blocks


def position(axes, r, x, c):
    index, width = 0, 1
    for axis in axes:
        index += {"row": r, "ctx": x, "core": c}[axis] * width
        width *= lax.axis_size(axis)
    return index


def places(axes):
    rows, ctxs = lax.axis_size("row"), lax.axis_size("ctx")
    return [
        position(axes, r, x, c) for r in range(rows) for x in range(ctxs) for c in range(2)
    ]


def to_cube(value, axes):
    order = places(axes)
    width = value.shape[-1] // len(order)
    blocks = [None] * len(order)
    for k, place in enumerate(order):
        blocks[place] = value[..., k * width : (k + 1) * width]
    return jnp.concatenate(crossed(blocks, axes), -1)


def from_cube(value, axes):
    order = places(axes)
    width = value.shape[-1] // len(order)
    blocks = [value[..., k * width : (k + 1) * width] for k in range(len(order))]
    blocks = crossed(blocks, axes)
    return jnp.concatenate([blocks[place] for place in order], -1)


def stream_order(value):
    rows, ctxs = lax.axis_size("row"), lax.axis_size("ctx")
    width = value.shape[-1] // (rows * ctxs * 2)
    return jnp.concatenate(
        [
            lax.slice_in_dim(value, j * width, (j + 1) * width, axis=value.ndim - 1)
            for r in range(rows)
            for x in range(ctxs)
            for c in range(2)
            for j in [(r * 2 + c) * ctxs + x]
        ],
        -1,
    )


def natural_order(value):
    rows, ctxs = lax.axis_size("row"), lax.axis_size("ctx")
    width = value.shape[-1] // (rows * ctxs * 2)
    return jnp.concatenate(
        [
            lax.slice_in_dim(value, j * width, (j + 1) * width, axis=value.ndim - 1)
            for r in range(rows)
            for c in range(2)
            for x in range(ctxs)
            for j in [(r * ctxs + x) * 2 + c]
        ],
        -1,
    )


def swap_core(value):
    return lax.ppermute(value, "core", [(0, 1), (1, 0)])


def along(value, step):
    count = lax.axis_size("ctx") * lax.axis_size("tp")
    pairs = [(i, i + step) for i in range(count) if 0 <= i + step < count]
    return lax.ppermute(value, ("ctx", "tp"), pairs)


def widen_tp(rows):
    return lax.all_gather(rows, "tp", axis=0, tiled=True)


def narrow_tp(partial_value):
    count = lax.axis_size("tp")
    pieces = partial_value.astype(BF16).reshape(
        count, partial_value.shape[0] // count, partial_value.shape[1]
    )
    return jnp.sum(lax.all_to_all(pieces, "tp", 0, 0).astype(F32), axis=0)


def widen_core(rows):
    return jnp.concatenate([rows, swap_core(rows)], 0)


def narrow_core(partial_value):
    half = partial_value.shape[0] // 2
    arrived = swap_core(partial_value[half:].astype(BF16))
    return partial_value[:half].astype(F32) + arrived.astype(F32)


def pick(flag, pair_value, axis):
    return jnp.where(
        flag,
        lax.index_in_dim(pair_value, 1, axis, keepdims=False),
        lax.index_in_dim(pair_value, 0, axis, keepdims=False),
    )


def core_weights(matrices, second):
    halves = jnp.concatenate(
        [m.reshape(m.shape[0], 2, 1, m.shape[1] // 2) for m in matrices], 2
    )
    rows, count, half = halves.shape[0], halves.shape[2], halves.shape[3]
    own = pick(second, halves, 1)
    other = swap_core(pick(jnp.logical_not(second), halves, 1))
    own = own.reshape(rows, count * half)
    other = other.reshape(rows, count * half)
    both = jnp.concatenate(
        [jnp.where(second, other, own), jnp.where(second, own, other)], 0
    )
    whole = lax.all_gather(both, ("tp", "row", "ctx"), axis=0, tiled=True)
    whole = whole.reshape(lax.axis_size("tp"), D, count * half)
    return [
        jnp.concatenate([whole[z][:, m * half : (m + 1) * half] for z in range(whole.shape[0])], 1)
        for m in range(count)
    ]


def core_settle(grads, second):
    tp = lax.axis_size("tp")
    group = lax.axis_size("row") * lax.axis_size("ctx")
    count, half = len(grads), grads[0].shape[1] // tp
    columns = [g[:, z * half : (z + 1) * half] for z in range(tp) for g in grads]
    packed = jnp.concatenate(columns, 1).astype(BF16)
    packed = packed.reshape(group, D // group, packed.shape[1])
    total = jnp.sum(lax.all_to_all(packed, ("row", "ctx"), 0, 0).astype(F32), axis=0).astype(BF16)
    width = count * half
    stacked = jnp.stack([total[:, z * width : (z + 1) * width] for z in range(tp)], 0)
    total = jnp.sum(lax.all_to_all(stacked, "tp", 0, 0).astype(F32), axis=0)
    total = total.reshape(2, total.shape[0] // 2, count, half)
    own = pick(second, total, 0)
    other = swap_core(pick(jnp.logical_not(second), total, 0).astype(BF16)).astype(F32)
    whole = jnp.concatenate(
        [jnp.where(second, other, own), jnp.where(second, own, other)], 2
    )
    return [whole[:, m] for m in range(count)]


def window(first_ref, lens_ref, clip, height):
    rows = lax.broadcasted_iota(jnp.int32, (height, KEYS), 0)
    lanes = lax.broadcasted_iota(jnp.int32, (height, KEYS), 1)
    offset = lanes - rows
    frame = lanes + (first_ref[0] - LEFT)
    in_band = (offset >= 0) & (offset < SPAN)
    allowed = in_band & (frame >= 0) & (frame < lens_ref[clip])
    return in_band, allowed


def keys_of(left_ref, own_ref, right_ref, clip, height):
    rest = KEYS - LEFT - RIGHT - height
    return jnp.concatenate(
        [
            left_ref[clip],
            own_ref[clip * height : (clip + 1) * height],
            right_ref[clip],
            jnp.zeros((rest, PAIR), BF16),
        ],
        0,
    )


def attend_kernel(
    height, first_ref, lens_ref, q_ref, k_ref, v_ref, kl_ref, vl_ref, kr_ref, vr_ref,
    rel_ref, out_ref, context_ref, chance_ref, branch_ref, total
):
    step = pl.program_id(0)
    odd = lax.broadcasted_iota(jnp.int32, (1, PAIR), 1) >= HD
    for clip in range(2):
        query = q_ref[clip * height : (clip + 1) * height]
        keys = keys_of(kl_ref, k_ref, kr_ref, clip, height)
        values = keys_of(vl_ref, v_ref, vr_ref, clip, height)
        in_band, allowed = window(first_ref, lens_ref, clip, height)
        context = jnp.zeros((height, PAIR), F32)
        for head in range(2):
            mine = odd if head else jnp.logical_not(odd)
            q_head = jnp.where(mine, query, jnp.zeros_like(query))
            relative = product(q_head, rel_ref[...])
            relative = jnp.concatenate([relative, jnp.zeros((height, KEYS - PAIR), F32)], 1)
            relative = pltpu.roll(relative, 0, 1, stride=1, stride_axis=0)
            score = (product_nt(q_head, keys) + relative) * SCALE
            masked = jnp.where(allowed, score, MASKED)
            ceiling = jnp.max(masked, axis=-1, keepdims=True)
            raised = jnp.where(in_band, jnp.exp(masked - ceiling), 0.0)
            chance = raised / jnp.sum(raised, axis=-1, keepdims=True)
            chance_ref[0, clip, head] = chance
            part = product(chance.astype(BF16), values)
            context = jnp.where(mine, part, context)
        context_ref[clip * height : (clip + 1) * height] = context.astype(BF16)
    branch = product_nt(context_ref[...], out_ref[...])

    @pl.when(step == 0)
    def _():
        total[...] = branch

    @pl.when(step > 0)
    def _():
        total[...] += branch

    @pl.when(step == pl.num_programs(0) - 1)
    def _():
        branch_ref[...] = total[...].astype(BF16)


def attend_back_kernel(
    height, first_ref, lens_ref, up_ref, q_ref, k_ref, v_ref, kl_ref, vl_ref, kr_ref, vr_ref,
    rel_ref, out_ref, chance_ref, dq_ref, own_ref, left_ref, right_ref, table_ref
):
    step = pl.program_id(0)
    odd = lax.broadcasted_iota(jnp.int32, (1, PAIR), 1) >= HD
    d_context = product(up_ref[...], out_ref[...]).astype(BF16)
    table = jnp.zeros((PAIR, PAIR), F32)
    flip = (
        lax.broadcasted_iota(jnp.int32, (height, height), 0)
        + lax.broadcasted_iota(jnp.int32, (height, height), 1)
        == height - 1
    ).astype(BF16)
    for clip in range(2):
        query = q_ref[clip * height : (clip + 1) * height]
        upstream = d_context[clip * height : (clip + 1) * height]
        keys = keys_of(kl_ref, k_ref, kr_ref, clip, height)
        values = keys_of(vl_ref, v_ref, vr_ref, clip, height)
        _, allowed = window(first_ref, lens_ref, clip, height)
        d_query = jnp.zeros((height, PAIR), F32)
        d_keys = jnp.zeros((KEYS, PAIR), F32)
        d_values = jnp.zeros((KEYS, PAIR), F32)
        for head in range(2):
            mine = odd if head else jnp.logical_not(odd)
            q_head = jnp.where(mine, query, jnp.zeros_like(query))
            up_head = jnp.where(mine, upstream, jnp.zeros_like(upstream))
            chance = chance_ref[0, clip, head]
            d_chance = product_nt(up_head, values)
            inner = jnp.sum(d_chance * chance, axis=-1, keepdims=True)
            d_score = jnp.where(allowed, chance * (d_chance - inner), 0.0).astype(BF16)
            d_values += product_tn(chance.astype(BF16), up_head)
            d_keys += product_tn(d_score, q_head)
            relative = pltpu.roll(
                product(flip, d_score), KEYS - height + 1, 1, stride=1, stride_axis=0
            )[:, :PAIR].astype(BF16)
            relative = product(flip, relative).astype(BF16)
            part = product(d_score, keys) + product_nt(relative, rel_ref[...])
            d_query = jnp.where(mine, part, d_query)
            table += product_tn(q_head, relative)
        dq_ref[clip * height : (clip + 1) * height] = (d_query * SCALE).astype(BF16)
        for slot, value in ((0, d_keys * SCALE), (1, d_values)):
            left_ref[slot, clip] = value[:LEFT].astype(BF16)
            own_ref[slot, clip] = value[LEFT : LEFT + height]
            right_ref[slot, clip] = value[LEFT + height : LEFT + height + RIGHT].astype(BF16)

    @pl.when(step == 0)
    def _():
        table_ref[...] = table * SCALE

    @pl.when(step > 0)
    def _():
        table_ref[...] += table * SCALE


def attend_specs(height, channels):
    steps = channels // PAIR
    rows = pl.BlockSpec((2 * height, PAIR), lambda z: (0, z))
    k_own = pl.BlockSpec((2 * height, PAIR), lambda z: (0, steps + z))
    v_own = pl.BlockSpec((2 * height, PAIR), lambda z: (0, 2 * steps + z))
    k_left = pl.BlockSpec((2, LEFT, PAIR), lambda z: (0, 0, z))
    v_left = pl.BlockSpec((2, LEFT, PAIR), lambda z: (0, 0, steps + z))
    k_right = pl.BlockSpec((2, RIGHT, PAIR), lambda z: (0, 0, z))
    v_right = pl.BlockSpec((2, RIGHT, PAIR), lambda z: (0, 0, steps + z))
    table = pl.BlockSpec((PAIR, PAIR), lambda z: (0, 0))
    weight = pl.BlockSpec((D, PAIR), lambda z: (0, z))
    scalar = pl.BlockSpec(memory_space=pltpu.SMEM)
    return steps, rows, k_own, v_own, k_left, v_left, k_right, v_right, table, weight, scalar


def attend(first, lens, project, left, right, rel, out_all):
    height, channels = project.shape[0] // 2, project.shape[1] // 3
    steps, rows, k_own, v_own, k_left, v_left, k_right, v_right, table, weight, scalar = (
        attend_specs(height, channels)
    )
    return pl.pallas_call(
        functools.partial(attend_kernel, height),
        grid=(steps,),
        in_specs=[
            scalar, scalar, rows, k_own, v_own, k_left, v_left, k_right, v_right, table, weight
        ],
        out_specs=[
            rows,
            pl.BlockSpec((1, 2, 2, height, KEYS), lambda z: (z, 0, 0, 0, 0)),
            pl.BlockSpec((2 * height, D), lambda z: (0, 0)),
        ],
        out_shape=[
            jax.ShapeDtypeStruct((2 * height, channels), BF16),
            jax.ShapeDtypeStruct((steps, 2, 2, height, KEYS), F32),
            jax.ShapeDtypeStruct((2 * height, D), BF16),
        ],
        scratch_shapes=[pltpu.VMEM((2 * height, D), F32)],
        compiler_params=pltpu.CompilerParams(vmem_limit_bytes=32 << 20),
        name="attend",
    )(first, lens, project, project, project, left, left, right, right, rel, out_all)


def attend_back(first, lens, upstream, project, left, right, rel, out_all, chance):
    height, channels = project.shape[0] // 2, project.shape[1] // 3
    steps, rows, k_own, v_own, k_left, v_left, k_right, v_right, table, weight, scalar = (
        attend_specs(height, channels)
    )
    sided = lambda n: pl.BlockSpec((2, 2, n, PAIR), lambda z: (0, 0, 0, z))
    return pl.pallas_call(
        functools.partial(attend_back_kernel, height),
        grid=(steps,),
        in_specs=[
            scalar, scalar, pl.BlockSpec((2 * height, D), lambda z: (0, 0)), rows, k_own, v_own,
            k_left, v_left, k_right, v_right, table, weight,
            pl.BlockSpec((1, 2, 2, height, KEYS), lambda z: (z, 0, 0, 0, 0)),
        ],
        out_specs=[rows, sided(height), sided(LEFT), sided(RIGHT), table],
        out_shape=[
            jax.ShapeDtypeStruct((2 * height, channels), BF16),
            jax.ShapeDtypeStruct((2, 2, height, channels), F32),
            jax.ShapeDtypeStruct((2, 2, LEFT, channels), BF16),
            jax.ShapeDtypeStruct((2, 2, RIGHT, channels), BF16),
            jax.ShapeDtypeStruct((PAIR, PAIR), F32),
        ],
        compiler_params=pltpu.CompilerParams(vmem_limit_bytes=32 << 20),
        name="attend_back",
    )(
        first, lens, upstream, project, project, project, left, left, right, right, rel,
        out_all, chance,
    )


def ffn_forward(hidden, weight_in, weight_out):
    before = product(hidden, weight_in)
    active = jax.nn.silu(before).astype(BF16)
    return narrow_tp(product_nt(active, weight_out)), before, active


def ffn_backward(d_branch_in, d_branch_out, before, active, hidden, weight_in, weight_out):
    d_active = product(d_branch_out, weight_out)
    d_before = (d_active * silu_slope(before)).astype(BF16)
    d_hidden = product_nt(d_before, weight_in)
    grad_out = product_tn(d_branch_in, active)
    grad_in = product_tn(hidden, d_before)
    return d_hidden, grad_in, grad_out


def settle_wide(value):
    count = lax.axis_size("row") * lax.axis_size("ctx") * 2
    pieces = value.astype(BF16).reshape(count, value.shape[0] // count, value.shape[1])
    pieces = lax.all_to_all(pieces, ("row", "ctx", "core"), 0, 0)
    return jnp.sum(pieces.astype(F32), axis=0)


def settle_cut(value):
    return jnp.sum(lax.all_to_all(value, ("row", "ctx", "core"), 0, 0), axis=0)


IN_AXES = ("row", "ctx", "core")
OUT_AXES = ("ctx", "row", "core")


def body(
    inputs,
    cotangent,
    lengths,
    buckets,
    ffn1_in,
    ffn1_out,
    norm_gains,
    norm_biases,
    qkv_weight,
    attn_out,
    distance,
    glu_in,
    depthwise,
    conv_gain,
    conv_bias,
    conv_out,
    ffn2_in,
    ffn2_out,
):
    rows, ctxs, tp = lax.axis_size("row"), lax.axis_size("ctx"), lax.axis_size("tp")
    group = rows * ctxs * 2
    second = lax.axis_index("core") == 1
    local = ffn1_in.shape[0]
    height = inputs.shape[1]
    first = (lax.axis_index("ctx") * tp + lax.axis_index("tp")) * height
    lens = widen_core(lengths)
    frame_ids = first + jnp.arange(height, dtype=jnp.int32)
    live = (frame_ids[None, :] < lens[:, None]).astype(F32).reshape(2 * height, 1)

    near = stream_order(inputs[0])
    wide_inputs = widen_tp(near)
    one_in = cube_gather(ffn1_in, IN_AXES).reshape(D, -1)
    one_out = cube_gather(ffn1_out, OUT_AXES).reshape(D, -1)

    small = jnp.concatenate(
        [
            norm_gains.T.reshape(-1),
            norm_biases.T.reshape(-1),
            distance.reshape(-1),
            depthwise.T.reshape(-1),
            conv_gain,
            conv_bias,
        ]
    )
    norm_count, table_count = 10 * local, distance.size
    cube = cube_gather(small, ("core", "row", "ctx"))
    blocks = crossed([cube[k] for k in range(group)], ("core", "row", "ctx"))
    order = [
        (x * rows + r) * 2 + c for r in range(rows) for x in range(ctxs) for c in range(2)
    ]
    norms = jnp.concatenate([blocks[k][:norm_count].reshape(10, local) for k in order], 1)
    norms = norms.astype(F32)
    gains, biases = norms[:5], norms[5:]
    natural = [
        (x * rows + r) * 2 + c for r in range(rows) for c in range(2) for x in range(ctxs)
    ]
    table_all = jnp.concatenate(
        [
            blocks[k][norm_count : norm_count + table_count].reshape(-1, SPAN)
            for k in natural
        ],
        0,
    )
    width = conv_gain.shape[0]
    conv_small = jnp.concatenate(
        [blocks[k][norm_count + table_count :].reshape(KERNEL + 2, width) for k in natural], 1
    )
    half = conv_small.shape[1] // 2
    conv_small = jnp.where(second, conv_small[:, half:], conv_small[:, :half])
    conv_cube = cube_gather(conv_small, ("tp",))
    conv_blocks = crossed([conv_cube[k] for k in range(tp)], ("tp",))
    conv_small = jnp.concatenate(conv_blocks, 1).astype(F32)
    taps, conv_scale, conv_shift = conv_small[:KERNEL], conv_small[KERNEL], conv_small[KERNEL + 1]

    wq, wk, wv, w_attn = core_weights(
        [qkv_weight[:, 0], qkv_weight[:, 1], qkv_weight[:, 2], attn_out], second
    )
    qkv_all = jnp.concatenate([wq, wk, wv], 1)
    w_value, w_gate, w_conv = core_weights([glu_in[:, 0], glu_in[:, 1], conv_out], second)
    glu_all = jnp.concatenate([w_value, w_gate], 1)
    two = lax.all_gather(
        jnp.concatenate([ffn2_in, ffn2_out], 1), ("row", "ctx", "core"), axis=0, tiled=True
    )
    two_in, two_out = two[:, : ffn2_in.shape[1]], two[:, ffn2_in.shape[1] :]

    selector = (jnp.arange(SPAN, dtype=jnp.int32)[:, None] == buckets[None, :]).astype(BF16)
    rel = product(table_all, selector).astype(BF16)
    rel = jnp.pad(jnp.concatenate([rel, rel], 0), ((0, 0), (0, PAIR - SPAN)))

    hidden0, _, _ = norm_rows(wide_inputs.astype(F32), gains[0], biases[0])
    hidden0 = to_cube(hidden0.astype(BF16), IN_AXES)
    stream0 = near.astype(F32)
    branch, before0, active0 = ffn_forward(hidden0, one_in, one_out)
    stream1 = stream0 + 0.5 * from_cube(branch, OUT_AXES)

    normed, normal1, inverse1 = norm_rows(stream1, gains[1], biases[1])
    hidden1 = widen_core(normed.astype(BF16))
    project = product(hidden1, qkv_all).astype(BF16)
    channels = qkv_all.shape[1] // 3
    key_value = project[:, channels:].reshape(2, height, 2 * channels)
    left = along(key_value[:, height - LEFT :], 1)
    right = along(key_value[:, :RIGHT], -1)
    first_ref = first.reshape(1).astype(jnp.int32)
    context, chance, branch = attend(first_ref, lens, project, left, right, rel, w_attn)
    stream2 = stream1 + narrow_core(branch)

    normed, normal2, inverse2 = norm_rows(stream2, gains[2], biases[2])
    hidden2 = widen_core(normed.astype(BF16))
    halves = product(hidden2, glu_all)
    value_half, gate_half = halves[:, :channels], halves[:, channels:]
    logistic = jax.nn.sigmoid(gate_half)
    gated = (value_half * logistic * live).astype(BF16).reshape(2, height, channels)
    tail = KERNEL - 1
    earlier = along(gated[:, height - tail :], 1)
    extended = jnp.concatenate([earlier, gated], 1)
    mixed = extended[:, 0:height] * taps[0]
    for offset in range(1, KERNEL):
        mixed = mixed + extended[:, offset : offset + height] * taps[offset]
    mixed = mixed.reshape(2 * height, channels)
    sums = jnp.stack([jnp.sum(mixed, axis=1), jnp.sum(mixed * mixed, axis=1)], 1)
    sums = (sums + turned(swap_core(sums))) / D
    centre, square = sums[:, :1], sums[:, 1:]
    inverse_conv = lax.rsqrt(square - centre * centre + EPSILON)
    conv_normal = (mixed - centre) * inverse_conv
    levels = conv_normal * conv_scale + conv_shift
    active_conv = jax.nn.silu(levels).astype(BF16)
    stream3 = stream2 + narrow_core(product_nt(active_conv, w_conv))

    normed, normal3, inverse3 = norm_rows(stream3, gains[3], biases[3])
    hidden3 = widen_tp(normed.astype(BF16))
    branch, before3, active3 = ffn_forward(hidden3, two_in, two_out)
    stream4 = stream3 + 0.5 * branch
    result, normal4, inverse4 = norm_rows(stream4, gains[4], biases[4])

    d_stream, gain4, bias4 = norm_back(
        stream_order(cotangent[0]).astype(F32), normal4, inverse4, gains[4]
    )
    d_branch = widen_tp((0.5 * d_stream).astype(BF16))
    d_hidden, grad_two_in, grad_two_out = ffn_backward(
        d_branch, d_branch, before3, active3, hidden3, two_in, two_out
    )
    d_input, gain3, bias3 = norm_back(narrow_tp(d_hidden), normal3, inverse3, gains[3])
    d_stream = d_stream + d_input
    grad_two_in, grad_two_out = settle_wide(grad_two_in), settle_wide(grad_two_out)

    d_branch = widen_core(d_stream.astype(BF16))
    d_levels = product(d_branch, w_conv) * silu_slope(levels)
    grad_w_conv = product_tn(d_branch, active_conv)
    grad_scale = jnp.sum(d_levels * conv_normal, axis=0)
    grad_shift = jnp.sum(d_levels, axis=0)
    scaled = d_levels * conv_scale
    sums = jnp.stack([jnp.sum(scaled, axis=1), jnp.sum(scaled * conv_normal, axis=1)], 1)
    sums = (sums + turned(swap_core(sums))) / D
    d_mixed = inverse_conv * (scaled - sums[:, :1] - conv_normal * sums[:, 1:])
    d_mixed = d_mixed.reshape(2, height, channels)
    d_extended = jnp.zeros((2, height + tail, channels), F32)
    tap_grads = []
    for offset in range(KERNEL):
        d_extended = d_extended + jnp.pad(
            d_mixed * taps[offset], ((0, 0), (offset, tail - offset), (0, 0))
        )
        tap_grads.append(jnp.sum(d_mixed * extended[:, offset : offset + height], axis=(0, 1)))
    later = along(d_extended[:, :tail], -1)
    d_gated = d_extended[:, tail:] + jnp.pad(later, ((0, 0), (height - tail, 0), (0, 0)))
    d_gated = d_gated.reshape(2 * height, channels) * live
    d_halves = jnp.concatenate(
        [d_gated * logistic, d_gated * value_half * logistic * (1.0 - logistic)], 1
    ).astype(BF16)
    d_hidden = narrow_core(product_nt(d_halves, glu_all))
    grad_glu = product_tn(hidden2, d_halves)
    d_input, gain2, bias2 = norm_back(d_hidden, normal2, inverse2, gains[2])
    d_stream = d_stream + d_input
    grad_value, grad_gate, grad_w_conv = core_settle(
        [grad_glu[:, :channels], grad_glu[:, channels:], grad_w_conv], second
    )

    d_branch = widen_core(d_stream.astype(BF16))
    d_query, d_own, d_left, d_right, d_table = attend_back(
        first_ref, lens, d_branch, project, left, right, rel, w_attn, chance
    )
    grad_w_attn = product_tn(d_branch, context)
    from_next = along(d_left, -1).astype(F32)
    from_last = along(d_right, 1).astype(F32)
    d_own = d_own + jnp.pad(from_next, ((0, 0), (0, 0), (height - LEFT, 0), (0, 0)))
    d_own = d_own + jnp.pad(from_last, ((0, 0), (0, 0), (0, height - RIGHT), (0, 0)))
    d_own = d_own.astype(BF16).reshape(2, 2 * height, channels)
    d_project = jnp.concatenate([d_query, d_own[0], d_own[1]], 1)
    d_hidden = narrow_core(product_nt(d_project, qkv_all))
    grad_qkv = product_tn(hidden1, d_project)
    d_input, gain1, bias1 = norm_back(d_hidden, normal1, inverse1, gains[1])
    d_stream = d_stream + d_input
    grad_q, grad_k, grad_v, grad_w_attn = core_settle(
        [
            grad_qkv[:, :channels],
            grad_qkv[:, channels : 2 * channels],
            grad_qkv[:, 2 * channels :],
            grad_w_attn,
        ],
        second,
    )

    _, normal0, inverse0 = norm_rows(stream0, gains[0], biases[0])
    d_branch = widen_tp((0.5 * d_stream).astype(BF16))
    d_branch = to_cube(d_branch, OUT_AXES)
    d_hidden, grad_one_in, grad_one_out = ffn_backward(
        d_branch, d_branch, before0, active0, hidden0, one_in, one_out
    )
    d_hidden = from_cube(narrow_tp(d_hidden), IN_AXES)
    d_input, gain0, bias0 = norm_back(d_hidden, normal0, inverse0, gains[0])
    d_stream = d_stream + d_input
    grad_one_in = cube_settle(grad_one_in.reshape(group, local, -1), IN_AXES)
    grad_one_out = cube_settle(grad_one_out.reshape(group, local, -1), OUT_AXES)

    d_rel = (d_table[:HD] + d_table[HD:])[:, :SPAN]
    grad_table = jnp.dot(d_rel, selector.astype(F32).T, precision=lax.Precision.HIGHEST)
    table_cut = grad_table.reshape(rows, 2, ctxs, table_count).transpose(0, 2, 1, 3)
    conv_cut = jnp.concatenate(
        [jnp.stack(tap_grads, 0), grad_scale[None], grad_shift[None]], 0
    ).reshape(KERNEL + 2, tp, half)
    conv_cut = jnp.where(
        second,
        jnp.concatenate([jnp.zeros_like(conv_cut), conv_cut], 2),
        jnp.concatenate([conv_cut, jnp.zeros_like(conv_cut)], 2),
    )
    conv_cut = conv_cut.reshape(KERNEL + 2, tp, rows, 2, ctxs, width)
    conv_cut = conv_cut.transpose(2, 4, 3, 1, 0, 5)
    packed = jnp.concatenate(
        [table_cut.reshape(group, -1), conv_cut.reshape(group, -1)], 1
    )
    packed = lax.psum(settle_cut(packed), "tp")
    grad_table = packed[:table_count].reshape(distance.shape)
    conv_cut = packed[table_count:].reshape(tp, KERNEL + 2, width)
    conv_cut = lax.dynamic_index_in_dim(conv_cut, lax.axis_index("tp"), 0, keepdims=False)

    norm_grads = jnp.stack(
        [gain0, gain1, gain2, gain3, gain4, bias0, bias1, bias2, bias3, bias4], 0
    )
    norm_grads = norm_grads.reshape(10, group, local).transpose(1, 0, 2)
    norm_grads = lax.psum(settle_cut(norm_grads.reshape(group, -1)), "tp").reshape(10, local)

    return (
        natural_order(result.astype(BF16))[None],
        natural_order(d_stream)[None],
        grad_one_in,
        grad_one_out,
        norm_grads[:5].T,
        norm_grads[5:].T,
        jnp.stack([grad_q, grad_k, grad_v], 1),
        grad_w_attn,
        grad_table,
        jnp.stack([grad_value, grad_gate], 1),
        conv_cut[:KERNEL].T,
        conv_cut[KERNEL],
        conv_cut[KERNEL + 1],
        grad_w_conv,
        grad_two_in,
        grad_two_out,
    )


def turned(sums):
    half = sums.shape[0] // 2
    return jnp.concatenate([sums[half:], sums[:half]], 0)


def solution(mesh):
    shards, ctxs, tp = (mesh.shape[axis] for axis in ("shard", "ctx", "tp"))
    cut = Mesh(mesh.devices.reshape(shards // 2, 2, ctxs, tp), ("row", "core", "ctx", "tp"))
    shard = ("row", "core")
    block = ("row", "core", "ctx")
    every = ("tp", "row", "core", "ctx")
    weight = P(block, "tp")
    narrow = P(block, None)
    deep = P(block, None, "tp")
    frames = P(shard, ("ctx", "tp"), None)
    return jax.shard_map(
        body,
        mesh=cut,
        in_specs=(
            frames, frames, P(shard), P(), weight, weight, narrow, narrow, deep, weight, narrow,
            deep, P(every, None), P(every), P(every), weight, weight, weight,
        ),
        out_specs=(
            frames, frames, weight, weight, narrow, narrow, deep, weight, narrow, deep,
            P(every, None), P(every), P(every), weight, weight, weight,
        ),
        check_vma=False,
    )
```

```python
import functools

import jax
import jax.numpy as jnp
from jax import lax
from jax.experimental import pallas as pl
from jax.experimental.pallas import tpu as pltpu
from jax.sharding import Mesh
from jax.sharding import PartitionSpec as P

D = 1024
HD = 64
KERNEL = 31
LEFT = 64
RIGHT = 16
SPAN = 73
PAIR = 128
KEYS = 256
EPSILON = 1e-05
MASKED = -1e30
SCALE = HD**-0.5
F32 = jnp.float32
BF16 = jnp.bfloat16


def product(left, right):
    return jnp.dot(left, right, preferred_element_type=F32)


def product_nt(left, right):
    return lax.dot_general(left, right, (((1,), (1,)), ((), ())), preferred_element_type=F32)


def product_tn(left, right):
    return lax.dot_general(left, right, (((0,), (0,)), ((), ())), preferred_element_type=F32)


def silu_slope(values):
    logistic = jax.nn.sigmoid(values)
    return logistic * (1.0 + values * (1.0 - logistic))


def bits_of(axis):
    count = lax.axis_size(axis)
    return [1 << k for k in range(count.bit_length() - 1)]


def stream_places():
    rows, ctxs = lax.axis_size("row"), lax.axis_size("ctx")
    return [(0, b, a) for b in range(ctxs) for a in range(rows)] + [
        (1, b, a) for a in range(rows) for b in range(ctxs)
    ]


def ffn_places(core, kind):
    rows, ctxs = lax.axis_size("row"), lax.axis_size("ctx")
    if kind == "in":
        return [(e ^ core, b, a) for e in range(2) for b in range(ctxs) for a in range(rows)]
    return [(e ^ core, b, a) for e in range(2) for a in range(rows) for b in range(ctxs)]


def reorder(value, source, target):
    width = value.shape[-1] // len(source)
    where = {place: k for k, place in enumerate(source)}
    return jnp.concatenate(
        [value[..., where[p] * width : (where[p] + 1) * width] for p in target], -1
    )


def to_ffn(value, kind, second):
    source = stream_places()
    return jnp.where(
        second,
        reorder(value, source, ffn_places(1, kind)),
        reorder(value, source, ffn_places(0, kind)),
    )


def from_ffn(value, kind, second):
    target = stream_places()
    return jnp.where(
        second,
        reorder(value, ffn_places(1, kind), target),
        reorder(value, ffn_places(0, kind), target),
    )


def crossed(blocks):
    rows = lax.axis_size("row")
    flags = [((lax.axis_index("row") & m) != 0, m) for m in bits_of("row")]
    flags += [((lax.axis_index("ctx") & m) != 0, m * rows) for m in bits_of("ctx")]
    for flag, mask in flags:
        blocks = [jnp.where(flag, blocks[i ^ mask], blocks[i]) for i in range(len(blocks))]
    return blocks


def natural_places():
    rows, ctxs = lax.axis_size("row"), lax.axis_size("ctx")
    return [(c, b, a) for a in range(rows) for c in range(2) for b in range(ctxs)]


def from_natural(value):
    rows, ctxs = lax.axis_size("row"), lax.axis_size("ctx")
    grid = [(c, b, a) for c in range(2) for b in range(ctxs) for a in range(rows)]
    value = reorder(value, natural_places(), grid)
    width = value.shape[-1] // len(grid)
    blocks = [value[..., k * width : (k + 1) * width] for k in range(len(grid))]
    half = len(grid) // 2
    value = jnp.concatenate(crossed(blocks[:half]) + crossed(blocks[half:]), -1)
    return reorder(value, grid, stream_places())


def to_natural(value):
    rows, ctxs = lax.axis_size("row"), lax.axis_size("ctx")
    grid = [(c, b, a) for c in range(2) for b in range(ctxs) for a in range(rows)]
    value = reorder(value, stream_places(), grid)
    width = value.shape[-1] // len(grid)
    blocks = [value[..., k * width : (k + 1) * width] for k in range(len(grid))]
    half = len(grid) // 2
    value = jnp.concatenate(crossed(blocks[:half]) + crossed(blocks[half:]), -1)
    return reorder(value, grid, natural_places())


def partner(value, axis, mask):
    count = lax.axis_size(axis)
    return lax.ppermute(value, axis, [(i, i ^ mask) for i in range(count)])


def swap_core(value):
    return partner(value, "core", 1)


def stages_of(axes):
    return [(axis, mask) for axis in axes for mask in bits_of(axis)]


def cube_pair(value, axes):
    value = value[None]
    stages = stages_of(axes)
    for axis, mask in stages[:-1]:
        value = jnp.concatenate([value, partner(value, axis, mask)], 0)
    return value, partner(value, *stages[-1])


def cube_settle(near, far, axes):
    stages = stages_of(axes)[::-1]
    total = near.astype(F32) + partner(far, *stages[0]).astype(F32)
    for axis, mask in stages[1:]:
        half = total.shape[0] // 2
        arrived = partner(total[half:].astype(BF16), axis, mask)
        total = total[:half] + arrived.astype(F32)
    return total[0]


def ffn_weight(weight, axes):
    near, far = cube_pair(weight, axes)
    return [near, far, swap_core(near), swap_core(far)]


def ffn_settle(chunks, axes):
    near = chunks[0].astype(F32) + swap_core(chunks[2]).astype(F32)
    far = chunks[1].astype(F32) + swap_core(chunks[3]).astype(F32)
    return cube_settle(near, far.astype(BF16), axes)


A_AXES = ("row", "ctx")
B_AXES = ("ctx", "row")


def tp_joined(own, arrived, mask, axis):
    upper = (lax.axis_index("tp") & mask) != 0
    return jnp.concatenate(
        [jnp.where(upper, arrived, own), jnp.where(upper, own, arrived)], axis
    )


def tp_halves(value, mask, axis):
    upper = (lax.axis_index("tp") & mask) != 0
    half = value.shape[axis] // 2
    low = lax.slice_in_dim(value, 0, half, axis=axis)
    high = lax.slice_in_dim(value, half, 2 * half, axis=axis)
    return jnp.where(upper, high, low), jnp.where(upper, low, high)


def core_shares(matrices, second):
    halves = jnp.concatenate(
        [m.reshape(m.shape[0], 2, 1, m.shape[1] // 2) for m in matrices], 2
    )
    own, other = halves[:, 0], halves[:, 1]
    own, other = jnp.where(second, other, own), jnp.where(second, own, other)
    own = own.reshape(own.shape[0], -1)
    other = swap_core(other.reshape(own.shape))
    value = jnp.stack([jnp.where(second, other, own), jnp.where(second, own, other)], 0)[:, None]
    for mask in bits_of("tp"):
        value = tp_joined(value, partner(value, "tp", mask), mask, 1)
    return value


def core_weight(value):
    return [*cube_pair(value[0], A_AXES), *cube_pair(value[1], B_AXES)]


def core_settle(chunks, second, count):
    total = jnp.stack(
        [
            cube_settle(chunks[0], chunks[1], A_AXES),
            cube_settle(chunks[2], chunks[3], B_AXES),
        ],
        0,
    )
    for mask in bits_of("tp")[::-1]:
        kept, sent = tp_halves(total, mask, 1)
        total = kept + partner(sent.astype(BF16), "tp", mask).astype(F32)
    total = total[:, 0]
    own = jnp.where(second, total[1], total[0])
    other = swap_core(jnp.where(second, total[0], total[1]).astype(BF16)).astype(F32)
    own = own.reshape(own.shape[0], count, -1)
    other = other.reshape(own.shape)
    whole = jnp.concatenate(
        [jnp.where(second, other, own), jnp.where(second, own, other)], 2
    )
    return [whole[:, m] for m in range(count)]


def along(value, step):
    count = lax.axis_size("ctx") * lax.axis_size("tp")
    pairs = [(i, i + step) for i in range(count) if 0 <= i + step < count]
    return lax.ppermute(value, ("ctx", "tp"), pairs)


def widen_tp(rows):
    return lax.all_gather(rows, "tp", axis=0, tiled=True)


def widen_early(rows):
    count = lax.axis_size("tp")
    index = lax.axis_index("tp")
    parts = [rows] + [
        lax.ppermute(rows, "tp", [(i, i ^ k) for i in range(count)]) for k in range(1, count)
    ]
    for mask in bits_of("tp"):
        flag = (index & mask) != 0
        parts = [jnp.where(flag, parts[k ^ mask], parts[k]) for k in range(count)]
    return jnp.concatenate(parts, 0)


def exchange_tp(partial_value):
    count = lax.axis_size("tp")
    pieces = partial_value.reshape(
        count, partial_value.shape[0] // count, partial_value.shape[1]
    )
    return lax.all_to_all(pieces, "tp", 0, 0)


def widen_core(rows):
    return jnp.concatenate([rows, swap_core(rows)], 0)


def exchange_core(partial_value):
    half = partial_value.shape[0] // 2
    return [partial_value[:half], swap_core(partial_value[half:])]


PARAMS = pltpu.CompilerParams(vmem_limit_bytes=48 << 20)
VMEM = pl.BlockSpec(memory_space=pltpu.VMEM)
SMEM = pl.BlockSpec(memory_space=pltpu.SMEM)


def run(kernel, name, outs, *args, smem=0, scratch=()):
    return pl.pallas_call(
        kernel,
        in_specs=[SMEM] * smem + [VMEM] * (len(args) - smem),
        out_specs=[VMEM] * len(outs),
        out_shape=[jax.ShapeDtypeStruct(shape, dtype) for shape, dtype in outs],
        scratch_shapes=list(scratch),
        compiler_params=PARAMS,
        name=name,
    )(*args)


def stacked(refs):
    return jnp.concatenate([r[...].reshape(-1, r.shape[-1]) for r in refs], 0)


def heads_of(refs, start, stop):
    return jnp.concatenate(
        [
            jnp.concatenate(
                [r[:, z, :, start:stop].reshape(-1, stop - start) for r in refs], 0
            )
            for z in range(refs[0].shape[1])
        ],
        1,
    )


def block_order(value, source, target, width):
    where = {place: k for k, place in enumerate(source)}
    return jnp.concatenate(
        [value[:, where[p] * width : (where[p] + 1) * width] for p in target], 1
    )


def by_core(value, kind, second, inverse=False):
    places, width = stream_places(), D // len(stream_places())
    options = []
    for core in range(2):
        other = ffn_places(core, kind)
        options.append(
            block_order(value, other, places, width)
            if inverse
            else block_order(value, places, other, width)
        )
    return jnp.where(second, options[1], options[0])


def normal_of(stream):
    centre = stream - jnp.mean(stream, axis=-1, keepdims=True)
    inverse = lax.rsqrt(jnp.mean(centre * centre, axis=-1, keepdims=True) + EPSILON)
    return centre * inverse, inverse


def summed(refs):
    total = None
    for ref in refs:
        value = ref[...].astype(F32)
        value = jnp.sum(value, axis=0) if value.ndim == 3 else value
        total = value if total is None else total + value
    return total


def back_through(upstream, normal, inverse, gain, grads_ref):
    scaled = upstream * gain
    grads_ref[0:1] = jnp.sum(upstream * normal, axis=0, keepdims=True)
    grads_ref[1:2] = jnp.sum(upstream, axis=0, keepdims=True)
    return inverse * (
        scaled
        - jnp.mean(scaled, axis=-1, keepdims=True)
        - normal * jnp.mean(scaled * normal, axis=-1, keepdims=True)
    )


def onward_kernel(count, scale, source, target, core_ref, *refs):
    pieces, stream_ref, norm_ref = refs[:count], refs[count], refs[count + 1]
    next_ref, hidden_ref = refs[count + 2 :]
    second = core_ref[0] == 1
    total = summed(pieces)
    if source:
        total = by_core(total, source, second, inverse=True)
    stream = stream_ref[...] + scale * total
    next_ref[...] = stream
    hidden = normal_of(stream)[0] * norm_ref[0:1] + norm_ref[1:2]
    if target:
        hidden = by_core(hidden, target, second)
    hidden_ref[...] = hidden.astype(BF16)


def onward(core, pieces, stream, norm, scale, source, target):
    return run(
        functools.partial(onward_kernel, len(pieces), scale, source, target),
        "onward",
        [(stream.shape, F32), (stream.shape, BF16)],
        core,
        *pieces,
        stream,
        norm,
        smem=1,
    )


def turn_kernel(count, core_ref, *refs):
    pieces, stream_ref, up_ref, norm_ref = refs[:count], *refs[count : count + 3]
    result_ref, back_ref, branch_ref, grads_ref = refs[count + 3 :]
    second = core_ref[0] == 1
    total = by_core(summed(pieces), "out", second, inverse=True)
    normal, inverse = normal_of(stream_ref[...] + 0.5 * total)
    result_ref[...] = (normal * norm_ref[0:1] + norm_ref[1:2]).astype(BF16)
    back = back_through(up_ref[...].astype(F32), normal, inverse, norm_ref[0:1], grads_ref)
    back_ref[...] = back
    branch_ref[...] = by_core(0.5 * back, "out", second).astype(BF16)


def turn(core, pieces, stream, upstream, norm):
    shape = stream.shape
    return run(
        functools.partial(turn_kernel, len(pieces)),
        "turn",
        [(shape, BF16), (shape, F32), (shape, BF16), ((2, D), F32)],
        core,
        *pieces,
        stream,
        upstream,
        norm,
        smem=1,
    )


def return_kernel(count, scale, source, target, core_ref, *refs):
    pieces, stream_ref, up_ref, norm_ref = refs[:count], *refs[count : count + 3]
    back_ref, branch_ref, grads_ref = refs[count + 3 :]
    second = core_ref[0] == 1
    total = summed(pieces)
    if source:
        total = by_core(total, source, second, inverse=True)
    normal, inverse = normal_of(stream_ref[...].astype(F32))
    back = up_ref[...] + back_through(total, normal, inverse, norm_ref[0:1], grads_ref)
    back_ref[...] = back
    branch = scale * back
    if target:
        branch = by_core(branch, target, second)
    branch_ref[...] = branch.astype(BF16)


def returning(core, pieces, stream, upstream, norm, scale, source, target):
    shape = stream.shape
    return run(
        functools.partial(return_kernel, len(pieces), scale, source, target),
        "returning",
        [(shape, F32), (shape, BF16), ((2, D), F32)],
        core,
        *pieces,
        stream,
        upstream,
        norm,
        smem=1,
    )


def first_kernel(wide_ref, norm_ref, *refs):
    hidden_ref = refs[8]
    hidden = normal_of(wide_ref[...].astype(F32))[0] * norm_ref[0:1] + norm_ref[1:2]
    hidden_ref[...] = hidden.astype(BF16)
    ffn_forward_kernel(hidden_ref, *refs[:8], *refs[9:])


def ffn_forward_kernel(rows_ref, *refs):
    ins, outs = refs[:4], refs[4:8]
    before_ref, active_ref, branch_ref = refs[8:]
    before = product(rows_ref[...], stacked(ins))
    before_ref[...] = before
    active = (before * jax.nn.sigmoid(before)).astype(BF16)
    active_ref[...] = active
    branch_ref[...] = product_nt(active, stacked(outs)).astype(BF16)


def ffn_outs(height, width):
    return [((height, width), F32), ((height, width), BF16), ((height, D), BF16)]


def ffn_first(wide, norm, ins, outs):
    height, width = wide.shape[0], ins[0].shape[-1]
    return run(
        first_kernel, "ffn_first", [((height, D), BF16), *ffn_outs(height, width)],
        wide, norm, *ins, *outs,
    )


def ffn_forward(hidden, ins, outs):
    height, width = hidden.shape[0], ins[0].shape[-1]
    return run(
        ffn_forward_kernel, "ffn_forward", ffn_outs(height, width), hidden, *ins, *outs
    )


def ffn_backward_kernel(rows_ref, before_ref, *refs):
    ins, outs = refs[:4], refs[4:8]
    d_before_ref, branch_ref = refs[8:]
    d_active = product(rows_ref[...], stacked(outs))
    d_before = (d_active * silu_slope(before_ref[...])).astype(BF16)
    d_before_ref[...] = d_before
    branch_ref[...] = product_nt(d_before, stacked(ins)).astype(BF16)


def ffn_backward(upstream, before, ins, outs):
    height, width = before.shape
    return run(
        ffn_backward_kernel, "ffn_backward", [((height, width), BF16), ((height, D), BF16)],
        upstream, before, *ins, *outs,
    )


def scatter_rows(value, refs):
    rows = value.shape[0] // len(refs)
    for j, ref in enumerate(refs):
        ref[...] = value[j * rows : (j + 1) * rows].reshape(ref.shape)


def ffn_grads_kernel(hidden_ref, d_before_ref, up_ref, active_ref, *outs):
    scatter_rows(product_tn(hidden_ref[...], d_before_ref[...]).astype(BF16), outs[:4])
    scatter_rows(product_tn(up_ref[...], active_ref[...]).astype(BF16), outs[4:])


def ffn_grads(hidden, d_before, upstream, active, like):
    grads = run(
        ffn_grads_kernel, "ffn_grads", [(like.shape, BF16)] * 8,
        hidden, d_before, upstream, active,
    )
    return grads[:4], grads[4:]


def project_kernel(rows_ref, *refs):
    chunks, outs = refs[:4], refs[4:]
    value = product(rows_ref[...], heads_of(chunks, 0, 3 * PAIR)).astype(BF16)
    for z in range(chunks[0].shape[1]):
        for m in range(3):
            outs[m][:, z * PAIR : (z + 1) * PAIR] = value[
                :, (3 * z + m) * PAIR : (3 * z + m + 1) * PAIR
            ]


def project_heads(hidden, chunks):
    shape = (hidden.shape[0], chunks[0].shape[1] * PAIR)
    return run(project_kernel, "project_heads", [(shape, BF16)] * 3, hidden, *chunks)


def core_grads_kernel(count, hidden_ref, up_ref, *refs):
    values, last_ref, outs = refs[:count], refs[count], refs[count + 1 :]
    tp = outs[0].shape[1]
    grads = [product_tn(hidden_ref[...], v[...]).astype(BF16) for v in values]
    grads.append(product_tn(up_ref[...], last_ref[...]).astype(BF16))
    for m, grad in enumerate(grads):
        rows = D // len(outs)
        for j, ref in enumerate(outs):
            for z in range(tp):
                piece = grad[j * rows : (j + 1) * rows, z * PAIR : (z + 1) * PAIR]
                ref[:, z, :, m * PAIR : (m + 1) * PAIR] = piece.reshape(
                    ref.shape[0], ref.shape[2], PAIR
                )


def core_grads(hidden, upstream, values, last, like):
    return run(
        functools.partial(core_grads_kernel, len(values)), "core_grads",
        [(like.shape, BF16)] * 4, hidden, upstream, *values, last,
    )


def interleaved(values):
    tp = values[0].shape[1] // PAIR
    return jnp.concatenate(
        [v[:, z * PAIR : (z + 1) * PAIR] for z in range(tp) for v in values], 1
    )


def window(first, length, height):
    rows = lax.broadcasted_iota(jnp.int32, (height, KEYS), 0)
    lanes = lax.broadcasted_iota(jnp.int32, (height, KEYS), 1)
    offset = lanes - rows
    frame = lanes + (first - LEFT)
    in_band = (offset >= 0) & (offset < SPAN)
    allowed = in_band & (frame >= 0) & (frame < length)
    return in_band, allowed


def both(mask):
    return jnp.concatenate([mask, mask], 0)


def window_of(left_ref, own_ref, right_ref, clip, z, side, height):
    channels = own_ref.shape[1]
    lanes = slice(z * PAIR, (z + 1) * PAIR)
    far = slice(side * channels + z * PAIR, side * channels + (z + 1) * PAIR)
    return jnp.concatenate(
        [
            left_ref[clip, :, far],
            own_ref[clip * height : (clip + 1) * height, lanes],
            right_ref[clip, :, far],
            jnp.zeros((KEYS - LEFT - RIGHT - height, PAIR), BF16),
        ],
        0,
    )


def split_heads(value, odd):
    zero = jnp.zeros_like(value)
    return jnp.concatenate([jnp.where(odd, zero, value), jnp.where(odd, value, zero)], 0)


def merge_heads(value, odd):
    height = value.shape[0] // 2
    return jnp.where(odd, value[height:], value[:height])


def attend_kernel(
    height, first_ref, lens_ref, q_ref, k_ref, v_ref, left_ref, right_ref, rel_ref,
    c0, c1, c2, c3, context_ref, chance_ref, branch_ref
):
    odd = lax.broadcasted_iota(jnp.int32, (1, PAIR), 1) >= HD
    for clip in range(2):
        rows = slice(clip * height, (clip + 1) * height)
        in_band, allowed = window(first_ref[0], lens_ref[clip], height)
        in_band, allowed = both(in_band), both(allowed)
        for z in range(c0.shape[1]):
            lanes = slice(z * PAIR, (z + 1) * PAIR)
            query = split_heads(q_ref[rows, lanes], odd)
            keys = window_of(left_ref, k_ref, right_ref, clip, z, 0, height)
            values = window_of(left_ref, v_ref, right_ref, clip, z, 1, height)
            relative = product(query, rel_ref[...])
            relative = jnp.concatenate([relative, jnp.zeros((2 * height, KEYS - PAIR), F32)], 1)
            relative = jnp.concatenate(
                [
                    pltpu.roll(relative[:height], 0, 1, stride=1, stride_axis=0),
                    pltpu.roll(relative[height:], 0, 1, stride=1, stride_axis=0),
                ],
                0,
            )
            score = (product_nt(query, keys) + relative) * SCALE
            masked = jnp.where(allowed, score, MASKED)
            ceiling = jnp.max(masked, axis=-1, keepdims=True)
            raised = jnp.where(in_band, jnp.exp(masked - ceiling), 0.0)
            chance = raised * (1.0 / jnp.sum(raised, axis=-1, keepdims=True))
            chance_ref[clip, z] = chance
            context = merge_heads(product(chance.astype(BF16), values), odd)
            context_ref[rows, lanes] = context.astype(BF16)
    weight = heads_of((c0, c1, c2, c3), 3 * PAIR, 4 * PAIR)
    branch_ref[...] = product_nt(context_ref[...], weight).astype(BF16)


def attend(first, lens, heads, left, right, rel, chunks):
    height, channels, tp = heads[0].shape[0] // 2, heads[0].shape[1], chunks[0].shape[1]
    return run(
        functools.partial(attend_kernel, height),
        "attend",
        [
            ((2 * height, channels), BF16),
            ((2, tp, 2 * height, KEYS), F32),
            ((2 * height, D), BF16),
        ],
        first, lens, *heads, left, right, rel, *chunks,
        smem=2,
    )


def attend_back_kernel(
    height, first_ref, lens_ref, up_ref, q_ref, k_ref, v_ref, left_ref, right_ref, rel_ref,
    c0, c1, c2, c3, chance_ref, dq_ref, own_ref, d_left_ref, d_right_ref, table_ref
):
    odd = lax.broadcasted_iota(jnp.int32, (1, PAIR), 1) >= HD
    weight = heads_of((c0, c1, c2, c3), 3 * PAIR, 4 * PAIR)
    d_context = product(up_ref[...], weight).astype(BF16)
    table = jnp.zeros((PAIR, PAIR), F32)
    flip = (
        lax.broadcasted_iota(jnp.int32, (height, height), 0)
        + lax.broadcasted_iota(jnp.int32, (height, height), 1)
        == height - 1
    ).astype(BF16)
    for clip in range(2):
        rows = slice(clip * height, (clip + 1) * height)
        allowed = both(window(first_ref[0], lens_ref[clip], height)[1])
        for z in range(c0.shape[1]):
            lanes = slice(z * PAIR, (z + 1) * PAIR)
            query = split_heads(q_ref[rows, lanes], odd)
            upstream = split_heads(d_context[rows, lanes], odd)
            keys = window_of(left_ref, k_ref, right_ref, clip, z, 0, height)
            values = window_of(left_ref, v_ref, right_ref, clip, z, 1, height)
            chance = chance_ref[clip, z]
            d_chance = product_nt(upstream, values)
            inner = jnp.sum(d_chance * chance, axis=-1, keepdims=True)
            d_score = jnp.where(allowed, chance * (d_chance - inner), 0.0).astype(BF16)
            d_values = product_tn(chance.astype(BF16), upstream)
            d_keys = product_tn(d_score, query) * SCALE
            relative = []
            for head in range(2):
                turned_rows = product(flip, d_score[head * height : (head + 1) * height])
                rolled = pltpu.roll(
                    turned_rows, KEYS - height + 1, 1, stride=1, stride_axis=0
                )[:, :PAIR].astype(BF16)
                relative.append(product(flip, rolled).astype(BF16))
            relative = jnp.concatenate(relative, 0)
            d_query = product(d_score, keys) + product_nt(relative, rel_ref[...])
            dq_ref[rows, lanes] = (merge_heads(d_query, odd) * SCALE).astype(BF16)
            table += product_tn(query, relative)
            for slot, value in ((0, d_keys), (1, d_values)):
                d_left_ref[slot, clip, :, lanes] = value[:LEFT].astype(BF16)
                own_ref[slot, rows, lanes] = value[LEFT : LEFT + height]
                d_right_ref[slot, clip, :, lanes] = value[
                    LEFT + height : LEFT + height + RIGHT
                ].astype(BF16)
    table_ref[...] = table * SCALE


def attend_back(first, lens, upstream, heads, left, right, rel, chunks, chance):
    height, channels = heads[0].shape[0] // 2, heads[0].shape[1]
    return run(
        functools.partial(attend_back_kernel, height),
        "attend_back",
        [
            ((2 * height, channels), BF16),
            ((2, 2 * height, channels), F32),
            ((2, 2, LEFT, channels), BF16),
            ((2, 2, RIGHT, channels), BF16),
            ((PAIR, PAIR), F32),
        ],
        first, lens, upstream, *heads, left, right, rel, *chunks, chance,
        smem=2,
    )


def heads_in_kernel(height, dq_ref, own_ref, left_ref, right_ref, *refs):
    chunks, dk_ref, dv_ref, branch_ref = refs[:4], *refs[4:]
    for slot, out_ref in ((0, dk_ref), (1, dv_ref)):
        for clip in range(2):
            start = clip * height
            own = own_ref[slot, start : start + height]
            top = own[:RIGHT] + right_ref[slot, clip].astype(F32)
            own = jnp.concatenate([top, own[RIGHT:]], 0)
            low = own[height - LEFT :] + left_ref[slot, clip].astype(F32)
            own = jnp.concatenate([own[: height - LEFT], low], 0)
            out_ref[start : start + height] = own.astype(BF16)
    value = interleaved([dq_ref[...], dk_ref[...], dv_ref[...]])
    branch_ref[...] = product_nt(value, heads_of(chunks, 0, 3 * PAIR)).astype(BF16)


def heads_in(d_query, own, from_next, from_last, chunks):
    shape = d_query.shape
    return run(
        functools.partial(heads_in_kernel, shape[0] // 2), "heads_in",
        [(shape, BF16), (shape, BF16), ((shape[0], D), BF16)],
        d_query, own, from_next, from_last, *chunks,
    )


REACH = 32


def gate_kernel(rows_ref, live_ref, *refs):
    chunks, value_ref, logistic_ref, gated_ref = refs[:4], *refs[4:]
    value = product(rows_ref[...], heads_of(chunks, 0, 2 * PAIR))
    for z in range(chunks[0].shape[1]):
        lanes = slice(z * PAIR, (z + 1) * PAIR)
        linear = value[:, 2 * z * PAIR : (2 * z + 1) * PAIR]
        logistic = jax.nn.sigmoid(value[:, (2 * z + 1) * PAIR : (2 * z + 2) * PAIR])
        value_ref[:, lanes] = linear
        logistic_ref[:, lanes] = logistic
        gated_ref[:, lanes] = (linear * logistic * live_ref[...]).astype(BF16)


def gate_channels(hidden, live, chunks):
    shape = (hidden.shape[0], chunks[0].shape[1] * PAIR)
    return run(
        gate_kernel, "gate_channels", [(shape, F32), (shape, F32), (shape, BF16)],
        hidden, live, *chunks,
    )


def extend(earlier_ref, own_ref, wide, height):
    for clip in range(2):
        wide[clip, :REACH] = earlier_ref[clip].astype(F32)
        wide[clip, REACH : REACH + height] = own_ref[
            clip * height : (clip + 1) * height
        ].astype(F32)


def mix_kernel(height, gated_ref, earlier_ref, taps_ref, mixed_ref, sums_ref, wide):
    extend(earlier_ref, gated_ref, wide, height)
    lead = REACH - (KERNEL - 1)
    for clip in range(2):
        rows = slice(clip * height, (clip + 1) * height)
        first = second = jnp.zeros((height, 1), F32)
        for z in range(gated_ref.shape[1] // PAIR):
            lanes = slice(z * PAIR, (z + 1) * PAIR)
            mixed = wide[clip, lead : lead + height, lanes] * taps_ref[0:1, lanes]
            for j in range(1, KERNEL):
                mixed += wide[clip, lead + j : lead + j + height, lanes] * taps_ref[j : j + 1, lanes]
            mixed_ref[rows, lanes] = mixed
            first += jnp.sum(mixed, axis=1, keepdims=True)
            second += jnp.sum(mixed * mixed, axis=1, keepdims=True)
        sums_ref[rows] = jnp.concatenate([first, second], 1)


def mix_channels(gated, earlier, taps):
    height, channels = gated.shape[0] // 2, gated.shape[1]
    return run(
        functools.partial(mix_kernel, height), "mix_channels",
        [((2 * height, channels), F32), ((2 * height, 2), F32)],
        gated, earlier, taps,
        scratch=[pltpu.VMEM((2, height + REACH, channels), F32)],
    )


def paired(own_ref, other_ref):
    half = own_ref.shape[0] // 2
    other = other_ref[...]
    return (own_ref[...] + jnp.concatenate([other[half:], other[:half]], 0)) * (1.0 / D)


def conv_norm(mixed_ref, sums_ref, other_ref):
    means = paired(sums_ref, other_ref)
    centre, square = means[:, 0:1], means[:, 1:2]
    inverse = lax.rsqrt(square - centre * centre + EPSILON)
    return (mixed_ref[...] - centre) * inverse, inverse


def conv_out_kernel(mixed_ref, sums_ref, other_ref, affine_ref, *refs):
    chunks, active_ref, branch_ref = refs[:4], *refs[4:]
    normal, _ = conv_norm(mixed_ref, sums_ref, other_ref)
    levels = normal * affine_ref[0:1] + affine_ref[1:2]
    active = (levels * jax.nn.sigmoid(levels)).astype(BF16)
    active_ref[...] = active
    weight = heads_of(chunks, 2 * PAIR, 3 * PAIR)
    branch_ref[...] = product_nt(active, weight).astype(BF16)


def conv_forward(mixed, sums, other, affine, chunks):
    return run(
        conv_out_kernel, "conv_forward", [(mixed.shape, BF16), ((mixed.shape[0], D), BF16)],
        mixed, sums, other, affine, *chunks,
    )


def conv_level_kernel(up_ref, mixed_ref, sums_ref, other_ref, affine_ref, *refs):
    chunks, scaled_ref, totals_ref, affine_grad_ref = refs[:4], *refs[4:]
    normal, _ = conv_norm(mixed_ref, sums_ref, other_ref)
    levels = normal * affine_ref[0:1] + affine_ref[1:2]
    weight = heads_of(chunks, 2 * PAIR, 3 * PAIR)
    d_levels = product(up_ref[...], weight) * silu_slope(levels)
    scaled = d_levels * affine_ref[0:1]
    scaled_ref[...] = scaled
    totals_ref[...] = jnp.concatenate(
        [
            jnp.sum(scaled, axis=1, keepdims=True),
            jnp.sum(scaled * normal, axis=1, keepdims=True),
        ],
        1,
    )
    affine_grad_ref[0:1] = jnp.sum(d_levels * normal, axis=0, keepdims=True)
    affine_grad_ref[1:2] = jnp.sum(d_levels, axis=0, keepdims=True)


def conv_levels_back(upstream, mixed, sums, other, affine, chunks):
    return run(
        conv_level_kernel, "conv_levels_back",
        [(mixed.shape, F32), (sums.shape, F32), ((2, mixed.shape[1]), F32)],
        upstream, mixed, sums, other, affine, *chunks,
    )


def unmix_kernel(
    height, scaled_ref, totals_ref, far_totals_ref, mixed_ref, sums_ref, other_ref, taps_ref,
    d_mixed_ref, own_ref, earlier_ref, wide
):
    normal, inverse = conv_norm(mixed_ref, sums_ref, other_ref)
    means = paired(totals_ref, far_totals_ref)
    d_mixed = inverse * (scaled_ref[...] - means[:, 0:1] - normal * means[:, 1:2])
    d_mixed_ref[...] = d_mixed
    for clip in range(2):
        rows = slice(clip * height, (clip + 1) * height)
        wide[clip, :REACH] = jnp.zeros((REACH, d_mixed.shape[1]), F32)
        wide[clip, REACH : REACH + height] = d_mixed[rows]
        wide[clip, REACH + height :] = jnp.zeros((REACH, d_mixed.shape[1]), F32)
        last = REACH + KERNEL - 1
        for z in range(d_mixed.shape[1] // PAIR):
            lanes = slice(z * PAIR, (z + 1) * PAIR)
            own = wide[clip, last : last + height, lanes] * taps_ref[0:1, lanes]
            for j in range(1, KERNEL):
                own += wide[clip, last - j : last - j + height, lanes] * taps_ref[j : j + 1, lanes]
            own_ref[rows, lanes] = own
            early = wide[clip, KERNEL - 1 : KERNEL - 1 + REACH, lanes] * taps_ref[0:1, lanes]
            for j in range(1, KERNEL):
                start = KERNEL - 1 - j
                early += wide[clip, start : start + REACH, lanes] * taps_ref[j : j + 1, lanes]
            earlier_ref[clip, :, lanes] = early


def unmix_channels(scaled, totals, far_totals, mixed, sums, other, taps):
    height, channels = mixed.shape[0] // 2, mixed.shape[1]
    return run(
        functools.partial(unmix_kernel, height), "unmix_channels",
        [(mixed.shape, F32), (mixed.shape, F32), ((2, REACH, channels), F32)],
        scaled, totals, far_totals, mixed, sums, other, taps,
        scratch=[pltpu.VMEM((2, height + 2 * REACH, channels), F32)],
    )


def gate_back_kernel(height, own_ref, later_ref, value_ref, logistic_ref, live_ref, *refs):
    chunks, d_value_ref, d_gate_ref, branch_ref = refs[:4], *refs[4:]
    for clip in range(2):
        rows = slice(clip * height, (clip + 1) * height)
        own = own_ref[rows]
        low = own[height - REACH :] + later_ref[clip]
        own = jnp.concatenate([own[: height - REACH], low], 0) * live_ref[rows]
        logistic = logistic_ref[rows]
        d_value_ref[rows] = (own * logistic).astype(BF16)
        d_gate_ref[rows] = (own * value_ref[rows] * logistic * (1.0 - logistic)).astype(BF16)
    value = interleaved([d_value_ref[...], d_gate_ref[...]])
    branch_ref[...] = product_nt(value, heads_of(chunks, 0, 2 * PAIR)).astype(BF16)


def gate_back(own, later, value_half, logistic, live, chunks):
    shape = own.shape
    return run(
        functools.partial(gate_back_kernel, shape[0] // 2), "gate_back",
        [(shape, BF16), (shape, BF16), ((shape[0], D), BF16)],
        own, later, value_half, logistic, live, *chunks,
    )


def tap_kernel(height, d_mixed_ref, gated_ref, earlier_ref, taps_ref, wide):
    extend(earlier_ref, gated_ref, wide, height)
    lead = REACH - (KERNEL - 1)
    for z in range(gated_ref.shape[1] // PAIR):
        lanes = slice(z * PAIR, (z + 1) * PAIR)
        for j in range(KERNEL):
            total = jnp.zeros((1, PAIR), F32)
            for clip in range(2):
                total += jnp.sum(
                    d_mixed_ref[clip * height : (clip + 1) * height, lanes]
                    * wide[clip, lead + j : lead + j + height, lanes],
                    axis=0,
                    keepdims=True,
                )
            taps_ref[j : j + 1, lanes] = total


def tap_grads_of(d_mixed, gated, earlier):
    height, channels = gated.shape[0] // 2, gated.shape[1]
    return run(
        functools.partial(tap_kernel, height), "tap_grads", [((KERNEL, channels), F32)],
        d_mixed, gated, earlier,
        scratch=[pltpu.VMEM((2, height + REACH, channels), F32)],
    )[0]


def norm_grads_settle(grads, second):
    rows = lax.axis_size("row")
    width = grads.shape[1] // len(stream_places())
    where = {place: k for k, place in enumerate(stream_places())}
    cut = lambda p: grads[:, where[p] * width : (where[p] + 1) * width]
    order = [(b, a) for b in range(lax.axis_size("ctx")) for a in range(rows)]
    halves = [jnp.stack([cut((c, b, a)) for b, a in order], 0) for c in range(2)]
    own = jnp.where(second, halves[1], halves[0])
    total = own + swap_core(jnp.where(second, halves[0], halves[1]))
    for axis, mask in stages_of(A_AXES)[::-1]:
        count = total.shape[0] // 2
        total = total[:count] + partner(total[count:], axis, mask)
    return total[0]


def body(
    inputs,
    cotangent,
    lengths,
    buckets,
    ffn1_in,
    ffn1_out,
    norm_gains,
    norm_biases,
    qkv_weight,
    attn_out,
    distance,
    glu_in,
    depthwise,
    conv_gain,
    conv_bias,
    conv_out,
    ffn2_in,
    ffn2_out,
):
    rows, ctxs, tp = lax.axis_size("row"), lax.axis_size("ctx"), lax.axis_size("tp")
    second = lax.axis_index("core") == 1
    core = lax.axis_index("core").reshape(1).astype(jnp.int32)
    local = ffn1_in.shape[0]
    height = inputs.shape[1]
    first = (lax.axis_index("ctx") * tp + lax.axis_index("tp")) * height
    lens = widen_core(lengths)
    frame_ids = first + jnp.arange(height, dtype=jnp.int32)
    live = (frame_ids[None, :] < lens[:, None]).astype(F32).reshape(2 * height, 1)

    near = from_natural(inputs[0])
    wide_inputs = widen_early(to_ffn(near, "in", second))
    one_in, one_out = ffn_weight(ffn1_in, A_AXES), ffn_weight(ffn1_out, B_AXES)

    padded = lambda v: jnp.pad(v, ((0, 0), (0, PAIR - v.shape[1])))
    table_rows, width = distance.shape[0], conv_gain.shape[0]
    small = jnp.concatenate(
        [
            padded(norm_gains.T),
            padded(norm_biases.T),
            padded(depthwise.T),
            padded(conv_gain[None]),
            padded(conv_bias[None]),
            padded(distance),
        ],
        0,
    )
    cube = jnp.stack([small, swap_core(small)], 0)[None]
    for axis, mask in stages_of(A_AXES):
        cube = jnp.concatenate([cube, partner(cube, axis, mask)], 0)
    take = lambda c, k: jnp.where(second, cube[k, 1 - c], cube[k, c])
    norms = jnp.concatenate(
        [take(c, b * rows + a)[:10, :local] for c, b, a in stream_places()], 1
    ).astype(F32)
    norm = [jnp.stack([norms[k], norms[5 + k]], 0) for k in range(5)]
    blocks = [
        crossed([take(c, k)[10:] for k in range(rows * ctxs)]) for c in range(2)
    ]
    natural = [blocks[c][b * rows + a] for c, b, a in natural_places()]
    table_all = jnp.concatenate([n[KERNEL + 2 :, :SPAN] for n in natural], 0)
    conv_small = jnp.concatenate([n[: KERNEL + 2, :width] for n in natural], 1)
    half = conv_small.shape[1] // 2
    conv_small = jnp.where(second, conv_small[:, half:], conv_small[:, :half])
    for mask in bits_of("tp"):
        conv_small = tp_joined(conv_small, partner(conv_small, "tp", mask), mask, 1)
    conv_small = conv_small.astype(F32)
    taps, affine = conv_small[:KERNEL], conv_small[KERNEL:]

    w_attn = core_weight(
        core_shares([qkv_weight[:, 0], qkv_weight[:, 1], qkv_weight[:, 2], attn_out], second)
    )
    w_conv = core_weight(core_shares([glu_in[:, 0], glu_in[:, 1], conv_out], second))
    two_in, two_out = ffn_weight(ffn2_in, A_AXES), ffn_weight(ffn2_out, B_AXES)

    selector = (jnp.arange(SPAN, dtype=jnp.int32)[:, None] == buckets[None, :]).astype(BF16)
    rel = product(table_all, selector).astype(BF16)
    rel = jnp.pad(jnp.concatenate([rel, rel], 0), ((0, 0), (0, PAIR - SPAN)))

    hidden0, before0, active0, branch = ffn_first(
        wide_inputs, to_ffn(norm[0], "in", second), one_in, one_out
    )
    stream1, hidden1 = onward(
        core, [exchange_tp(branch)], near.astype(F32), norm[1], 0.5, "out", None
    )

    hidden1 = widen_core(hidden1)
    heads = project_heads(hidden1, w_attn)
    channels = heads[0].shape[1]
    key_value = [h.reshape(2, height, channels) for h in heads[1:]]
    left = along(jnp.concatenate([h[:, height - LEFT :] for h in key_value], 2), 1)
    right = along(jnp.concatenate([h[:, :RIGHT] for h in key_value], 2), -1)
    first_ref = first.reshape(1).astype(jnp.int32)
    context, chance, branch = attend(first_ref, lens, heads, left, right, rel, w_attn)
    stream2, hidden2 = onward(core, exchange_core(branch), stream1, norm[2], 1.0, None, None)

    hidden2 = widen_core(hidden2)
    value_half, logistic, gated = gate_channels(hidden2, live, w_conv)
    earlier = along(gated.reshape(2, height, channels)[:, height - REACH :], 1)
    mixed, sums = mix_channels(gated, earlier, taps)
    other = swap_core(sums)
    active_conv, branch = conv_forward(mixed, sums, other, affine, w_conv)
    stream3, hidden3 = onward(core, exchange_core(branch), stream2, norm[3], 1.0, None, "in")

    hidden3 = widen_tp(hidden3)
    before3, active3, branch = ffn_forward(hidden3, two_in, two_out)
    result, d_stream, d_branch, grads4 = turn(
        core, [exchange_tp(branch)], stream3, from_natural(cotangent[0]), norm[4]
    )

    d_branch = widen_tp(d_branch)
    d_before, branch = ffn_backward(d_branch, before3, two_in, two_out)
    grad_in, grad_out = ffn_grads(hidden3, d_before, d_branch, active3, two_in[0])
    grad_two_in, grad_two_out = ffn_settle(grad_in, A_AXES), ffn_settle(grad_out, B_AXES)
    d_stream, d_branch, grads3 = returning(
        core, [exchange_tp(branch)], stream3, d_stream, norm[3], 1.0, "in", None
    )

    d_branch = widen_core(d_branch)
    scaled, totals, affine_grads = conv_levels_back(d_branch, mixed, sums, other, affine, w_conv)
    d_mixed, d_own, d_earlier = unmix_channels(
        scaled, totals, swap_core(totals), mixed, sums, other, taps
    )
    later = along(d_earlier, -1)
    d_value, d_gate, branch = gate_back(d_own, later, value_half, logistic, live, w_conv)
    grads = core_grads(hidden2, d_branch, (d_value, d_gate), active_conv, w_conv[0])
    tap_grads = tap_grads_of(d_mixed, gated, earlier)
    grad_value, grad_gate, grad_w_conv = core_settle(grads, second, 3)
    d_stream, d_branch, grads2 = returning(
        core, exchange_core(branch), stream2, d_stream, norm[2], 1.0, None, None
    )

    d_branch = widen_core(d_branch)
    d_query, d_own, d_left, d_right, d_table = attend_back(
        first_ref, lens, d_branch, heads, left, right, rel, w_attn, chance
    )
    d_key, d_val, branch = heads_in(d_query, d_own, along(d_left, -1), along(d_right, 1), w_attn)
    grads = core_grads(hidden1, d_branch, (d_query, d_key, d_val), context, w_attn[0])
    grad_q, grad_k, grad_v, grad_w_attn = core_settle(grads, second, 4)
    d_stream, d_branch, grads1 = returning(
        core, exchange_core(branch), stream1, d_stream, norm[1], 0.5, None, "out"
    )

    d_branch = widen_tp(d_branch)
    d_before, branch = ffn_backward(d_branch, before0, one_in, one_out)
    grad_in, grad_out = ffn_grads(hidden0, d_before, d_branch, active0, one_in[0])
    grad_one_in, grad_one_out = ffn_settle(grad_in, A_AXES), ffn_settle(grad_out, B_AXES)
    d_stream, _, grads0 = returning(
        core, [exchange_tp(branch)], near, d_stream, norm[0], 1.0, "in", None
    )

    d_rel = (d_table[:HD] + d_table[HD:])[:, :SPAN]
    grad_table = jnp.dot(d_rel, selector.astype(F32).T, precision=lax.Precision.HIGHEST)
    early = jnp.concatenate([tap_grads, affine_grads], 0)
    for mask in bits_of("tp")[::-1]:
        kept, sent = tp_halves(early, mask, 1)
        early = kept + partner(sent, "tp", mask)
    early = jnp.concatenate([early, padded(grad_table)], 0)
    for axis, mask in stages_of(A_AXES):
        early = early + partner(early, axis, mask)
    far_early = swap_core(early)
    grad_table = (early + far_early)[KERNEL + 2 :, :SPAN]
    conv_cut = jnp.concatenate(
        [jnp.where(second, far_early, early), jnp.where(second, early, far_early)], 1
    )[: KERNEL + 2]
    place = (lax.axis_index("row") * 2 + lax.axis_index("core")) * ctxs + lax.axis_index("ctx")
    conv_cut = lax.dynamic_slice_in_dim(conv_cut, place * width, width, 1)
    grad_table = lax.dynamic_slice_in_dim(grad_table, place * table_rows, table_rows, 0)

    norm_grads = jnp.concatenate([grads0, grads1, grads2, grads3, grads4], 0)
    norm_grads = norm_grads_settle(norm_grads, second)
    final = jnp.concatenate([padded(norm_grads), padded(grad_table)], 0)
    for mask in bits_of("tp"):
        final = final + partner(final, "tp", mask)
    norm_grads = final[:10, :local].reshape(5, 2, local)
    grad_table = final[10:, :SPAN]

    return (
        to_natural(result)[None],
        to_natural(d_stream)[None],
        grad_one_in,
        grad_one_out,
        norm_grads[:, 0].T,
        norm_grads[:, 1].T,
        jnp.stack([grad_q, grad_k, grad_v], 1),
        grad_w_attn,
        grad_table,
        jnp.stack([grad_value, grad_gate], 1),
        conv_cut[:KERNEL].T,
        conv_cut[KERNEL],
        conv_cut[KERNEL + 1],
        grad_w_conv,
        grad_two_in,
        grad_two_out,
    )


def solution(mesh):
    shards, ctxs, tp = (mesh.shape[axis] for axis in ("shard", "ctx", "tp"))
    cut = Mesh(mesh.devices.reshape(shards // 2, 2, ctxs, tp), ("row", "core", "ctx", "tp"))
    shard = ("row", "core")
    block = ("row", "core", "ctx")
    every = ("tp", "row", "core", "ctx")
    weight = P(block, "tp")
    narrow = P(block, None)
    deep = P(block, None, "tp")
    frames = P(shard, ("ctx", "tp"), None)
    return jax.shard_map(
        body,
        mesh=cut,
        in_specs=(
            frames, frames, P(shard), P(), weight, weight, narrow, narrow, deep, weight, narrow,
            deep, P(every, None), P(every), P(every), weight, weight, weight,
        ),
        out_specs=(
            frames, frames, weight, weight, narrow, narrow, deep, weight, narrow, deep,
            P(every, None), P(every), P(every), weight, weight, weight,
        ),
        check_vma=False,
    )
```

```python
import functools

import jax
import jax.numpy as jnp
from jax import lax
from jax.experimental import pallas as pl
from jax.experimental.pallas import tpu as pltpu
from jax.sharding import Mesh
from jax.sharding import PartitionSpec as P

D = 1024
HD = 64
KERNEL = 31
LEFT = 64
RIGHT = 16
SPAN = 73
PAIR = 128
KEYS = 256
EPSILON = 1e-05
MASKED = -1e30
SCALE = HD**-0.5
F32 = jnp.float32
BF16 = jnp.bfloat16


def product(left, right):
    return jnp.dot(left, right, preferred_element_type=F32)


def product_nt(left, right):
    return lax.dot_general(left, right, (((1,), (1,)), ((), ())), preferred_element_type=F32)


def product_tn(left, right):
    return lax.dot_general(left, right, (((0,), (0,)), ((), ())), preferred_element_type=F32)


def silu_slope(values):
    logistic = jax.nn.sigmoid(values)
    return logistic * (1.0 + values * (1.0 - logistic))


def bits_of(axis):
    count = lax.axis_size(axis)
    return [1 << k for k in range(count.bit_length() - 1)]


def stream_places():
    rows, ctxs = lax.axis_size("row"), lax.axis_size("ctx")
    return [(0, b, a) for b in range(ctxs) for a in range(rows)] + [
        (1, b, a) for a in range(rows) for b in range(ctxs)
    ]


def ffn_places(core, kind):
    rows, ctxs = lax.axis_size("row"), lax.axis_size("ctx")
    if kind == "in":
        return [(e ^ core, b, a) for e in range(2) for b in range(ctxs) for a in range(rows)]
    return [(e ^ core, b, a) for e in range(2) for a in range(rows) for b in range(ctxs)]


def reorder(value, source, target):
    width = value.shape[-1] // len(source)
    where = {place: k for k, place in enumerate(source)}
    return jnp.concatenate(
        [value[..., where[p] * width : (where[p] + 1) * width] for p in target], -1
    )


def to_ffn(value, kind, second):
    source = stream_places()
    return jnp.where(
        second,
        reorder(value, source, ffn_places(1, kind)),
        reorder(value, source, ffn_places(0, kind)),
    )


def from_ffn(value, kind, second):
    target = stream_places()
    return jnp.where(
        second,
        reorder(value, ffn_places(1, kind), target),
        reorder(value, ffn_places(0, kind), target),
    )


def crossed(blocks):
    rows = lax.axis_size("row")
    flags = [((lax.axis_index("row") & m) != 0, m) for m in bits_of("row")]
    flags += [((lax.axis_index("ctx") & m) != 0, m * rows) for m in bits_of("ctx")]
    for flag, mask in flags:
        blocks = [jnp.where(flag, blocks[i ^ mask], blocks[i]) for i in range(len(blocks))]
    return blocks


def natural_places():
    rows, ctxs = lax.axis_size("row"), lax.axis_size("ctx")
    return [(c, b, a) for a in range(rows) for c in range(2) for b in range(ctxs)]


def tied(*groups):
    return lax.optimization_barrier(groups)


def partner(value, axis, mask):
    count = lax.axis_size(axis)
    return lax.ppermute(value, axis, [(i, i ^ mask) for i in range(count)])


def swap_core(value):
    return partner(value, "core", 1)


def stages_of(axes):
    return [(axis, mask) for axis in axes for mask in bits_of(axis)]


A_AXES = ("row", "ctx")
B_AXES = ("ctx", "row")


def gather_first(weights):
    values = [w[None] for w in weights]
    rounds = [stages_of(axes)[:-1] for axes in (A_AXES, B_AXES)]
    for k in range(len(rounds[0])):
        values = join_pairs(values, [partner(v, *stages[k]) for v, stages in zip(values, rounds)])
    return values


def gather_last(values):
    far = [
        partner(values[0], *stages_of(A_AXES)[-1]),
        partner(values[1], *stages_of(B_AXES)[-1]),
    ]
    return [values[0], far[0], values[1], far[1]]


def ffn_weights(halves):
    other = [swap_core(h) for h in halves]
    return [*halves[:2], *other[:2]], [*halves[2:], *other[2:]]


def settle_open(chunks):
    near_a, far_a, near_b, far_b = chunks
    arrived = [
        partner(far_a, *stages_of(A_AXES)[-1]),
        partner(far_b, *stages_of(B_AXES)[-1]),
    ]
    return [near_a, near_b], arrived


def settle_close(own, far):
    halves = sum_halves(own, far)
    rounds = [stages_of(axes)[:-1][::-1] for axes in (A_AXES, B_AXES)]
    for k in range(len(rounds[0])):
        kept, sent = halves[:2], halves[2:]
        arrived = [partner(s, *stages[k]) for s, stages in zip(sent, rounds)]
        if k < len(rounds[0]) - 1:
            halves = sum_halves(kept, arrived)
    return kept, arrived


def ffn_halves(grads_in, grads_out):
    own = [*grads_in[:2], *grads_out[:2]]
    far = [swap_core(g) for g in (*grads_in[2:], *grads_out[2:])]
    return sum_pairs(own, far, BF16)


def tp_joined(own, arrived, mask, axis):
    upper = (lax.axis_index("tp") & mask) != 0
    return jnp.concatenate(
        [jnp.where(upper, arrived, own), jnp.where(upper, own, arrived)], axis
    )


def core_shares(matrices, second):
    halves = jnp.concatenate(
        [m.reshape(m.shape[0], 2, 1, m.shape[1] // 2) for m in matrices], 2
    )
    own, other = halves[:, 0], halves[:, 1]
    own, other = jnp.where(second, other, own), jnp.where(second, own, other)
    own = own.reshape(own.shape[0], -1)
    other = swap_core(other.reshape(own.shape))
    return jnp.stack([jnp.where(second, other, own), jnp.where(second, own, other)], 0)


def tp_first(value):
    steps = lax.axis_size("tp").bit_length() - 1
    value = value.reshape((2,) + (1,) * steps + value.shape[1:])
    mask = bits_of("tp")[-1]
    return tp_joined(value, partner(value, "tp", mask), mask, 1)


def tp_rest(value):
    for k, mask in enumerate(bits_of("tp")[:-1][::-1]):
        value = tp_joined(value, partner(value, "tp", mask), mask, 2 + k)
    return value.reshape((2, -1) + value.shape[-2:])


def core_finish(ids, kept, arrived, count):
    own, sent = tp_open(ids, kept, arrived)
    for mask in bits_of("tp")[::-1]:
        own, sent = tp_next(ids, own, partner(sent, "tp", mask))
    return core_last(ids, own, swap_core(sent), count)


def along(value, step):
    count = lax.axis_size("ctx") * lax.axis_size("tp")
    pairs = [(i, i + step) for i in range(count) if 0 <= i + step < count]
    return lax.ppermute(value, ("ctx", "tp"), pairs)


def widen_tp(rows):
    return lax.all_gather(rows, "tp", axis=0, tiled=True)


def exchange_tp(partial_value):
    count = lax.axis_size("tp")
    pieces = partial_value.reshape(
        count, partial_value.shape[0] // count, partial_value.shape[1]
    )
    return lax.all_to_all(pieces, "tp", 0, 0)


def widen_core(rows):
    return jnp.concatenate([rows, swap_core(rows)], 0)


def exchange_core(partial_value):
    half = partial_value.shape[0] // 2
    return [partial_value[:half], swap_core(partial_value[half:])]


PARAMS = pltpu.CompilerParams(vmem_limit_bytes=24 << 20)
SMEM = pl.BlockSpec(memory_space=pltpu.SMEM)


def whole(shape):
    return pl.BlockSpec(shape, lambda step: (0,) * len(shape))


def run(kernel, name, outs, *args, smem=0, scratch=()):
    return pl.pallas_call(
        kernel,
        grid=(1,),
        in_specs=[SMEM] * smem + [whole(a.shape) for a in args[smem:]],
        out_specs=[whole(shape) for shape, _ in outs],
        out_shape=[jax.ShapeDtypeStruct(shape, dtype) for shape, dtype in outs],
        scratch_shapes=list(scratch),
        compiler_params=PARAMS,
        name=name,
    )(*args)


def join_kernel(count, *refs):
    for own, far, out_ref in zip(refs[:count], refs[count : 2 * count], refs[2 * count :]):
        half = own.shape[0]
        out_ref[:half] = own[...]
        out_ref[half:] = far[...]


def join_pairs(own, far):
    outs = [((2 * v.shape[0], *v.shape[1:]), v.dtype) for v in own]
    return list(run(functools.partial(join_kernel, len(own)), "join_pairs", outs, *own, *far))


def sum_kernel(count, *refs):
    for own, far, out_ref in zip(refs[:count], refs[count : 2 * count], refs[2 * count :]):
        total = own[...].astype(F32) + far[...].astype(F32)
        out_ref[...] = total.reshape(out_ref.shape).astype(out_ref.dtype)


def sum_pairs(own, far, dtype, shape=None):
    outs = [(shape or v.shape, dtype) for v in own]
    return list(run(functools.partial(sum_kernel, len(own)), "sum_pairs", outs, *own, *far))


def halves_kernel(*refs):
    for k in range(2):
        own, far, kept_ref, sent_ref = refs[k::2]
        total = (own[...].astype(F32) + far[...].astype(F32)).astype(BF16)
        half = total.shape[0] // 2
        kept_ref[...] = total[:half]
        sent_ref[...] = total[half:]


def sum_halves(own, far):
    outs = [((v.shape[0] // 2, *v.shape[1:]), BF16) for v in own] * 2
    return list(run(halves_kernel, "sum_halves", outs, *own, *far))


def tp_open_kernel(ids_ref, *refs):
    own_ref, sent_ref = refs[4:]
    half = own_ref.shape[1]
    upper = lax.rem(ids_ref[3] // half, 2)
    for c in range(2):
        for ref, at in ((own_ref, upper), (sent_ref, 1 - upper)):
            rows = pl.ds(at * half, half)
            total = refs[c][0, rows].astype(F32) + refs[2 + c][0, rows].astype(F32)
            ref[c] = total.astype(BF16)


def tp_open(ids, kept, arrived):
    _, tp, rows, width = kept[0].shape
    outs = [((2, tp // 2, rows, width), BF16)] * 2
    return run(tp_open_kernel, "tp_open", outs, ids, *kept, *arrived, smem=1)


def tp_next_kernel(ids_ref, own_ref, far_ref, kept_ref, sent_ref):
    half = own_ref.shape[1] // 2
    if half:
        upper = lax.rem(ids_ref[3] // half, 2)
        for c in range(2):
            for ref, at in ((kept_ref, upper), (sent_ref, 1 - upper)):
                rows = pl.ds(at * half, half)
                total = own_ref[c, rows].astype(F32) + far_ref[c, rows].astype(F32)
                ref[c] = total.astype(BF16)
    else:
        for ref, at in ((kept_ref, ids_ref[0]), (sent_ref, 1 - ids_ref[0])):
            total = own_ref[at, 0].astype(F32) + far_ref[at, 0].astype(F32)
            ref[...] = total.astype(ref.dtype)


def tp_next(ids, own, far):
    _, tp, rows, width = own.shape
    outs = [((2, tp // 2, rows, width), BF16)] * 2
    if tp == 1:
        outs = [((rows, width), F32), ((rows, width), BF16)]
    return run(tp_next_kernel, "tp_next", outs, ids, own, far, smem=1)


def core_last_kernel(ids_ref, own_ref, far_ref, *outs):
    second = ids_ref[0] == 1
    half = own_ref.shape[1] // len(outs)
    for m, out_ref in enumerate(outs):
        lanes = slice(m * half, (m + 1) * half)
        own, far = own_ref[:, lanes], far_ref[:, lanes].astype(F32)
        out_ref[:, :half] = jnp.where(second, far, own)
        out_ref[:, half:] = jnp.where(second, own, far)


def core_last(ids, own, far, count):
    outs = [((own.shape[0], 2 * own.shape[1] // count), F32)] * count
    return run(core_last_kernel, "core_last", outs, ids, own, far, smem=1)


def stacked(refs):
    local = D // (4 * refs[0].shape[0])
    return jnp.concatenate([r[:, :local].reshape(-1, r.shape[-1]) for r in refs], 0)


def heads_of(refs, start, stop):
    return jnp.concatenate(
        [
            jnp.concatenate(
                [r[:, z, :, start:stop].reshape(-1, stop - start) for r in refs], 0
            )
            for z in range(refs[0].shape[1])
        ],
        1,
    )


def block_order(value, source, target, width):
    where = {place: k for k, place in enumerate(source)}
    return jnp.concatenate(
        [value[:, where[p] * width : (where[p] + 1) * width] for p in target], 1
    )


def by_core(value, kind, second, inverse=False):
    places, width = stream_places(), D // len(stream_places())
    options = []
    for core in range(2):
        other = ffn_places(core, kind)
        options.append(
            block_order(value, other, places, width)
            if inverse
            else block_order(value, places, other, width)
        )
    return jnp.where(second, options[1], options[0])


def grid_places():
    rows, ctxs = lax.axis_size("row"), lax.axis_size("ctx")
    return [(c, b, a) for c in range(2) for b in range(ctxs) for a in range(rows)]


def across(value, ids_ref, source, target):
    grid, rows = grid_places(), lax.axis_size("row")
    width = D // len(grid)
    value = block_order(value, source, grid, width)
    blocks = [value[:, k * width : (k + 1) * width] for k in range(len(grid))]
    flags = [((ids_ref[1] & m) != 0, m) for m in bits_of("row")]
    flags += [((ids_ref[2] & m) != 0, m * rows) for m in bits_of("ctx")]
    for flag, mask in flags:
        blocks = [jnp.where(flag, blocks[i ^ mask], blocks[i]) for i in range(len(blocks))]
    return block_order(jnp.concatenate(blocks, 1), grid, target, width)


def arrive_kernel(ids_ref, inputs_ref, near_ref, wide_ref):
    near = across(inputs_ref[0].astype(F32), ids_ref, natural_places(), stream_places())
    near_ref[...] = near.astype(BF16)
    wide_ref[...] = by_core(near, "in", ids_ref[0] == 1).astype(BF16)


def arrive(ids, inputs):
    shape = inputs.shape[1:]
    return run(arrive_kernel, "arrive", [(shape, BF16), (shape, BF16)], ids, inputs, smem=1)


SMALL = 64


def pack_kernel(count, weight_ref, *refs):
    out_ref, wide = refs[count:]
    local = weight_ref.shape[0]
    out_ref[:local] = weight_ref[...]
    wide[...] = jnp.zeros(wide.shape, F32)
    start = 0
    for ref in refs[:count]:
        rows, width = ref.shape
        wide[start : start + rows, :width] = ref[...].astype(F32)
        start += rows
    for k in range(out_ref.shape[1] // PAIR):
        lanes = slice(k * PAIR, (k + 1) * PAIR)
        out_ref[local:, lanes] = wide[8 * k : 8 * k + 8].astype(BF16)


def pack_below(weight, values):
    shape = (weight.shape[0] + 8, weight.shape[1])
    return run(
        functools.partial(pack_kernel, len(values)), "pack_below", [(shape, BF16)],
        weight, *values,
        scratch=[pltpu.VMEM((SMALL, PAIR), F32)],
    )[0]


def unpack_kernel(ids_ref, *refs):
    chunks, out_ref = refs[:4], refs[4]
    second = ids_ref[0] == 1
    half = out_ref.shape[0] // 2
    for k in range(out_ref.shape[0]):
        for c in range(2):
            own, other = chunks[2 * c + k // half], chunks[2 * (1 - c) + k // half]
            value = jnp.where(second, other[k % half], own[k % half])
            for m in range(SMALL // 8):
                out_ref[k, c, 8 * m : 8 * m + 8] = value[:, m * PAIR : (m + 1) * PAIR]


def unpack_below(ids, chunks, local):
    blocks, _, width = chunks[0].shape
    spec = pl.BlockSpec((blocks, 8, width), lambda step: (0, local // 8, 0))
    shape = (2 * blocks, 2, SMALL, PAIR)
    return pl.pallas_call(
        unpack_kernel,
        grid=(1,),
        in_specs=[SMEM, *[spec] * 4],
        out_specs=whole(shape),
        out_shape=jax.ShapeDtypeStruct(shape, BF16),
        compiler_params=PARAMS,
        name="unpack_below",
    )(ids, *chunks)


def normal_of(stream):
    centre = stream - jnp.mean(stream, axis=-1, keepdims=True)
    inverse = lax.rsqrt(jnp.mean(centre * centre, axis=-1, keepdims=True) + EPSILON)
    return centre * inverse, inverse


def summed(refs):
    total = None
    for ref in refs:
        value = ref[...].astype(F32)
        value = jnp.sum(value, axis=0) if value.ndim == 3 else value
        total = value if total is None else total + value
    return total


def back_through(upstream, normal, inverse, gain, ids_ref, grads_ref):
    scaled = upstream * gain
    grads = jnp.concatenate(
        [
            jnp.sum(upstream * normal, axis=0, keepdims=True),
            jnp.sum(upstream, axis=0, keepdims=True),
        ],
        0,
    )
    grads_ref[...] = across(grads, ids_ref, stream_places(), natural_places())
    return inverse * (
        scaled
        - jnp.mean(scaled, axis=-1, keepdims=True)
        - normal * jnp.mean(scaled * normal, axis=-1, keepdims=True)
    )


def onward_kernel(count, scale, source, target, core_ref, *refs):
    pieces, stream_ref, norm_ref = refs[:count], refs[count], refs[count + 1]
    next_ref, hidden_ref = refs[count + 2 :]
    second = core_ref[0] == 1
    total = summed(pieces)
    if source:
        total = by_core(total, source, second, inverse=True)
    stream = stream_ref[...] + scale * total
    next_ref[...] = stream
    hidden = normal_of(stream)[0] * norm_ref[0:1] + norm_ref[1:2]
    if target:
        hidden = by_core(hidden, target, second)
    hidden_ref[...] = hidden.astype(BF16)


def onward(core, pieces, stream, norm, scale, source, target):
    return run(
        functools.partial(onward_kernel, len(pieces), scale, source, target),
        "onward",
        [(stream.shape, F32), (stream.shape, BF16)],
        core,
        *pieces,
        stream,
        norm,
        smem=1,
    )


def turn_kernel(count, core_ref, *refs):
    pieces, stream_ref, up_ref, norm_ref = refs[:count], *refs[count : count + 3]
    result_ref, back_ref, branch_ref, grads_ref = refs[count + 3 :]
    second = core_ref[0] == 1
    upstream = across(up_ref[0].astype(F32), core_ref, natural_places(), stream_places())
    total = by_core(summed(pieces), "out", second, inverse=True)
    normal, inverse = normal_of(stream_ref[...] + 0.5 * total)
    result = normal * norm_ref[0:1] + norm_ref[1:2]
    result = across(result, core_ref, stream_places(), natural_places())
    result_ref[0] = result.astype(BF16)
    back = back_through(upstream, normal, inverse, norm_ref[0:1], core_ref, grads_ref)
    back_ref[...] = back
    branch_ref[...] = by_core(0.5 * back, "out", second).astype(BF16)


def turn(core, pieces, stream, upstream, norm):
    shape = stream.shape
    return run(
        functools.partial(turn_kernel, len(pieces)),
        "turn",
        [((1, *shape), BF16), (shape, F32), (shape, BF16), ((2, D), F32)],
        core,
        *pieces,
        stream,
        upstream,
        norm,
        smem=1,
    )


def return_kernel(count, scale, source, target, core_ref, *refs):
    pieces, stream_ref, up_ref, norm_ref = refs[:count], *refs[count : count + 3]
    back_ref, grads_ref = refs[count + 3 : count + 5]
    branch_ref = refs[-1]
    second = core_ref[0] == 1
    total = summed(pieces)
    if source:
        total = by_core(total, source, second, inverse=True)
    normal, inverse = normal_of(stream_ref[...].astype(F32))
    back = up_ref[...] + back_through(total, normal, inverse, norm_ref[0:1], core_ref, grads_ref)
    if scale is None:
        back_ref[0] = across(back, core_ref, stream_places(), natural_places())
        return
    back_ref[...] = back
    branch = scale * back
    if target:
        branch = by_core(branch, target, second)
    branch_ref[...] = branch.astype(BF16)


def returning(core, pieces, stream, upstream, norm, scale, source, target):
    shape = stream.shape
    outs = [(shape, F32), ((2, D), F32), (shape, BF16)]
    if scale is None:
        outs = [((1, *shape), F32), ((2, D), F32)]
    return run(
        functools.partial(return_kernel, len(pieces), scale, source, target),
        "returning",
        outs,
        core,
        *pieces,
        stream,
        upstream,
        norm,
        smem=1,
    )


def first_kernel(wide_ref, norm_ref, *refs):
    hidden_ref = refs[8]
    hidden = normal_of(wide_ref[...].astype(F32))[0] * norm_ref[0:1] + norm_ref[1:2]
    hidden_ref[...] = hidden.astype(BF16)
    ffn_forward_kernel(hidden_ref, *refs[:8], *refs[9:])


def ffn_forward_kernel(rows_ref, *refs):
    ins, outs = refs[:4], refs[4:8]
    before_ref, active_ref, branch_ref = refs[8:]
    before = product(rows_ref[...], stacked(ins))
    before_ref[...] = before.astype(BF16)
    active = (before * jax.nn.sigmoid(before)).astype(BF16)
    active_ref[...] = active
    branch_ref[...] = product_nt(active, stacked(outs)).astype(BF16)


def ffn_outs(height, width):
    return [((height, width), BF16), ((height, width), BF16), ((height, D), BF16)]


def ffn_first(wide, norm, ins, outs):
    height, width = wide.shape[0], ins[0].shape[-1]
    return run(
        first_kernel, "ffn_first", [((height, D), BF16), *ffn_outs(height, width)],
        wide, norm, *ins, *outs,
    )


def ffn_forward(hidden, ins, outs):
    height, width = hidden.shape[0], ins[0].shape[-1]
    return run(
        ffn_forward_kernel, "ffn_forward", ffn_outs(height, width), hidden, *ins, *outs
    )


def ffn_backward_kernel(rows_ref, before_ref, *refs):
    ins, outs = refs[:4], refs[4:8]
    d_before_ref, branch_ref = refs[8:]
    d_active = product(rows_ref[...], stacked(outs))
    d_before = (d_active * silu_slope(before_ref[...].astype(F32))).astype(BF16)
    d_before_ref[...] = d_before
    branch_ref[...] = product_nt(d_before, stacked(ins)).astype(BF16)


def ffn_backward(upstream, before, ins, outs):
    height, width = before.shape
    return run(
        ffn_backward_kernel, "ffn_backward", [((height, width), BF16), ((height, D), BF16)],
        upstream, before, *ins, *outs,
    )


def scatter_rows(value, refs):
    rows = value.shape[0] // len(refs)
    for j, ref in enumerate(refs):
        ref[...] = value[j * rows : (j + 1) * rows].reshape(ref.shape)


def ffn_grads_kernel(hidden_ref, d_before_ref, up_ref, active_ref, *outs):
    scatter_rows(product_tn(hidden_ref[...], d_before_ref[...]).astype(BF16), outs[:4])
    scatter_rows(product_tn(up_ref[...], active_ref[...]).astype(BF16), outs[4:])


def ffn_grads(hidden, d_before, upstream, active, like):
    grads = run(
        ffn_grads_kernel, "ffn_grads", [(like.shape, BF16)] * 8,
        hidden, d_before, upstream, active,
    )
    return grads[:4], grads[4:]


def project_kernel(rows_ref, *refs):
    chunks, outs = refs[:4], refs[4:]
    value = product(rows_ref[...], heads_of(chunks, 0, 3 * PAIR)).astype(BF16)
    for z in range(chunks[0].shape[1]):
        for m in range(3):
            outs[m][:, z * PAIR : (z + 1) * PAIR] = value[
                :, (3 * z + m) * PAIR : (3 * z + m + 1) * PAIR
            ]


def project_heads(hidden, chunks):
    shape = (hidden.shape[0], chunks[0].shape[1] * PAIR)
    return run(project_kernel, "project_heads", [(shape, BF16)] * 3, hidden, *chunks)


def core_grads_kernel(count, hidden_ref, up_ref, *refs):
    values, last_ref, outs = refs[:count], refs[count], refs[count + 1 :]
    tp = outs[0].shape[1]
    grads = [product_tn(hidden_ref[...], v[...]).astype(BF16) for v in values]
    grads.append(product_tn(up_ref[...], last_ref[...]).astype(BF16))
    for m, grad in enumerate(grads):
        rows = D // len(outs)
        for j, ref in enumerate(outs):
            for z in range(tp):
                piece = grad[j * rows : (j + 1) * rows, z * PAIR : (z + 1) * PAIR]
                ref[:, z, :, m * PAIR : (m + 1) * PAIR] = piece.reshape(
                    ref.shape[0], ref.shape[2], PAIR
                )


def core_grads(hidden, upstream, values, last, like):
    return run(
        functools.partial(core_grads_kernel, len(values)), "core_grads",
        [(like.shape, BF16)] * 4, hidden, upstream, *values, last,
    )


def interleaved(values):
    tp = values[0].shape[1] // PAIR
    return jnp.concatenate(
        [v[:, z * PAIR : (z + 1) * PAIR] for z in range(tp) for v in values], 1
    )


def window(first, length, height):
    rows = lax.broadcasted_iota(jnp.int32, (height, KEYS), 0)
    lanes = lax.broadcasted_iota(jnp.int32, (height, KEYS), 1)
    offset = lanes - rows
    frame = lanes + (first - LEFT)
    in_band = (offset >= 0) & (offset < SPAN)
    allowed = in_band & (frame >= 0) & (frame < length)
    return in_band, allowed


def both(mask):
    return jnp.concatenate([mask, mask], 0)


def window_of(left_ref, own_ref, right_ref, clip, z, side, height):
    channels = own_ref.shape[1]
    lanes = slice(z * PAIR, (z + 1) * PAIR)
    far = slice(side * channels + z * PAIR, side * channels + (z + 1) * PAIR)
    return jnp.concatenate(
        [
            left_ref[clip, :, far],
            own_ref[clip * height : (clip + 1) * height, lanes],
            right_ref[clip, :, far],
            jnp.zeros((KEYS - LEFT - RIGHT - height, PAIR), BF16),
        ],
        0,
    )


def split_heads(value, odd):
    zero = jnp.zeros_like(value)
    return jnp.concatenate([jnp.where(odd, zero, value), jnp.where(odd, value, zero)], 0)


def merge_heads(value, odd):
    height = value.shape[0] // 2
    return jnp.where(odd, value[height:], value[:height])


def attend_kernel(
    height, first_ref, lens_ref, q_ref, k_ref, v_ref, left_ref, right_ref, rel_ref,
    c0, c1, c2, c3, context_ref, chance_ref, branch_ref
):
    odd = lax.broadcasted_iota(jnp.int32, (1, PAIR), 1) >= HD
    for clip in range(2):
        rows = slice(clip * height, (clip + 1) * height)
        in_band, allowed = window(first_ref[0], lens_ref[clip], height)
        in_band, allowed = both(in_band), both(allowed)
        for z in range(c0.shape[1]):
            lanes = slice(z * PAIR, (z + 1) * PAIR)
            query = split_heads(q_ref[rows, lanes], odd)
            keys = window_of(left_ref, k_ref, right_ref, clip, z, 0, height)
            values = window_of(left_ref, v_ref, right_ref, clip, z, 1, height)
            relative = product(query, rel_ref[...])
            relative = jnp.concatenate([relative, jnp.zeros((2 * height, KEYS - PAIR), F32)], 1)
            relative = jnp.concatenate(
                [
                    pltpu.roll(relative[:height], 0, 1, stride=1, stride_axis=0),
                    pltpu.roll(relative[height:], 0, 1, stride=1, stride_axis=0),
                ],
                0,
            )
            score = (product_nt(query, keys) + relative) * SCALE
            masked = jnp.where(allowed, score, MASKED)
            ceiling = jnp.max(masked, axis=-1, keepdims=True)
            raised = jnp.where(in_band, jnp.exp(masked - ceiling), 0.0)
            chance = raised * (1.0 / jnp.sum(raised, axis=-1, keepdims=True))
            chance_ref[clip, z] = chance
            context = merge_heads(product(chance.astype(BF16), values), odd)
            context_ref[rows, lanes] = context.astype(BF16)
    weight = heads_of((c0, c1, c2, c3), 3 * PAIR, 4 * PAIR)
    branch_ref[...] = product_nt(context_ref[...], weight).astype(BF16)


def attend(first, lens, heads, left, right, rel, chunks):
    height, channels, tp = heads[0].shape[0] // 2, heads[0].shape[1], chunks[0].shape[1]
    return run(
        functools.partial(attend_kernel, height),
        "attend",
        [
            ((2 * height, channels), BF16),
            ((2, tp, 2 * height, KEYS), F32),
            ((2 * height, D), BF16),
        ],
        first, lens, *heads, left, right, rel, *chunks,
        smem=2,
    )


def attend_back_kernel(
    height, first_ref, lens_ref, up_ref, q_ref, k_ref, v_ref, left_ref, right_ref, rel_ref,
    c0, c1, c2, c3, chance_ref, dq_ref, own_ref, d_left_ref, d_right_ref, table_ref
):
    odd = lax.broadcasted_iota(jnp.int32, (1, PAIR), 1) >= HD
    weight = heads_of((c0, c1, c2, c3), 3 * PAIR, 4 * PAIR)
    d_context = product(up_ref[...], weight).astype(BF16)
    table = jnp.zeros((PAIR, PAIR), F32)
    flip = (
        lax.broadcasted_iota(jnp.int32, (height, height), 0)
        + lax.broadcasted_iota(jnp.int32, (height, height), 1)
        == height - 1
    ).astype(BF16)
    for clip in range(2):
        rows = slice(clip * height, (clip + 1) * height)
        allowed = both(window(first_ref[0], lens_ref[clip], height)[1])
        for z in range(c0.shape[1]):
            lanes = slice(z * PAIR, (z + 1) * PAIR)
            query = split_heads(q_ref[rows, lanes], odd)
            upstream = split_heads(d_context[rows, lanes], odd)
            keys = window_of(left_ref, k_ref, right_ref, clip, z, 0, height)
            values = window_of(left_ref, v_ref, right_ref, clip, z, 1, height)
            chance = chance_ref[clip, z]
            d_chance = product_nt(upstream, values)
            inner = jnp.sum(d_chance * chance, axis=-1, keepdims=True)
            d_score = jnp.where(allowed, chance * (d_chance - inner), 0.0).astype(BF16)
            d_values = product_tn(chance.astype(BF16), upstream)
            d_keys = product_tn(d_score, query) * SCALE
            relative = []
            for head in range(2):
                turned_rows = product(flip, d_score[head * height : (head + 1) * height])
                rolled = pltpu.roll(
                    turned_rows, KEYS - height + 1, 1, stride=1, stride_axis=0
                )[:, :PAIR].astype(BF16)
                relative.append(product(flip, rolled).astype(BF16))
            relative = jnp.concatenate(relative, 0)
            d_query = product(d_score, keys) + product_nt(relative, rel_ref[...])
            dq_ref[rows, lanes] = (merge_heads(d_query, odd) * SCALE).astype(BF16)
            table += product_tn(query, relative)
            for slot, value in ((0, d_keys), (1, d_values)):
                d_left_ref[slot, clip, :, lanes] = value[:LEFT].astype(BF16)
                own_ref[slot, rows, lanes] = value[LEFT : LEFT + height]
                d_right_ref[slot, clip, :, lanes] = value[
                    LEFT + height : LEFT + height + RIGHT
                ].astype(BF16)
    table_ref[...] = table * SCALE


def attend_back(first, lens, upstream, heads, left, right, rel, chunks, chance):
    height, channels = heads[0].shape[0] // 2, heads[0].shape[1]
    return run(
        functools.partial(attend_back_kernel, height),
        "attend_back",
        [
            ((2 * height, channels), BF16),
            ((2, 2 * height, channels), F32),
            ((2, 2, LEFT, channels), BF16),
            ((2, 2, RIGHT, channels), BF16),
            ((PAIR, PAIR), F32),
        ],
        first, lens, upstream, *heads, left, right, rel, *chunks, chance,
        smem=2,
    )


def heads_in_kernel(height, dq_ref, own_ref, left_ref, right_ref, *refs):
    chunks, dk_ref, dv_ref, branch_ref = refs[:4], *refs[4:]
    for slot, out_ref in ((0, dk_ref), (1, dv_ref)):
        for clip in range(2):
            start = clip * height
            own = own_ref[slot, start : start + height]
            top = own[:RIGHT] + right_ref[slot, clip].astype(F32)
            own = jnp.concatenate([top, own[RIGHT:]], 0)
            low = own[height - LEFT :] + left_ref[slot, clip].astype(F32)
            own = jnp.concatenate([own[: height - LEFT], low], 0)
            out_ref[start : start + height] = own.astype(BF16)
    value = interleaved([dq_ref[...], dk_ref[...], dv_ref[...]])
    branch_ref[...] = product_nt(value, heads_of(chunks, 0, 3 * PAIR)).astype(BF16)


def heads_in(d_query, own, from_next, from_last, chunks):
    shape = d_query.shape
    return run(
        functools.partial(heads_in_kernel, shape[0] // 2), "heads_in",
        [(shape, BF16), (shape, BF16), ((shape[0], D), BF16)],
        d_query, own, from_next, from_last, *chunks,
    )


REACH = 32


def gate_kernel(rows_ref, live_ref, *refs):
    chunks, value_ref, logistic_ref, gated_ref = refs[:4], *refs[4:]
    value = product(rows_ref[...], heads_of(chunks, 0, 2 * PAIR))
    for z in range(chunks[0].shape[1]):
        lanes = slice(z * PAIR, (z + 1) * PAIR)
        linear = value[:, 2 * z * PAIR : (2 * z + 1) * PAIR]
        logistic = jax.nn.sigmoid(value[:, (2 * z + 1) * PAIR : (2 * z + 2) * PAIR])
        value_ref[:, lanes] = linear
        logistic_ref[:, lanes] = logistic
        gated_ref[:, lanes] = (linear * logistic * live_ref[...]).astype(BF16)


def gate_channels(hidden, live, chunks):
    shape = (hidden.shape[0], chunks[0].shape[1] * PAIR)
    return run(
        gate_kernel, "gate_channels", [(shape, F32), (shape, F32), (shape, BF16)],
        hidden, live, *chunks,
    )


def extend(earlier_ref, own_ref, wide, height):
    for clip in range(2):
        wide[clip, :REACH] = earlier_ref[clip].astype(F32)
        wide[clip, REACH : REACH + height] = own_ref[
            clip * height : (clip + 1) * height
        ].astype(F32)


def mix_kernel(height, gated_ref, earlier_ref, taps_ref, mixed_ref, sums_ref, wide):
    extend(earlier_ref, gated_ref, wide, height)
    lead = REACH - (KERNEL - 1)
    for clip in range(2):
        rows = slice(clip * height, (clip + 1) * height)
        first = second = jnp.zeros((height, 1), F32)
        for z in range(gated_ref.shape[1] // PAIR):
            lanes = slice(z * PAIR, (z + 1) * PAIR)
            mixed = wide[clip, lead : lead + height, lanes] * taps_ref[0:1, lanes]
            for j in range(1, KERNEL):
                mixed += wide[clip, lead + j : lead + j + height, lanes] * taps_ref[j : j + 1, lanes]
            mixed_ref[rows, lanes] = mixed
            first += jnp.sum(mixed, axis=1, keepdims=True)
            second += jnp.sum(mixed * mixed, axis=1, keepdims=True)
        sums_ref[rows] = jnp.concatenate([first, second], 1)


def mix_channels(gated, earlier, taps):
    height, channels = gated.shape[0] // 2, gated.shape[1]
    return run(
        functools.partial(mix_kernel, height), "mix_channels",
        [((2 * height, channels), F32), ((2 * height, 2), F32)],
        gated, earlier, taps,
        scratch=[pltpu.VMEM((2, height + REACH, channels), F32)],
    )


def paired(own_ref, other_ref):
    half = own_ref.shape[0] // 2
    other = other_ref[...]
    return (own_ref[...] + jnp.concatenate([other[half:], other[:half]], 0)) * (1.0 / D)


def conv_norm(mixed_ref, sums_ref, other_ref):
    means = paired(sums_ref, other_ref)
    centre, square = means[:, 0:1], means[:, 1:2]
    inverse = lax.rsqrt(square - centre * centre + EPSILON)
    return (mixed_ref[...] - centre) * inverse, inverse


def conv_out_kernel(mixed_ref, sums_ref, other_ref, affine_ref, *refs):
    chunks, active_ref, branch_ref = refs[:4], *refs[4:]
    normal, _ = conv_norm(mixed_ref, sums_ref, other_ref)
    levels = normal * affine_ref[0:1] + affine_ref[1:2]
    active = (levels * jax.nn.sigmoid(levels)).astype(BF16)
    active_ref[...] = active
    weight = heads_of(chunks, 2 * PAIR, 3 * PAIR)
    branch_ref[...] = product_nt(active, weight).astype(BF16)


def conv_forward(mixed, sums, other, affine, chunks):
    return run(
        conv_out_kernel, "conv_forward", [(mixed.shape, BF16), ((mixed.shape[0], D), BF16)],
        mixed, sums, other, affine, *chunks,
    )


def conv_level_kernel(up_ref, mixed_ref, sums_ref, other_ref, affine_ref, *refs):
    chunks, scaled_ref, totals_ref, affine_grad_ref = refs[:4], *refs[4:]
    normal, _ = conv_norm(mixed_ref, sums_ref, other_ref)
    levels = normal * affine_ref[0:1] + affine_ref[1:2]
    weight = heads_of(chunks, 2 * PAIR, 3 * PAIR)
    d_levels = product(up_ref[...], weight) * silu_slope(levels)
    scaled = d_levels * affine_ref[0:1]
    scaled_ref[...] = scaled
    totals_ref[...] = jnp.concatenate(
        [
            jnp.sum(scaled, axis=1, keepdims=True),
            jnp.sum(scaled * normal, axis=1, keepdims=True),
        ],
        1,
    )
    affine_grad_ref[0:1] = jnp.sum(d_levels * normal, axis=0, keepdims=True)
    affine_grad_ref[1:2] = jnp.sum(d_levels, axis=0, keepdims=True)


def conv_levels_back(upstream, mixed, sums, other, affine, chunks):
    return run(
        conv_level_kernel, "conv_levels_back",
        [(mixed.shape, F32), (sums.shape, F32), ((2, mixed.shape[1]), F32)],
        upstream, mixed, sums, other, affine, *chunks,
    )


def unmix_kernel(
    height, scaled_ref, totals_ref, far_totals_ref, mixed_ref, sums_ref, other_ref, taps_ref,
    d_mixed_ref, own_ref, earlier_ref, wide
):
    normal, inverse = conv_norm(mixed_ref, sums_ref, other_ref)
    means = paired(totals_ref, far_totals_ref)
    d_mixed = inverse * (scaled_ref[...] - means[:, 0:1] - normal * means[:, 1:2])
    d_mixed_ref[...] = d_mixed
    for clip in range(2):
        rows = slice(clip * height, (clip + 1) * height)
        wide[clip, :REACH] = jnp.zeros((REACH, d_mixed.shape[1]), F32)
        wide[clip, REACH : REACH + height] = d_mixed[rows]
        wide[clip, REACH + height :] = jnp.zeros((REACH, d_mixed.shape[1]), F32)
        last = REACH + KERNEL - 1
        for z in range(d_mixed.shape[1] // PAIR):
            lanes = slice(z * PAIR, (z + 1) * PAIR)
            own = wide[clip, last : last + height, lanes] * taps_ref[0:1, lanes]
            for j in range(1, KERNEL):
                own += wide[clip, last - j : last - j + height, lanes] * taps_ref[j : j + 1, lanes]
            own_ref[rows, lanes] = own
            early = wide[clip, KERNEL - 1 : KERNEL - 1 + REACH, lanes] * taps_ref[0:1, lanes]
            for j in range(1, KERNEL):
                start = KERNEL - 1 - j
                early += wide[clip, start : start + REACH, lanes] * taps_ref[j : j + 1, lanes]
            earlier_ref[clip, :, lanes] = early


def unmix_channels(scaled, totals, far_totals, mixed, sums, other, taps):
    height, channels = mixed.shape[0] // 2, mixed.shape[1]
    return run(
        functools.partial(unmix_kernel, height), "unmix_channels",
        [(mixed.shape, F32), (mixed.shape, F32), ((2, REACH, channels), F32)],
        scaled, totals, far_totals, mixed, sums, other, taps,
        scratch=[pltpu.VMEM((2, height + 2 * REACH, channels), F32)],
    )


def gate_back_kernel(height, own_ref, later_ref, value_ref, logistic_ref, live_ref, *refs):
    chunks, d_value_ref, d_gate_ref, branch_ref = refs[:4], *refs[4:]
    for clip in range(2):
        rows = slice(clip * height, (clip + 1) * height)
        own = own_ref[rows]
        low = own[height - REACH :] + later_ref[clip]
        own = jnp.concatenate([own[: height - REACH], low], 0) * live_ref[rows]
        logistic = logistic_ref[rows]
        d_value_ref[rows] = (own * logistic).astype(BF16)
        d_gate_ref[rows] = (own * value_ref[rows] * logistic * (1.0 - logistic)).astype(BF16)
    value = interleaved([d_value_ref[...], d_gate_ref[...]])
    branch_ref[...] = product_nt(value, heads_of(chunks, 0, 2 * PAIR)).astype(BF16)


def gate_back(own, later, value_half, logistic, live, chunks):
    shape = own.shape
    return run(
        functools.partial(gate_back_kernel, shape[0] // 2), "gate_back",
        [(shape, BF16), (shape, BF16), ((shape[0], D), BF16)],
        own, later, value_half, logistic, live, *chunks,
    )


def tap_kernel(height, d_mixed_ref, gated_ref, earlier_ref, taps_ref, wide):
    extend(earlier_ref, gated_ref, wide, height)
    lead = REACH - (KERNEL - 1)
    for z in range(gated_ref.shape[1] // PAIR):
        lanes = slice(z * PAIR, (z + 1) * PAIR)
        for j in range(KERNEL):
            total = jnp.zeros((1, PAIR), F32)
            for clip in range(2):
                total += jnp.sum(
                    d_mixed_ref[clip * height : (clip + 1) * height, lanes]
                    * wide[clip, lead + j : lead + j + height, lanes],
                    axis=0,
                    keepdims=True,
                )
            taps_ref[j : j + 1, lanes] = total


def tap_grads_of(d_mixed, gated, earlier):
    height, channels = gated.shape[0] // 2, gated.shape[1]
    return run(
        functools.partial(tap_kernel, height), "tap_grads", [((KERNEL, channels), F32)],
        d_mixed, gated, earlier,
        scratch=[pltpu.VMEM((2, height + REACH, channels), F32)],
    )[0]


def body(
    inputs,
    cotangent,
    lengths,
    buckets,
    ffn1_in,
    ffn1_out,
    norm_gains,
    norm_biases,
    qkv_weight,
    attn_out,
    distance,
    glu_in,
    depthwise,
    conv_gain,
    conv_bias,
    conv_out,
    ffn2_in,
    ffn2_out,
):
    rows, ctxs, tp = lax.axis_size("row"), lax.axis_size("ctx"), lax.axis_size("tp")
    second = lax.axis_index("core") == 1
    core = jnp.stack([lax.axis_index(axis) for axis in ("core", "row", "ctx", "tp")])
    core = core.astype(jnp.int32)
    local = ffn1_in.shape[0]
    height = inputs.shape[1]
    first = (lax.axis_index("ctx") * tp + lax.axis_index("tp")) * height
    attn_shares = core_shares(
        [qkv_weight[:, 0], qkv_weight[:, 1], qkv_weight[:, 2], attn_out], second
    )
    near, rows_in = arrive(core, inputs)
    small = [norm_gains.T, norm_biases.T, depthwise.T, conv_gain[None], conv_bias[None], distance]
    joined = gather_first([pack_below(ffn1_in, small), ffn1_out])
    attn_half = tp_first(attn_shares)
    joined, attn_half, wide_inputs = tied(joined, attn_half, widen_tp(rows_in))
    halves = gather_last(joined)
    attn_rows = tp_rest(attn_half)
    conv_shares = core_shares([glu_in[:, 0], glu_in[:, 1], conv_out], second)
    conv_shares, attn_rows, halves = tied(conv_shares, attn_rows, halves)
    one_in, one_out = ffn_weights(halves)
    conv_half = tp_first(conv_shares)
    w_attn = gather_last(gather_first(attn_rows))
    conv_rows, w_attn = tied(tp_rest(conv_half), w_attn)
    w_conv = gather_last(gather_first(conv_rows))
    two_rows, w_conv = tied([ffn2_in, ffn2_out], w_conv)
    two_in, two_out = ffn_weights(gather_last(gather_first(two_rows)))

    lens = widen_core(lengths)
    frame_ids = first + jnp.arange(height, dtype=jnp.int32)
    live = (frame_ids[None, :] < lens[:, None]).astype(F32).reshape(2 * height, 1)

    table_rows, width = distance.shape[0], conv_gain.shape[0]
    cube = unpack_below(core, one_in, local)
    take = lambda c, k: cube[k, c]
    norms = jnp.concatenate(
        [take(c, b * rows + a)[:10, :local] for c, b, a in stream_places()], 1
    ).astype(F32)
    norm = [jnp.stack([norms[k], norms[5 + k]], 0) for k in range(5)]
    blocks = [
        crossed([take(c, k)[10:] for k in range(rows * ctxs)]) for c in range(2)
    ]
    natural = [blocks[c][b * rows + a] for c, b, a in natural_places()]
    table_all = jnp.concatenate(
        [n[KERNEL + 2 : KERNEL + 2 + table_rows, :SPAN] for n in natural], 0
    )
    conv_small = jnp.concatenate([n[: KERNEL + 2, :width] for n in natural], 1)
    half = conv_small.shape[1] // 2
    conv_small = jnp.where(second, conv_small[:, half:], conv_small[:, :half])
    for mask in bits_of("tp"):
        conv_small = tp_joined(conv_small, partner(conv_small, "tp", mask), mask, 1)
    conv_small = conv_small.astype(F32)
    taps, affine = conv_small[:KERNEL], conv_small[KERNEL:]

    selector = (jnp.arange(SPAN, dtype=jnp.int32)[:, None] == buckets[None, :]).astype(BF16)
    rel = product(table_all, selector).astype(BF16)
    rel = jnp.pad(jnp.concatenate([rel, rel], 0), ((0, 0), (0, PAIR - SPAN)))

    hidden0, before0, active0, branch = ffn_first(
        wide_inputs, to_ffn(norm[0], "in", second), one_in, one_out
    )
    stream1, hidden1 = onward(
        core, [exchange_tp(branch)], near.astype(F32), norm[1], 0.5, "out", None
    )

    hidden1 = widen_core(hidden1)
    heads = project_heads(hidden1, w_attn)
    channels = heads[0].shape[1]
    key_value = [h.reshape(2, height, channels) for h in heads[1:]]
    left = along(jnp.concatenate([h[:, height - LEFT :] for h in key_value], 2), 1)
    right = along(jnp.concatenate([h[:, :RIGHT] for h in key_value], 2), -1)
    first_ref = first.reshape(1).astype(jnp.int32)
    context, chance, branch = attend(first_ref, lens, heads, left, right, rel, w_attn)
    stream2, hidden2 = onward(core, exchange_core(branch), stream1, norm[2], 1.0, None, None)

    hidden2 = widen_core(hidden2)
    value_half, logistic, gated = gate_channels(hidden2, live, w_conv)
    earlier = along(gated.reshape(2, height, channels)[:, height - REACH :], 1)
    mixed, sums = mix_channels(gated, earlier, taps)
    other = swap_core(sums)
    active_conv, branch = conv_forward(mixed, sums, other, affine, w_conv)
    stream3, hidden3 = onward(core, exchange_core(branch), stream2, norm[3], 1.0, None, "in")

    hidden3 = widen_tp(hidden3)
    before3, active3, branch = ffn_forward(hidden3, two_in, two_out)
    result, d_stream, d_branch, grads4 = turn(
        core, [exchange_tp(branch)], stream3, cotangent, norm[4]
    )

    d_branch = widen_tp(d_branch)
    d_before, branch = ffn_backward(d_branch, before3, two_in, two_out)
    two_own, two_far = settle_open(
        ffn_halves(*ffn_grads(hidden3, d_before, d_branch, active3, two_in[0]))
    )
    d_stream, grads3, d_branch = returning(
        core, [exchange_tp(branch)], stream3, d_stream, norm[3], 1.0, "in", None
    )

    d_branch = widen_core(d_branch)
    scaled, totals, affine_grads = conv_levels_back(d_branch, mixed, sums, other, affine, w_conv)
    d_mixed, d_own, d_earlier = unmix_channels(
        scaled, totals, swap_core(totals), mixed, sums, other, taps
    )
    two_own, two_far = settle_close(two_own, two_far)
    later = along(d_earlier, -1)
    d_value, d_gate, branch = gate_back(d_own, later, value_half, logistic, live, w_conv)
    conv_grads = core_grads(hidden2, d_branch, (d_value, d_gate), active_conv, w_conv[0])
    conv_own, conv_far = settle_open(conv_grads)
    d_stream, grads2, d_branch = returning(
        core, exchange_core(branch), stream2, d_stream, norm[2], 1.0, None, None
    )

    d_branch = widen_core(d_branch)
    grad_two_in, grad_two_out = sum_pairs(two_own, two_far, F32, ffn2_in.shape)
    d_query, d_own, d_left, d_right, d_table = attend_back(
        first_ref, lens, d_branch, heads, left, right, rel, w_attn, chance
    )
    from_next = along(d_left, -1)
    d_key, d_val, branch = heads_in(d_query, d_own, from_next, along(d_right, 1), w_attn)
    conv_own, conv_far = settle_close(conv_own, conv_far)
    attn_grads = core_grads(hidden1, d_branch, (d_query, d_key, d_val), context, w_attn[0])
    d_stream, grads1, d_branch = returning(
        core, exchange_core(branch), stream1, d_stream, norm[1], 0.5, None, "out"
    )
    d_branch, attn_grads = tied(d_branch, attn_grads)
    attn_own, attn_far = settle_open(attn_grads)

    d_branch, attn_far = tied(widen_tp(d_branch), attn_far)
    grad_value, grad_gate, grad_w_conv = core_finish(core, conv_own, conv_far, 3)
    d_before, branch = ffn_backward(d_branch, before0, one_in, one_out)
    one_grads = ffn_grads(hidden0, d_before, d_branch, active0, one_out[0])
    one_grads, attn_far = tied(one_grads, attn_far)
    attn_own, attn_far = settle_close(attn_own, attn_far)
    one_own, one_far = settle_open(ffn_halves(*one_grads))
    pieces = exchange_tp(branch)
    grad_q, grad_k, grad_v, grad_w_attn = core_finish(core, attn_own, attn_far, 4)
    input_grad, grads0 = returning(
        core, [pieces], near, d_stream, norm[0], None, "in", None
    )
    one_own, one_far = settle_close(one_own, one_far)
    grad_one_in, grad_one_out = sum_pairs(one_own, one_far, F32, ffn1_in.shape)

    d_rel = (d_table[:HD] + d_table[HD:])[:, :SPAN]
    grad_table = jnp.dot(d_rel, selector.astype(F32).T, precision=lax.Precision.HIGHEST)
    grad_table = jnp.pad(grad_table, ((0, 0), (0, PAIR - SPAN)))
    wide = tp * half
    fold_rows = lambda v: jnp.concatenate(
        [v[:, k : k + wide] for k in range(0, v.shape[1], wide)], 0
    )
    tap_grads = tap_grads_of(d_mixed, gated, earlier)
    packed = jnp.concatenate(
        [
            tap_grads,
            affine_grads,
            grad_table.reshape(-1, wide),
            *[fold_rows(g) for g in (grads4, grads3, grads2, grads1, grads0)],
        ],
        0,
    )
    for axis, mask in [*stages_of(A_AXES), *stages_of(("tp",))]:
        packed = packed + partner(packed, axis, mask)
    far_packed = swap_core(packed)
    total = (packed + far_packed)[KERNEL + 2 :]
    table_size = grad_table.size // wide
    grad_table = total[:table_size].reshape(HD, PAIR)[:, :SPAN]
    norm_grads = total[table_size:].reshape(5, D // wide, 2, wide)
    norm_grads = norm_grads.transpose(0, 2, 1, 3).reshape(10, D)[::-1]
    conv_cut = jnp.concatenate(
        [
            jnp.where(second, far_packed, packed)[: KERNEL + 2].reshape(-1, tp, half),
            jnp.where(second, packed, far_packed)[: KERNEL + 2].reshape(-1, tp, half),
        ],
        2,
    )
    place = (lax.axis_index("row") * 2 + lax.axis_index("core")) * ctxs + lax.axis_index("ctx")
    conv_cut = lax.dynamic_index_in_dim(conv_cut, lax.axis_index("tp"), 1, keepdims=False)
    conv_cut = lax.dynamic_slice_in_dim(conv_cut, place * width, width, 1)
    grad_table = lax.dynamic_slice_in_dim(grad_table, place * table_rows, table_rows, 0)
    norm_grads = lax.dynamic_slice_in_dim(norm_grads, place * local, local, 1)

    return (
        result,
        input_grad,
        grad_one_in,
        grad_one_out,
        norm_grads[1::2].T,
        norm_grads[::2].T,
        jnp.stack([grad_q, grad_k, grad_v], 1),
        grad_w_attn,
        grad_table,
        jnp.stack([grad_value, grad_gate], 1),
        conv_cut[:KERNEL].T,
        conv_cut[KERNEL],
        conv_cut[KERNEL + 1],
        grad_w_conv,
        grad_two_in,
        grad_two_out,
    )


def solution(mesh):
    shards, ctxs, tp = (mesh.shape[axis] for axis in ("shard", "ctx", "tp"))
    cut = Mesh(mesh.devices.reshape(shards // 2, 2, ctxs, tp), ("row", "core", "ctx", "tp"))
    shard = ("row", "core")
    block = ("row", "core", "ctx")
    every = ("tp", "row", "core", "ctx")
    weight = P(block, "tp")
    narrow = P(block, None)
    deep = P(block, None, "tp")
    frames = P(shard, ("ctx", "tp"), None)
    return jax.shard_map(
        body,
        mesh=cut,
        in_specs=(
            frames, frames, P(shard), P(), weight, weight, narrow, narrow, deep, weight, narrow,
            deep, P(every, None), P(every), P(every), weight, weight, weight,
        ),
        out_specs=(
            frames, frames, weight, weight, narrow, narrow, deep, weight, narrow, deep,
            P(every, None), P(every), P(every), weight, weight, weight,
        ),
        check_vma=False,
    )
```

```python
import functools

import jax
import jax.numpy as jnp
from jax import lax
from jax.experimental import pallas as pl
from jax.experimental.pallas import tpu as pltpu
from jax.sharding import Mesh
from jax.sharding import PartitionSpec as P

D = 1024
HD = 64
KERNEL = 31
LEFT = 64
RIGHT = 16
SPAN = 73
PAIR = 128
KEYS = 256
EPSILON = 1e-05
MASKED = -1e30
SCALE = HD**-0.5
F32 = jnp.float32
BF16 = jnp.bfloat16


def product(left, right):
    return jnp.dot(left, right, preferred_element_type=F32)


def product_nt(left, right):
    return lax.dot_general(left, right, (((1,), (1,)), ((), ())), preferred_element_type=F32)


def product_tn(left, right):
    return lax.dot_general(left, right, (((0,), (0,)), ((), ())), preferred_element_type=F32)


def silu_slope(values):
    logistic = jax.nn.sigmoid(values)
    return logistic * (1.0 + values * (1.0 - logistic))


def bits_of(axis):
    count = lax.axis_size(axis)
    return [1 << k for k in range(count.bit_length() - 1)]


def stream_places():
    rows, ctxs = lax.axis_size("row"), lax.axis_size("ctx")
    return [(0, b, a) for b in range(ctxs) for a in range(rows)] + [
        (1, b, a) for a in range(rows) for b in range(ctxs)
    ]


def ffn_places(core, kind):
    rows, ctxs = lax.axis_size("row"), lax.axis_size("ctx")
    if kind == "in":
        return [(e ^ core, b, a) for e in range(2) for b in range(ctxs) for a in range(rows)]
    return [(e ^ core, b, a) for e in range(2) for a in range(rows) for b in range(ctxs)]


def reorder(value, source, target):
    width = value.shape[-1] // len(source)
    where = {place: k for k, place in enumerate(source)}
    return jnp.concatenate(
        [value[..., where[p] * width : (where[p] + 1) * width] for p in target], -1
    )


def to_ffn(value, kind, second):
    source = stream_places()
    return jnp.where(
        second,
        reorder(value, source, ffn_places(1, kind)),
        reorder(value, source, ffn_places(0, kind)),
    )


def from_ffn(value, kind, second):
    target = stream_places()
    return jnp.where(
        second,
        reorder(value, ffn_places(1, kind), target),
        reorder(value, ffn_places(0, kind), target),
    )


def crossed(blocks):
    rows = lax.axis_size("row")
    flags = [((lax.axis_index("row") & m) != 0, m) for m in bits_of("row")]
    flags += [((lax.axis_index("ctx") & m) != 0, m * rows) for m in bits_of("ctx")]
    for flag, mask in flags:
        blocks = [jnp.where(flag, blocks[i ^ mask], blocks[i]) for i in range(len(blocks))]
    return blocks


def natural_places():
    rows, ctxs = lax.axis_size("row"), lax.axis_size("ctx")
    return [(c, b, a) for a in range(rows) for c in range(2) for b in range(ctxs)]


def tied(*groups):
    return lax.optimization_barrier(groups)


def partner(value, axis, mask):
    count = lax.axis_size(axis)
    return lax.ppermute(value, axis, [(i, i ^ mask) for i in range(count)])


def swap_core(value):
    return partner(value, "core", 1)


def stages_of(axes):
    return [(axis, mask) for axis in axes for mask in bits_of(axis)]


A_AXES = ("row", "ctx")
B_AXES = ("ctx", "row")


def gather_first(weights):
    values = [w[None] for w in weights]
    rounds = [stages_of(axes)[:-1] for axes in (A_AXES, B_AXES)]
    for k in range(len(rounds[0])):
        values = join_pairs(values, [partner(v, *stages[k]) for v, stages in zip(values, rounds)])
    return values


def gather_last(values):
    far = [
        partner(values[0], *stages_of(A_AXES)[-1]),
        partner(values[1], *stages_of(B_AXES)[-1]),
    ]
    return [values[0], far[0], values[1], far[1]]


def ffn_weights(halves):
    other = [swap_core(h) for h in halves]
    return [*halves[:2], *other[:2]], [*halves[2:], *other[2:]]


def settle_open(chunks):
    near_a, far_a, near_b, far_b = chunks
    arrived = [
        partner(far_a, *stages_of(A_AXES)[-1]),
        partner(far_b, *stages_of(B_AXES)[-1]),
    ]
    return [near_a, near_b], arrived


def settle_close(own, far):
    halves = sum_halves(own, far)
    rounds = [stages_of(axes)[:-1][::-1] for axes in (A_AXES, B_AXES)]
    for k in range(len(rounds[0])):
        kept, sent = halves[:2], halves[2:]
        arrived = [partner(s, *stages[k]) for s, stages in zip(sent, rounds)]
        if k < len(rounds[0]) - 1:
            halves = sum_halves(kept, arrived)
    return kept, arrived


def ffn_halves(grads_in, grads_out):
    own = [*grads_in[:2], *grads_out[:2]]
    far = [swap_core(g) for g in (*grads_in[2:], *grads_out[2:])]
    return sum_pairs(own, far, BF16)


def tp_joined(own, arrived, mask, axis):
    upper = (lax.axis_index("tp") & mask) != 0
    return jnp.concatenate(
        [jnp.where(upper, arrived, own), jnp.where(upper, own, arrived)], axis
    )


def tp_first(value):
    steps = lax.axis_size("tp").bit_length() - 1
    value = value.reshape((2,) + (1,) * steps + value.shape[1:])
    mask = bits_of("tp")[-1]
    return tp_joined(value, partner(value, "tp", mask), mask, 1)


def tp_rest(value):
    for k, mask in enumerate(bits_of("tp")[:-1][::-1]):
        value = tp_joined(value, partner(value, "tp", mask), mask, 2 + k)
    return value.reshape((2, -1) + value.shape[-2:])


def core_finish(ids, kept, arrived, count):
    own, sent = tp_open(ids, kept, arrived)
    for mask in bits_of("tp")[::-1]:
        own, sent = tp_next(ids, own, partner(sent, "tp", mask))
    return core_last(ids, own, swap_core(sent), count)


def along(value, step):
    count = lax.axis_size("ctx") * lax.axis_size("tp")
    pairs = [(i, i + step) for i in range(count) if 0 <= i + step < count]
    return lax.ppermute(value, ("ctx", "tp"), pairs)


def widen_tp(rows):
    return lax.all_gather(rows, "tp", axis=0, tiled=True)


def exchange_tp(partial_value):
    count = lax.axis_size("tp")
    pieces = partial_value.reshape(
        count, partial_value.shape[0] // count, partial_value.shape[1]
    )
    return lax.all_to_all(pieces, "tp", 0, 0)


def widen_core(rows):
    return jnp.concatenate([rows, swap_core(rows)], 0)


def exchange_core(partial_value):
    half = partial_value.shape[0] // 2
    return [partial_value[:half], swap_core(partial_value[half:])]


PARAMS = pltpu.CompilerParams(vmem_limit_bytes=24 << 20)
SMEM = pl.BlockSpec(memory_space=pltpu.SMEM)


def whole(shape):
    return pl.BlockSpec(shape, lambda step: (0,) * len(shape))


def run(kernel, name, outs, *args, smem=0, scratch=()):
    return pl.pallas_call(
        kernel,
        grid=(1,),
        in_specs=[SMEM] * smem + [whole(a.shape) for a in args[smem:]],
        out_specs=[whole(shape) for shape, _ in outs],
        out_shape=[jax.ShapeDtypeStruct(shape, dtype) for shape, dtype in outs],
        scratch_shapes=list(scratch),
        compiler_params=PARAMS,
        name=name,
    )(*args)


def join_kernel(count, *refs):
    for own, far, out_ref in zip(refs[:count], refs[count : 2 * count], refs[2 * count :]):
        half = own.shape[0]
        out_ref[:half] = own[...]
        out_ref[half:] = far[...]


def join_pairs(own, far):
    outs = [((2 * v.shape[0], *v.shape[1:]), v.dtype) for v in own]
    return list(run(functools.partial(join_kernel, len(own)), "join_pairs", outs, *own, *far))


def sum_kernel(count, *refs):
    for own, far, out_ref in zip(refs[:count], refs[count : 2 * count], refs[2 * count :]):
        total = own[...].astype(F32) + far[...].astype(F32)
        out_ref[...] = total.reshape(out_ref.shape).astype(out_ref.dtype)


def sum_pairs(own, far, dtype, shape=None):
    outs = [(shape or v.shape, dtype) for v in own]
    return list(run(functools.partial(sum_kernel, len(own)), "sum_pairs", outs, *own, *far))


def halves_kernel(*refs):
    for k in range(2):
        own, far, kept_ref, sent_ref = refs[k::2]
        total = (own[...].astype(F32) + far[...].astype(F32)).astype(BF16)
        half = total.shape[0] // 2
        kept_ref[...] = total[:half]
        sent_ref[...] = total[half:]


def sum_halves(own, far):
    outs = [((v.shape[0] // 2, *v.shape[1:]), BF16) for v in own] * 2
    return list(run(halves_kernel, "sum_halves", outs, *own, *far))


def tp_open_kernel(ids_ref, *refs):
    own_ref, sent_ref = refs[4:]
    half = own_ref.shape[1]
    upper = lax.rem(ids_ref[3] // half, 2)
    for c in range(2):
        for ref, at in ((own_ref, upper), (sent_ref, 1 - upper)):
            rows = pl.ds(at * half, half)
            total = refs[c][0, rows].astype(F32) + refs[2 + c][0, rows].astype(F32)
            ref[c] = total.astype(BF16)


def tp_open(ids, kept, arrived):
    _, tp, rows, width = kept[0].shape
    outs = [((2, tp // 2, rows, width), BF16)] * 2
    return run(tp_open_kernel, "tp_open", outs, ids, *kept, *arrived, smem=1)


def tp_next_kernel(ids_ref, own_ref, far_ref, kept_ref, sent_ref):
    half = own_ref.shape[1] // 2
    if half:
        upper = lax.rem(ids_ref[3] // half, 2)
        for c in range(2):
            for ref, at in ((kept_ref, upper), (sent_ref, 1 - upper)):
                rows = pl.ds(at * half, half)
                total = own_ref[c, rows].astype(F32) + far_ref[c, rows].astype(F32)
                ref[c] = total.astype(BF16)
    else:
        for ref, at in ((kept_ref, ids_ref[0]), (sent_ref, 1 - ids_ref[0])):
            total = own_ref[at, 0].astype(F32) + far_ref[at, 0].astype(F32)
            ref[...] = total.astype(ref.dtype)


def tp_next(ids, own, far):
    _, tp, rows, width = own.shape
    outs = [((2, tp // 2, rows, width), BF16)] * 2
    if tp == 1:
        outs = [((rows, width), F32), ((rows, width), BF16)]
    return run(tp_next_kernel, "tp_next", outs, ids, own, far, smem=1)


def core_last_kernel(ids_ref, own_ref, far_ref, *outs):
    second = ids_ref[0] == 1
    half = own_ref.shape[1] // len(outs)
    for m, out_ref in enumerate(outs):
        lanes = slice(m * half, (m + 1) * half)
        own, far = own_ref[:, lanes], far_ref[:, lanes].astype(F32)
        out_ref[:, :half] = jnp.where(second, far, own)
        out_ref[:, half:] = jnp.where(second, own, far)


def core_last(ids, own, far, count):
    outs = [((own.shape[0], 2 * own.shape[1] // count), F32)] * count
    return run(core_last_kernel, "core_last", outs, ids, own, far, smem=1)


def stacked(refs):
    local = D // (4 * refs[0].shape[0])
    return jnp.concatenate([r[:, :local].reshape(-1, r.shape[-1]) for r in refs], 0)


def heads_of(refs, start, stop):
    return jnp.concatenate(
        [
            jnp.concatenate(
                [r[:, z, :, start:stop].reshape(-1, stop - start) for r in refs], 0
            )
            for z in range(refs[0].shape[1])
        ],
        1,
    )


def block_order(value, source, target, width):
    where = {place: k for k, place in enumerate(source)}
    return jnp.concatenate(
        [value[:, where[p] * width : (where[p] + 1) * width] for p in target], 1
    )


def by_core(value, kind, second, inverse=False):
    places, width = stream_places(), D // len(stream_places())
    options = []
    for core in range(2):
        other = ffn_places(core, kind)
        options.append(
            block_order(value, other, places, width)
            if inverse
            else block_order(value, places, other, width)
        )
    return jnp.where(second, options[1], options[0])


def grid_places():
    rows, ctxs = lax.axis_size("row"), lax.axis_size("ctx")
    return [(c, b, a) for c in range(2) for b in range(ctxs) for a in range(rows)]


def across(value, ids_ref, source, target):
    grid, rows = grid_places(), lax.axis_size("row")
    width = D // len(grid)
    value = block_order(value, source, grid, width)
    blocks = [value[:, k * width : (k + 1) * width] for k in range(len(grid))]
    flags = [((ids_ref[1] & m) != 0, m) for m in bits_of("row")]
    flags += [((ids_ref[2] & m) != 0, m * rows) for m in bits_of("ctx")]
    for flag, mask in flags:
        blocks = [jnp.where(flag, blocks[i ^ mask], blocks[i]) for i in range(len(blocks))]
    return block_order(jnp.concatenate(blocks, 1), grid, target, width)


def arrive_kernel(ids_ref, inputs_ref, near_ref, wide_ref):
    near = across(inputs_ref[0].astype(F32), ids_ref, natural_places(), stream_places())
    near_ref[...] = near.astype(BF16)
    wide_ref[...] = by_core(near, "in", ids_ref[0] == 1).astype(BF16)


def arrive(ids, inputs):
    shape = inputs.shape[1:]
    return run(arrive_kernel, "arrive", [(shape, BF16), (shape, BF16)], ids, inputs, smem=1)


SMALL = 64


def pack_kernel(count, weight_ref, *refs):
    out_ref, wide = refs[count:]
    local = weight_ref.shape[0]
    out_ref[:local] = weight_ref[...]
    wide[...] = jnp.zeros(wide.shape, F32)
    start = 0
    for ref in refs[:count]:
        rows, width = ref.shape
        wide[start : start + rows, :width] = ref[...].astype(F32)
        start += rows
    for k in range(out_ref.shape[1] // PAIR):
        lanes = slice(k * PAIR, (k + 1) * PAIR)
        out_ref[local:, lanes] = wide[8 * k : 8 * k + 8].astype(BF16)


def pack_below(weight, values):
    shape = (weight.shape[0] + 8, weight.shape[1])
    return run(
        functools.partial(pack_kernel, len(values)), "pack_below", [(shape, BF16)],
        weight, *values,
        scratch=[pltpu.VMEM((SMALL, PAIR), F32)],
    )[0]


def below(ids_ref, chunks, k, c):
    blocks = chunks[0].shape[0]
    own, other = chunks[2 * c + k // blocks], chunks[2 * (1 - c) + k // blocks]
    value = jnp.where(ids_ref[0] == 1, other[k % blocks], own[k % blocks])
    return jnp.concatenate(
        [value[:, m * PAIR : (m + 1) * PAIR] for m in range(SMALL // 8)], 0
    ).astype(F32)


def unpack_kernel(ids_ref, *refs):
    chunks, out_ref = refs[:4], refs[4]
    for k in range(out_ref.shape[0]):
        for c in range(2):
            out_ref[k, c] = below(ids_ref, chunks, k, c).astype(BF16)


def unpack_all_kernel(ids_ref, *refs):
    chunks, selector_ref, norm_refs, first_ref = refs[:4], refs[4], refs[5:10], refs[10]
    rel_ref, conv_ref, table, wide = refs[11:]
    rows, ctxs = lax.axis_size("row"), lax.axis_size("ctx")
    second = ids_ref[0] == 1
    near = [[below(ids_ref, chunks, k, c) for k in range(rows * ctxs)] for c in range(2)]
    for k, (c, b, a) in enumerate(stream_places()):
        value = near[c][b * rows + a]
        lanes = slice(k * PAIR, (k + 1) * PAIR)
        for m in range(5):
            norm_refs[m][0:1, lanes] = value[m : m + 1]
            norm_refs[m][1:2, lanes] = value[5 + m : 6 + m]
    first_ref[...] = by_core(norm_refs[0][...], "in", second)
    flags = [((ids_ref[1] & m) != 0, m) for m in bits_of("row")]
    flags += [((ids_ref[2] & m) != 0, m * rows) for m in bits_of("ctx")]
    for flag, mask in flags:
        near = [
            [jnp.where(flag, blocks[i ^ mask], blocks[i]) for i in range(len(blocks))]
            for blocks in near
        ]
    natural = [near[c][b * rows + a] for c, b, a in natural_places()]
    start, count = 10 + KERNEL + 2, HD // len(natural)
    for k, value in enumerate(natural):
        table[k * count : (k + 1) * count] = value[start : start + count]
    rel = product(table[...].astype(BF16), selector_ref[...]).astype(BF16)
    rel_ref[:HD] = rel
    rel_ref[HD:] = rel
    half = len(natural) // 2
    width = PAIR // half
    for k in range(half):
        wide[...] = jnp.where(second, natural[half + k], natural[k])
        conv_ref[:, k * width : (k + 1) * width] = wide[10:start, :width]


def unpack_specs(chunks, local):
    blocks, _, width = chunks[0].shape
    return [SMEM, *[pl.BlockSpec((blocks, 8, width), lambda step: (0, local // 8, 0))] * 4]


def unpack_all(ids, chunks, selector, local):
    shapes = [((2, D), F32)] * 6 + [((PAIR, PAIR), BF16), ((KERNEL + 2, PAIR), F32)]
    return pl.pallas_call(
        unpack_all_kernel,
        grid=(1,),
        in_specs=[*unpack_specs(chunks, local), whole(selector.shape)],
        out_specs=[whole(s) for s, _ in shapes],
        out_shape=[jax.ShapeDtypeStruct(s, d) for s, d in shapes],
        scratch_shapes=[pltpu.VMEM((HD, PAIR), F32), pltpu.VMEM((SMALL, PAIR), F32)],
        compiler_params=PARAMS,
        name="unpack_all",
    )(ids, *chunks, selector)


def unpack_below(ids, chunks, local):
    shape = (2 * chunks[0].shape[0], 2, SMALL, PAIR)
    return pl.pallas_call(
        unpack_kernel,
        grid=(1,),
        in_specs=unpack_specs(chunks, local),
        out_specs=whole(shape),
        out_shape=jax.ShapeDtypeStruct(shape, BF16),
        compiler_params=PARAMS,
        name="unpack_below",
    )(ids, *chunks)


def share_kernel(count, ids_ref, *refs):
    own_ref, other_ref = refs[-2:]
    second = ids_ref[0] == 1
    at = 0
    for ref in refs[:-2]:
        for m in range(ref.shape[1] // (2 * count)):
            low = ref[:, 2 * m * count : (2 * m + 1) * count]
            high = ref[:, (2 * m + 1) * count : (2 * m + 2) * count]
            own_ref[:, at : at + count] = jnp.where(second, high, low)
            other_ref[:, at : at + count] = jnp.where(second, low, high)
            at += count


def pair_kernel(ids_ref, own_ref, other_ref, out_ref):
    second = ids_ref[0] == 1
    out_ref[0] = jnp.where(second, other_ref[...], own_ref[...])
    out_ref[1] = jnp.where(second, own_ref[...], other_ref[...])


def core_shares(ids, matrices, half):
    rows, width = matrices[0].shape[0], sum(m.shape[1] for m in matrices) // 2
    own, other = run(
        functools.partial(share_kernel, half), "core_shares", [((rows, width), BF16)] * 2,
        ids, *matrices,
        smem=1,
    )
    outs = [((2, rows, width), BF16)]
    return run(pair_kernel, "core_pair", outs, ids, own, swap_core(other), smem=1)[0]


def normal_of(stream):
    centre = stream - jnp.mean(stream, axis=-1, keepdims=True)
    inverse = lax.rsqrt(jnp.mean(centre * centre, axis=-1, keepdims=True) + EPSILON)
    return centre * inverse, inverse


def summed(refs):
    total = None
    for ref in refs:
        value = ref[...].astype(F32)
        value = jnp.sum(value, axis=0) if value.ndim == 3 else value
        total = value if total is None else total + value
    return total


def back_through(upstream, normal, inverse, gain, ids_ref, grads_ref):
    scaled = upstream * gain
    grads = jnp.concatenate(
        [
            jnp.sum(upstream * normal, axis=0, keepdims=True),
            jnp.sum(upstream, axis=0, keepdims=True),
        ],
        0,
    )
    grads_ref[...] = across(grads, ids_ref, stream_places(), natural_places())
    return inverse * (
        scaled
        - jnp.mean(scaled, axis=-1, keepdims=True)
        - normal * jnp.mean(scaled * normal, axis=-1, keepdims=True)
    )


def onward_kernel(count, scale, source, target, core_ref, *refs):
    pieces, stream_ref, norm_ref = refs[:count], refs[count], refs[count + 1]
    next_ref, hidden_ref = refs[count + 2 :]
    second = core_ref[0] == 1
    total = summed(pieces)
    if source:
        total = by_core(total, source, second, inverse=True)
    stream = stream_ref[...] + scale * total
    next_ref[...] = stream
    hidden = normal_of(stream)[0] * norm_ref[0:1] + norm_ref[1:2]
    if target:
        hidden = by_core(hidden, target, second)
    hidden_ref[...] = hidden.astype(BF16)


def onward(core, pieces, stream, norm, scale, source, target):
    return run(
        functools.partial(onward_kernel, len(pieces), scale, source, target),
        "onward",
        [(stream.shape, F32), (stream.shape, BF16)],
        core,
        *pieces,
        stream,
        norm,
        smem=1,
    )


def turn_kernel(count, core_ref, *refs):
    pieces, stream_ref, up_ref, norm_ref = refs[:count], *refs[count : count + 3]
    result_ref, back_ref, branch_ref, grads_ref = refs[count + 3 :]
    second = core_ref[0] == 1
    upstream = across(up_ref[0].astype(F32), core_ref, natural_places(), stream_places())
    total = by_core(summed(pieces), "out", second, inverse=True)
    normal, inverse = normal_of(stream_ref[...] + 0.5 * total)
    result = normal * norm_ref[0:1] + norm_ref[1:2]
    result = across(result, core_ref, stream_places(), natural_places())
    result_ref[0] = result.astype(BF16)
    back = back_through(upstream, normal, inverse, norm_ref[0:1], core_ref, grads_ref)
    back_ref[...] = back
    branch_ref[...] = by_core(0.5 * back, "out", second).astype(BF16)


def turn(core, pieces, stream, upstream, norm):
    shape = stream.shape
    return run(
        functools.partial(turn_kernel, len(pieces)),
        "turn",
        [((1, *shape), BF16), (shape, F32), (shape, BF16), ((2, D), F32)],
        core,
        *pieces,
        stream,
        upstream,
        norm,
        smem=1,
    )


def return_kernel(count, scale, source, target, core_ref, *refs):
    pieces, stream_ref, up_ref, norm_ref = refs[:count], *refs[count : count + 3]
    back_ref, grads_ref = refs[count + 3 : count + 5]
    branch_ref = refs[-1]
    second = core_ref[0] == 1
    total = summed(pieces)
    if source:
        total = by_core(total, source, second, inverse=True)
    normal, inverse = normal_of(stream_ref[...].astype(F32))
    back = up_ref[...] + back_through(total, normal, inverse, norm_ref[0:1], core_ref, grads_ref)
    if scale is None:
        back_ref[0] = across(back, core_ref, stream_places(), natural_places())
        return
    back_ref[...] = back
    branch = scale * back
    if target:
        branch = by_core(branch, target, second)
    branch_ref[...] = branch.astype(BF16)


def returning(core, pieces, stream, upstream, norm, scale, source, target):
    shape = stream.shape
    outs = [(shape, F32), ((2, D), F32), (shape, BF16)]
    if scale is None:
        outs = [((1, *shape), F32), ((2, D), F32)]
    return run(
        functools.partial(return_kernel, len(pieces), scale, source, target),
        "returning",
        outs,
        core,
        *pieces,
        stream,
        upstream,
        norm,
        smem=1,
    )


def first_kernel(wide_ref, norm_ref, *refs):
    hidden_ref = refs[8]
    hidden = normal_of(wide_ref[...].astype(F32))[0] * norm_ref[0:1] + norm_ref[1:2]
    hidden_ref[...] = hidden.astype(BF16)
    ffn_forward_kernel(hidden_ref, *refs[:8], *refs[9:])


def ffn_forward_kernel(rows_ref, *refs):
    ins, outs = refs[:4], refs[4:8]
    before_ref, active_ref, branch_ref = refs[8:]
    before = product(rows_ref[...], stacked(ins))
    before_ref[...] = before.astype(BF16)
    active = (before * jax.nn.sigmoid(before)).astype(BF16)
    active_ref[...] = active
    branch_ref[...] = product_nt(active, stacked(outs)).astype(BF16)


def ffn_outs(height, width):
    return [((height, width), BF16), ((height, width), BF16), ((height, D), BF16)]


def ffn_first(wide, norm, ins, outs):
    height, width = wide.shape[0], ins[0].shape[-1]
    return run(
        first_kernel, "ffn_first", [((height, D), BF16), *ffn_outs(height, width)],
        wide, norm, *ins, *outs,
    )


def ffn_forward(hidden, ins, outs):
    height, width = hidden.shape[0], ins[0].shape[-1]
    return run(
        ffn_forward_kernel, "ffn_forward", ffn_outs(height, width), hidden, *ins, *outs
    )


def ffn_backward_kernel(rows_ref, before_ref, *refs):
    ins, outs = refs[:4], refs[4:8]
    d_before_ref, branch_ref = refs[8:]
    d_active = product(rows_ref[...], stacked(outs))
    d_before = (d_active * silu_slope(before_ref[...].astype(F32))).astype(BF16)
    d_before_ref[...] = d_before
    branch_ref[...] = product_nt(d_before, stacked(ins)).astype(BF16)


def ffn_backward(upstream, before, ins, outs):
    height, width = before.shape
    return run(
        ffn_backward_kernel, "ffn_backward", [((height, width), BF16), ((height, D), BF16)],
        upstream, before, *ins, *outs,
    )


def scatter_rows(value, refs):
    rows = value.shape[0] // len(refs)
    for j, ref in enumerate(refs):
        ref[...] = value[j * rows : (j + 1) * rows].reshape(ref.shape)


def ffn_grads_kernel(hidden_ref, d_before_ref, up_ref, active_ref, *outs):
    scatter_rows(product_tn(hidden_ref[...], d_before_ref[...]).astype(BF16), outs[:4])
    scatter_rows(product_tn(up_ref[...], active_ref[...]).astype(BF16), outs[4:])


def ffn_grads(hidden, d_before, upstream, active, like):
    grads = run(
        ffn_grads_kernel, "ffn_grads", [(like.shape, BF16)] * 8,
        hidden, d_before, upstream, active,
    )
    return grads[:4], grads[4:]


def project_kernel(rows_ref, *refs):
    chunks, outs = refs[:4], refs[4:]
    value = product(rows_ref[...], heads_of(chunks, 0, 3 * PAIR)).astype(BF16)
    for z in range(chunks[0].shape[1]):
        for m in range(3):
            outs[m][:, z * PAIR : (z + 1) * PAIR] = value[
                :, (3 * z + m) * PAIR : (3 * z + m + 1) * PAIR
            ]


def project_heads(hidden, chunks):
    shape = (hidden.shape[0], chunks[0].shape[1] * PAIR)
    return run(project_kernel, "project_heads", [(shape, BF16)] * 3, hidden, *chunks)


def core_grads_kernel(count, hidden_ref, up_ref, *refs):
    values, last_ref, outs = refs[:count], refs[count], refs[count + 1 :]
    tp = outs[0].shape[1]
    grads = [product_tn(hidden_ref[...], v[...]).astype(BF16) for v in values]
    grads.append(product_tn(up_ref[...], last_ref[...]).astype(BF16))
    for m, grad in enumerate(grads):
        rows = D // len(outs)
        for j, ref in enumerate(outs):
            for z in range(tp):
                piece = grad[j * rows : (j + 1) * rows, z * PAIR : (z + 1) * PAIR]
                ref[:, z, :, m * PAIR : (m + 1) * PAIR] = piece.reshape(
                    ref.shape[0], ref.shape[2], PAIR
                )


def core_grads(hidden, upstream, values, last, like):
    return run(
        functools.partial(core_grads_kernel, len(values)), "core_grads",
        [(like.shape, BF16)] * 4, hidden, upstream, *values, last,
    )


def interleaved(values):
    tp = values[0].shape[1] // PAIR
    return jnp.concatenate(
        [v[:, z * PAIR : (z + 1) * PAIR] for z in range(tp) for v in values], 1
    )


def window(first, length, height):
    rows = lax.broadcasted_iota(jnp.int32, (height, KEYS), 0)
    lanes = lax.broadcasted_iota(jnp.int32, (height, KEYS), 1)
    offset = lanes - rows
    frame = lanes + (first - LEFT)
    in_band = (offset >= 0) & (offset < SPAN)
    allowed = in_band & (frame >= 0) & (frame < length)
    return in_band, allowed


def both(mask):
    return jnp.concatenate([mask, mask], 0)


def window_of(left_ref, own_ref, right_ref, clip, z, side, height):
    channels = own_ref.shape[1]
    lanes = slice(z * PAIR, (z + 1) * PAIR)
    far = slice(side * channels + z * PAIR, side * channels + (z + 1) * PAIR)
    return jnp.concatenate(
        [
            left_ref[clip, :, far],
            own_ref[clip * height : (clip + 1) * height, lanes],
            right_ref[clip, :, far],
            jnp.zeros((KEYS - LEFT - RIGHT - height, PAIR), BF16),
        ],
        0,
    )


def split_heads(value, odd):
    zero = jnp.zeros_like(value)
    return jnp.concatenate([jnp.where(odd, zero, value), jnp.where(odd, value, zero)], 0)


def merge_heads(value, odd):
    height = value.shape[0] // 2
    return jnp.where(odd, value[height:], value[:height])


def attend_kernel(
    height, first_ref, lens_ref, q_ref, k_ref, v_ref, left_ref, right_ref, rel_ref,
    c0, c1, c2, c3, context_ref, chance_ref, branch_ref
):
    odd = lax.broadcasted_iota(jnp.int32, (1, PAIR), 1) >= HD
    for clip in range(2):
        rows = slice(clip * height, (clip + 1) * height)
        in_band, allowed = window(first_ref[0], lens_ref[clip], height)
        in_band, allowed = both(in_band), both(allowed)
        for z in range(c0.shape[1]):
            lanes = slice(z * PAIR, (z + 1) * PAIR)
            query = split_heads(q_ref[rows, lanes], odd)
            keys = window_of(left_ref, k_ref, right_ref, clip, z, 0, height)
            values = window_of(left_ref, v_ref, right_ref, clip, z, 1, height)
            relative = product(query, rel_ref[...])
            relative = jnp.concatenate([relative, jnp.zeros((2 * height, KEYS - PAIR), F32)], 1)
            relative = jnp.concatenate(
                [
                    pltpu.roll(relative[:height], 0, 1, stride=1, stride_axis=0),
                    pltpu.roll(relative[height:], 0, 1, stride=1, stride_axis=0),
                ],
                0,
            )
            score = (product_nt(query, keys) + relative) * SCALE
            masked = jnp.where(allowed, score, MASKED)
            ceiling = jnp.max(masked, axis=-1, keepdims=True)
            raised = jnp.where(in_band, jnp.exp(masked - ceiling), 0.0)
            chance = raised * (1.0 / jnp.sum(raised, axis=-1, keepdims=True))
            chance_ref[clip, z] = chance
            context = merge_heads(product(chance.astype(BF16), values), odd)
            context_ref[rows, lanes] = context.astype(BF16)
    weight = heads_of((c0, c1, c2, c3), 3 * PAIR, 4 * PAIR)
    branch_ref[...] = product_nt(context_ref[...], weight).astype(BF16)


def attend(first, lens, heads, left, right, rel, chunks):
    height, channels, tp = heads[0].shape[0] // 2, heads[0].shape[1], chunks[0].shape[1]
    return run(
        functools.partial(attend_kernel, height),
        "attend",
        [
            ((2 * height, channels), BF16),
            ((2, tp, 2 * height, KEYS), F32),
            ((2 * height, D), BF16),
        ],
        first, lens, *heads, left, right, rel, *chunks,
        smem=2,
    )


def attend_back_kernel(
    height, first_ref, lens_ref, up_ref, q_ref, k_ref, v_ref, left_ref, right_ref, rel_ref,
    c0, c1, c2, c3, chance_ref, dq_ref, own_ref, d_left_ref, d_right_ref, table_ref
):
    odd = lax.broadcasted_iota(jnp.int32, (1, PAIR), 1) >= HD
    weight = heads_of((c0, c1, c2, c3), 3 * PAIR, 4 * PAIR)
    d_context = product(up_ref[...], weight).astype(BF16)
    table = jnp.zeros((PAIR, PAIR), F32)
    flip = (
        lax.broadcasted_iota(jnp.int32, (height, height), 0)
        + lax.broadcasted_iota(jnp.int32, (height, height), 1)
        == height - 1
    ).astype(BF16)
    for clip in range(2):
        rows = slice(clip * height, (clip + 1) * height)
        allowed = both(window(first_ref[0], lens_ref[clip], height)[1])
        for z in range(c0.shape[1]):
            lanes = slice(z * PAIR, (z + 1) * PAIR)
            query = split_heads(q_ref[rows, lanes], odd)
            upstream = split_heads(d_context[rows, lanes], odd)
            keys = window_of(left_ref, k_ref, right_ref, clip, z, 0, height)
            values = window_of(left_ref, v_ref, right_ref, clip, z, 1, height)
            chance = chance_ref[clip, z]
            d_chance = product_nt(upstream, values)
            inner = jnp.sum(d_chance * chance, axis=-1, keepdims=True)
            d_score = jnp.where(allowed, chance * (d_chance - inner), 0.0).astype(BF16)
            d_values = product_tn(chance.astype(BF16), upstream)
            d_keys = product_tn(d_score, query) * SCALE
            relative = []
            for head in range(2):
                turned_rows = product(flip, d_score[head * height : (head + 1) * height])
                rolled = pltpu.roll(
                    turned_rows, KEYS - height + 1, 1, stride=1, stride_axis=0
                )[:, :PAIR].astype(BF16)
                relative.append(product(flip, rolled).astype(BF16))
            relative = jnp.concatenate(relative, 0)
            d_query = product(d_score, keys) + product_nt(relative, rel_ref[...])
            dq_ref[rows, lanes] = (merge_heads(d_query, odd) * SCALE).astype(BF16)
            table += product_tn(query, relative)
            for slot, value in ((0, d_keys), (1, d_values)):
                d_left_ref[slot, clip, :, lanes] = value[:LEFT].astype(BF16)
                own_ref[slot, rows, lanes] = value[LEFT : LEFT + height]
                d_right_ref[slot, clip, :, lanes] = value[
                    LEFT + height : LEFT + height + RIGHT
                ].astype(BF16)
    table_ref[...] = table * SCALE


def attend_back(first, lens, upstream, heads, left, right, rel, chunks, chance):
    height, channels = heads[0].shape[0] // 2, heads[0].shape[1]
    return run(
        functools.partial(attend_back_kernel, height),
        "attend_back",
        [
            ((2 * height, channels), BF16),
            ((2, 2 * height, channels), F32),
            ((2, 2, LEFT, channels), BF16),
            ((2, 2, RIGHT, channels), BF16),
            ((PAIR, PAIR), F32),
        ],
        first, lens, upstream, *heads, left, right, rel, *chunks, chance,
        smem=2,
    )


def heads_in_kernel(height, dq_ref, own_ref, left_ref, right_ref, *refs):
    chunks, dk_ref, dv_ref, branch_ref = refs[:4], *refs[4:]
    for slot, out_ref in ((0, dk_ref), (1, dv_ref)):
        for clip in range(2):
            start = clip * height
            own = own_ref[slot, start : start + height]
            top = own[:RIGHT] + right_ref[slot, clip].astype(F32)
            own = jnp.concatenate([top, own[RIGHT:]], 0)
            low = own[height - LEFT :] + left_ref[slot, clip].astype(F32)
            own = jnp.concatenate([own[: height - LEFT], low], 0)
            out_ref[start : start + height] = own.astype(BF16)
    value = interleaved([dq_ref[...], dk_ref[...], dv_ref[...]])
    branch_ref[...] = product_nt(value, heads_of(chunks, 0, 3 * PAIR)).astype(BF16)


def heads_in(d_query, own, from_next, from_last, chunks):
    shape = d_query.shape
    return run(
        functools.partial(heads_in_kernel, shape[0] // 2), "heads_in",
        [(shape, BF16), (shape, BF16), ((shape[0], D), BF16)],
        d_query, own, from_next, from_last, *chunks,
    )


REACH = 32


def gate_kernel(rows_ref, live_ref, *refs):
    chunks, value_ref, logistic_ref, gated_ref = refs[:4], *refs[4:]
    value = product(rows_ref[...], heads_of(chunks, 0, 2 * PAIR))
    for z in range(chunks[0].shape[1]):
        lanes = slice(z * PAIR, (z + 1) * PAIR)
        linear = value[:, 2 * z * PAIR : (2 * z + 1) * PAIR]
        logistic = jax.nn.sigmoid(value[:, (2 * z + 1) * PAIR : (2 * z + 2) * PAIR])
        value_ref[:, lanes] = linear
        logistic_ref[:, lanes] = logistic
        gated_ref[:, lanes] = (linear * logistic * live_ref[...]).astype(BF16)


def gate_channels(hidden, live, chunks):
    shape = (hidden.shape[0], chunks[0].shape[1] * PAIR)
    return run(
        gate_kernel, "gate_channels", [(shape, F32), (shape, F32), (shape, BF16)],
        hidden, live, *chunks,
    )


def extend(earlier_ref, own_ref, wide, height):
    for clip in range(2):
        wide[clip, :REACH] = earlier_ref[clip].astype(F32)
        wide[clip, REACH : REACH + height] = own_ref[
            clip * height : (clip + 1) * height
        ].astype(F32)


def mix_kernel(height, gated_ref, earlier_ref, taps_ref, mixed_ref, sums_ref, wide):
    extend(earlier_ref, gated_ref, wide, height)
    lead = REACH - (KERNEL - 1)
    for clip in range(2):
        rows = slice(clip * height, (clip + 1) * height)
        first = second = jnp.zeros((height, 1), F32)
        for z in range(gated_ref.shape[1] // PAIR):
            lanes = slice(z * PAIR, (z + 1) * PAIR)
            mixed = wide[clip, lead : lead + height, lanes] * taps_ref[0:1, lanes]
            for j in range(1, KERNEL):
                mixed += wide[clip, lead + j : lead + j + height, lanes] * taps_ref[j : j + 1, lanes]
            mixed_ref[rows, lanes] = mixed
            first += jnp.sum(mixed, axis=1, keepdims=True)
            second += jnp.sum(mixed * mixed, axis=1, keepdims=True)
        sums_ref[rows] = jnp.concatenate([first, second], 1)


def mix_channels(gated, earlier, taps):
    height, channels = gated.shape[0] // 2, gated.shape[1]
    return run(
        functools.partial(mix_kernel, height), "mix_channels",
        [((2 * height, channels), F32), ((2 * height, 2), F32)],
        gated, earlier, taps,
        scratch=[pltpu.VMEM((2, height + REACH, channels), F32)],
    )


def paired(own_ref, other_ref):
    half = own_ref.shape[0] // 2
    other = other_ref[...]
    return (own_ref[...] + jnp.concatenate([other[half:], other[:half]], 0)) * (1.0 / D)


def conv_norm(mixed_ref, sums_ref, other_ref):
    means = paired(sums_ref, other_ref)
    centre, square = means[:, 0:1], means[:, 1:2]
    inverse = lax.rsqrt(square - centre * centre + EPSILON)
    return (mixed_ref[...] - centre) * inverse, inverse


def conv_out_kernel(mixed_ref, sums_ref, other_ref, affine_ref, *refs):
    chunks, active_ref, branch_ref = refs[:4], *refs[4:]
    normal, _ = conv_norm(mixed_ref, sums_ref, other_ref)
    levels = normal * affine_ref[0:1] + affine_ref[1:2]
    active = (levels * jax.nn.sigmoid(levels)).astype(BF16)
    active_ref[...] = active
    weight = heads_of(chunks, 2 * PAIR, 3 * PAIR)
    branch_ref[...] = product_nt(active, weight).astype(BF16)


def conv_forward(mixed, sums, other, affine, chunks):
    return run(
        conv_out_kernel, "conv_forward", [(mixed.shape, BF16), ((mixed.shape[0], D), BF16)],
        mixed, sums, other, affine, *chunks,
    )


def conv_level_kernel(up_ref, mixed_ref, sums_ref, other_ref, affine_ref, *refs):
    chunks, scaled_ref, totals_ref, affine_grad_ref = refs[:4], *refs[4:]
    normal, _ = conv_norm(mixed_ref, sums_ref, other_ref)
    levels = normal * affine_ref[0:1] + affine_ref[1:2]
    weight = heads_of(chunks, 2 * PAIR, 3 * PAIR)
    d_levels = product(up_ref[...], weight) * silu_slope(levels)
    scaled = d_levels * affine_ref[0:1]
    scaled_ref[...] = scaled
    totals_ref[...] = jnp.concatenate(
        [
            jnp.sum(scaled, axis=1, keepdims=True),
            jnp.sum(scaled * normal, axis=1, keepdims=True),
        ],
        1,
    )
    affine_grad_ref[0:1] = jnp.sum(d_levels * normal, axis=0, keepdims=True)
    affine_grad_ref[1:2] = jnp.sum(d_levels, axis=0, keepdims=True)


def conv_levels_back(upstream, mixed, sums, other, affine, chunks):
    return run(
        conv_level_kernel, "conv_levels_back",
        [(mixed.shape, F32), (sums.shape, F32), ((2, mixed.shape[1]), F32)],
        upstream, mixed, sums, other, affine, *chunks,
    )


def unmix_kernel(
    height, scaled_ref, totals_ref, far_totals_ref, mixed_ref, sums_ref, other_ref, taps_ref,
    d_mixed_ref, own_ref, earlier_ref, wide
):
    normal, inverse = conv_norm(mixed_ref, sums_ref, other_ref)
    means = paired(totals_ref, far_totals_ref)
    d_mixed = inverse * (scaled_ref[...] - means[:, 0:1] - normal * means[:, 1:2])
    d_mixed_ref[...] = d_mixed
    for clip in range(2):
        rows = slice(clip * height, (clip + 1) * height)
        wide[clip, :REACH] = jnp.zeros((REACH, d_mixed.shape[1]), F32)
        wide[clip, REACH : REACH + height] = d_mixed[rows]
        wide[clip, REACH + height :] = jnp.zeros((REACH, d_mixed.shape[1]), F32)
        last = REACH + KERNEL - 1
        for z in range(d_mixed.shape[1] // PAIR):
            lanes = slice(z * PAIR, (z + 1) * PAIR)
            own = wide[clip, last : last + height, lanes] * taps_ref[0:1, lanes]
            for j in range(1, KERNEL):
                own += wide[clip, last - j : last - j + height, lanes] * taps_ref[j : j + 1, lanes]
            own_ref[rows, lanes] = own
            early = wide[clip, KERNEL - 1 : KERNEL - 1 + REACH, lanes] * taps_ref[0:1, lanes]
            for j in range(1, KERNEL):
                start = KERNEL - 1 - j
                early += wide[clip, start : start + REACH, lanes] * taps_ref[j : j + 1, lanes]
            earlier_ref[clip, :, lanes] = early


def unmix_channels(scaled, totals, far_totals, mixed, sums, other, taps):
    height, channels = mixed.shape[0] // 2, mixed.shape[1]
    return run(
        functools.partial(unmix_kernel, height), "unmix_channels",
        [(mixed.shape, F32), (mixed.shape, F32), ((2, REACH, channels), F32)],
        scaled, totals, far_totals, mixed, sums, other, taps,
        scratch=[pltpu.VMEM((2, height + 2 * REACH, channels), F32)],
    )


def gate_back_kernel(height, own_ref, later_ref, value_ref, logistic_ref, live_ref, *refs):
    chunks, d_value_ref, d_gate_ref, branch_ref = refs[:4], *refs[4:]
    for clip in range(2):
        rows = slice(clip * height, (clip + 1) * height)
        own = own_ref[rows]
        low = own[height - REACH :] + later_ref[clip]
        own = jnp.concatenate([own[: height - REACH], low], 0) * live_ref[rows]
        logistic = logistic_ref[rows]
        d_value_ref[rows] = (own * logistic).astype(BF16)
        d_gate_ref[rows] = (own * value_ref[rows] * logistic * (1.0 - logistic)).astype(BF16)
    value = interleaved([d_value_ref[...], d_gate_ref[...]])
    branch_ref[...] = product_nt(value, heads_of(chunks, 0, 2 * PAIR)).astype(BF16)


def gate_back(own, later, value_half, logistic, live, chunks):
    shape = own.shape
    return run(
        functools.partial(gate_back_kernel, shape[0] // 2), "gate_back",
        [(shape, BF16), (shape, BF16), ((shape[0], D), BF16)],
        own, later, value_half, logistic, live, *chunks,
    )


def tap_kernel(height, d_mixed_ref, gated_ref, earlier_ref, taps_ref, wide):
    extend(earlier_ref, gated_ref, wide, height)
    lead = REACH - (KERNEL - 1)
    for z in range(gated_ref.shape[1] // PAIR):
        lanes = slice(z * PAIR, (z + 1) * PAIR)
        for j in range(KERNEL):
            total = jnp.zeros((1, PAIR), F32)
            for clip in range(2):
                total += jnp.sum(
                    d_mixed_ref[clip * height : (clip + 1) * height, lanes]
                    * wide[clip, lead + j : lead + j + height, lanes],
                    axis=0,
                    keepdims=True,
                )
            taps_ref[j : j + 1, lanes] = total


def tap_grads_of(d_mixed, gated, earlier):
    height, channels = gated.shape[0] // 2, gated.shape[1]
    return run(
        functools.partial(tap_kernel, height), "tap_grads", [((KERNEL, channels), F32)],
        d_mixed, gated, earlier,
        scratch=[pltpu.VMEM((2, height + REACH, channels), F32)],
    )[0]


def body(
    inputs,
    cotangent,
    lengths,
    buckets,
    ffn1_in,
    ffn1_out,
    norm_gains,
    norm_biases,
    qkv_weight,
    attn_out,
    distance,
    glu_in,
    depthwise,
    conv_gain,
    conv_bias,
    conv_out,
    ffn2_in,
    ffn2_out,
):
    rows, ctxs, tp = lax.axis_size("row"), lax.axis_size("ctx"), lax.axis_size("tp")
    second = lax.axis_index("core") == 1
    core = jnp.stack([lax.axis_index(axis) for axis in ("core", "row", "ctx", "tp")])
    core = core.astype(jnp.int32)
    local = ffn1_in.shape[0]
    height = inputs.shape[1]
    first = (lax.axis_index("ctx") * tp + lax.axis_index("tp")) * height
    attn_shares = core_shares(
        core, [qkv_weight.reshape(local, -1), attn_out], attn_out.shape[1] // 2
    )
    near, rows_in = arrive(core, inputs)
    small = [norm_gains.T, norm_biases.T, depthwise.T, conv_gain[None], conv_bias[None], distance]
    joined = gather_first([pack_below(ffn1_in, small), ffn1_out])
    attn_half = tp_first(attn_shares)
    joined, attn_half, wide_inputs = tied(joined, attn_half, widen_tp(rows_in))
    halves = gather_last(joined)
    attn_rows = tp_rest(attn_half)
    conv_shares = core_shares(core, [glu_in.reshape(local, -1), conv_out], conv_out.shape[1] // 2)
    attn_rows, halves = tied(attn_rows, halves)
    one_in, one_out = ffn_weights(halves)
    w_attn = gather_last(gather_first(attn_rows))

    lens = widen_core(lengths)
    frame_ids = first + jnp.arange(height, dtype=jnp.int32)
    live = (frame_ids[None, :] < lens[:, None]).astype(F32).reshape(2 * height, 1)

    table_rows, width = distance.shape[0], conv_gain.shape[0]
    selector = (jnp.arange(SPAN, dtype=jnp.int32)[:, None] == buckets[None, :]).astype(BF16)
    selector_pad = jnp.pad(selector, ((0, PAIR - SPAN), (0, PAIR - SPAN)))
    width, table_rows = conv_gain.shape[0], distance.shape[0]
    half = conv_out.shape[1] // 2
    if local % PAIR == 0:
        *norm, first_norm, rel, conv_small = unpack_all(core, one_in, selector_pad, local)
    else:
        cube = unpack_below(core, one_in, local)
        take = lambda c, k: cube[k, c]
        norms = jnp.concatenate(
            [take(c, b * rows + a)[:10, :local] for c, b, a in stream_places()], 1
        ).astype(F32)
        norm = [jnp.stack([norms[k], norms[5 + k]], 0) for k in range(5)]
        blocks = [
            crossed([take(c, k)[10:] for k in range(rows * ctxs)]) for c in range(2)
        ]
        natural = [blocks[c][b * rows + a] for c, b, a in natural_places()]
        table_all = jnp.concatenate(
            [n[KERNEL + 2 : KERNEL + 2 + table_rows, :SPAN] for n in natural], 0
        )
        conv_small = jnp.concatenate([n[: KERNEL + 2, :width] for n in natural], 1)
        half = conv_small.shape[1] // 2
        conv_small = jnp.where(second, conv_small[:, half:], conv_small[:, :half])
        first_norm = to_ffn(norm[0], "in", second)
        rel = product(table_all, selector).astype(BF16)
        rel = jnp.pad(jnp.concatenate([rel, rel], 0), ((0, 0), (0, PAIR - SPAN)))
    for mask in bits_of("tp"):
        conv_small = tp_joined(conv_small, partner(conv_small, "tp", mask), mask, 1)
    conv_small = conv_small.astype(F32)
    taps, affine = conv_small[:KERNEL], conv_small[KERNEL:]


    hidden0, before0, active0, branch = ffn_first(
        wide_inputs, first_norm, one_in, one_out
    )
    branch, conv_shares = tied(branch, conv_shares)
    conv_half = tp_first(conv_shares)
    conv_rows, w_attn = tied(tp_rest(conv_half), w_attn)
    w_conv = gather_last(gather_first(conv_rows))
    two_rows, w_conv = tied([ffn2_in, ffn2_out], w_conv)
    two_in, two_out = ffn_weights(gather_last(gather_first(two_rows)))
    stream1, hidden1 = onward(
        core, [exchange_tp(branch)], near.astype(F32), norm[1], 0.5, "out", None
    )

    hidden1 = widen_core(hidden1)
    heads = project_heads(hidden1, w_attn)
    channels = heads[0].shape[1]
    key_value = [h.reshape(2, height, channels) for h in heads[1:]]
    left = along(jnp.concatenate([h[:, height - LEFT :] for h in key_value], 2), 1)
    right = along(jnp.concatenate([h[:, :RIGHT] for h in key_value], 2), -1)
    first_ref = first.reshape(1).astype(jnp.int32)
    context, chance, branch = attend(first_ref, lens, heads, left, right, rel, w_attn)
    stream2, hidden2 = onward(core, exchange_core(branch), stream1, norm[2], 1.0, None, None)

    hidden2 = widen_core(hidden2)
    value_half, logistic, gated = gate_channels(hidden2, live, w_conv)
    earlier = along(gated.reshape(2, height, channels)[:, height - REACH :], 1)
    mixed, sums = mix_channels(gated, earlier, taps)
    other = swap_core(sums)
    active_conv, branch = conv_forward(mixed, sums, other, affine, w_conv)
    stream3, hidden3 = onward(core, exchange_core(branch), stream2, norm[3], 1.0, None, "in")

    hidden3 = widen_tp(hidden3)
    before3, active3, branch = ffn_forward(hidden3, two_in, two_out)
    result, d_stream, d_branch, grads4 = turn(
        core, [exchange_tp(branch)], stream3, cotangent, norm[4]
    )

    d_branch = widen_tp(d_branch)
    d_before, branch = ffn_backward(d_branch, before3, two_in, two_out)
    two_own, two_far = settle_open(
        ffn_halves(*ffn_grads(hidden3, d_before, d_branch, active3, two_in[0]))
    )
    d_stream, grads3, d_branch = returning(
        core, [exchange_tp(branch)], stream3, d_stream, norm[3], 1.0, "in", None
    )

    d_branch = widen_core(d_branch)
    scaled, totals, affine_grads = conv_levels_back(d_branch, mixed, sums, other, affine, w_conv)
    d_mixed, d_own, d_earlier = unmix_channels(
        scaled, totals, swap_core(totals), mixed, sums, other, taps
    )
    two_own, two_far = settle_close(two_own, two_far)
    later = along(d_earlier, -1)
    d_value, d_gate, branch = gate_back(d_own, later, value_half, logistic, live, w_conv)
    conv_grads = core_grads(hidden2, d_branch, (d_value, d_gate), active_conv, w_conv[0])
    conv_own, conv_far = settle_open(conv_grads)
    d_stream, grads2, d_branch = returning(
        core, exchange_core(branch), stream2, d_stream, norm[2], 1.0, None, None
    )

    d_branch = widen_core(d_branch)
    grad_two_in, grad_two_out = sum_pairs(two_own, two_far, F32, ffn2_in.shape)
    d_query, d_own, d_left, d_right, d_table = attend_back(
        first_ref, lens, d_branch, heads, left, right, rel, w_attn, chance
    )
    from_next = along(d_left, -1)
    d_key, d_val, branch = heads_in(d_query, d_own, from_next, along(d_right, 1), w_attn)
    conv_own, conv_far = settle_close(conv_own, conv_far)
    attn_grads = core_grads(hidden1, d_branch, (d_query, d_key, d_val), context, w_attn[0])
    d_stream, grads1, d_branch = returning(
        core, exchange_core(branch), stream1, d_stream, norm[1], 0.5, None, "out"
    )
    d_branch, attn_grads = tied(d_branch, attn_grads)
    attn_own, attn_far = settle_open(attn_grads)

    d_branch, attn_far = tied(widen_tp(d_branch), attn_far)
    grad_value, grad_gate, grad_w_conv = core_finish(core, conv_own, conv_far, 3)
    d_before, branch = ffn_backward(d_branch, before0, one_in, one_out)
    one_grads = ffn_grads(hidden0, d_before, d_branch, active0, one_out[0])
    one_grads, attn_far = tied(one_grads, attn_far)
    attn_own, attn_far = settle_close(attn_own, attn_far)
    one_own, one_far = settle_open(ffn_halves(*one_grads))
    pieces = exchange_tp(branch)
    grad_q, grad_k, grad_v, grad_w_attn = core_finish(core, attn_own, attn_far, 4)
    input_grad, grads0 = returning(
        core, [pieces], near, d_stream, norm[0], None, "in", None
    )
    one_own, one_far = settle_close(one_own, one_far)
    grad_one_in, grad_one_out = sum_pairs(one_own, one_far, F32, ffn1_in.shape)

    d_rel = (d_table[:HD] + d_table[HD:])[:, :SPAN]
    grad_table = jnp.dot(d_rel, selector.astype(F32).T, precision=lax.Precision.HIGHEST)
    grad_table = jnp.pad(grad_table, ((0, 0), (0, PAIR - SPAN)))
    wide = tp * half
    fold_rows = lambda v: jnp.concatenate(
        [v[:, k : k + wide] for k in range(0, v.shape[1], wide)], 0
    )
    tap_grads = tap_grads_of(d_mixed, gated, earlier)
    packed = jnp.concatenate(
        [
            tap_grads,
            affine_grads,
            grad_table.reshape(-1, wide),
            *[fold_rows(g) for g in (grads4, grads3, grads2, grads1, grads0)],
        ],
        0,
    )
    for axis, mask in [*stages_of(A_AXES), *stages_of(("tp",))]:
        packed = packed + partner(packed, axis, mask)
    far_packed = swap_core(packed)
    total = (packed + far_packed)[KERNEL + 2 :]
    table_size = grad_table.size // wide
    grad_table = total[:table_size].reshape(HD, PAIR)[:, :SPAN]
    norm_grads = total[table_size:].reshape(5, D // wide, 2, wide)
    norm_grads = norm_grads.transpose(0, 2, 1, 3).reshape(10, D)[::-1]
    conv_cut = jnp.concatenate(
        [
            jnp.where(second, far_packed, packed)[: KERNEL + 2].reshape(-1, tp, half),
            jnp.where(second, packed, far_packed)[: KERNEL + 2].reshape(-1, tp, half),
        ],
        2,
    )
    place = (lax.axis_index("row") * 2 + lax.axis_index("core")) * ctxs + lax.axis_index("ctx")
    conv_cut = lax.dynamic_index_in_dim(conv_cut, lax.axis_index("tp"), 1, keepdims=False)
    conv_cut = lax.dynamic_slice_in_dim(conv_cut, place * width, width, 1)
    grad_table = lax.dynamic_slice_in_dim(grad_table, place * table_rows, table_rows, 0)
    norm_grads = lax.dynamic_slice_in_dim(norm_grads, place * local, local, 1)

    return (
        result,
        input_grad,
        grad_one_in,
        grad_one_out,
        norm_grads[1::2].T,
        norm_grads[::2].T,
        jnp.stack([grad_q, grad_k, grad_v], 1),
        grad_w_attn,
        grad_table,
        jnp.stack([grad_value, grad_gate], 1),
        conv_cut[:KERNEL].T,
        conv_cut[KERNEL],
        conv_cut[KERNEL + 1],
        grad_w_conv,
        grad_two_in,
        grad_two_out,
    )


def solution(mesh):
    shards, ctxs, tp = (mesh.shape[axis] for axis in ("shard", "ctx", "tp"))
    cut = Mesh(mesh.devices.reshape(shards // 2, 2, ctxs, tp), ("row", "core", "ctx", "tp"))
    shard = ("row", "core")
    block = ("row", "core", "ctx")
    every = ("tp", "row", "core", "ctx")
    weight = P(block, "tp")
    narrow = P(block, None)
    deep = P(block, None, "tp")
    frames = P(shard, ("ctx", "tp"), None)
    return jax.shard_map(
        body,
        mesh=cut,
        in_specs=(
            frames, frames, P(shard), P(), weight, weight, narrow, narrow, deep, weight, narrow,
            deep, P(every, None), P(every), P(every), weight, weight, weight,
        ),
        out_specs=(
            frames, frames, weight, weight, narrow, narrow, deep, weight, narrow, deep,
            P(every, None), P(every), P(every), weight, weight, weight,
        ),
        check_vma=False,
    )
```

```python
import functools

import jax
import jax.numpy as jnp
from jax import lax
from jax.experimental import pallas as pl
from jax.experimental.pallas import tpu as pltpu
from jax.sharding import Mesh
from jax.sharding import PartitionSpec as P

D = 1024
HD = 64
KERNEL = 31
LEFT = 64
RIGHT = 16
SPAN = 73
PAIR = 128
KEYS = 256
EPSILON = 1e-05
MASKED = -1e30
SCALE = HD**-0.5
F32 = jnp.float32
BF16 = jnp.bfloat16


def product(left, right):
    return jnp.dot(left, right, preferred_element_type=F32)


def product_nt(left, right):
    return lax.dot_general(left, right, (((1,), (1,)), ((), ())), preferred_element_type=F32)


def product_tn(left, right):
    return lax.dot_general(left, right, (((0,), (0,)), ((), ())), preferred_element_type=F32)


def silu_slope(values):
    logistic = jax.nn.sigmoid(values)
    return logistic * (1.0 + values * (1.0 - logistic))


def bits_of(axis):
    count = lax.axis_size(axis)
    return [1 << k for k in range(count.bit_length() - 1)]


def stream_places():
    rows, ctxs = lax.axis_size("row"), lax.axis_size("ctx")
    return [(0, b, a) for b in range(ctxs) for a in range(rows)] + [
        (1, b, a) for a in range(rows) for b in range(ctxs)
    ]


def ffn_places(core, kind):
    rows, ctxs = lax.axis_size("row"), lax.axis_size("ctx")
    if kind == "in":
        return [(e ^ core, b, a) for e in range(2) for b in range(ctxs) for a in range(rows)]
    return [(e ^ core, b, a) for e in range(2) for a in range(rows) for b in range(ctxs)]


def reorder(value, source, target):
    width = value.shape[-1] // len(source)
    where = {place: k for k, place in enumerate(source)}
    return jnp.concatenate(
        [value[..., where[p] * width : (where[p] + 1) * width] for p in target], -1
    )


def to_ffn(value, kind, second):
    source = stream_places()
    return jnp.where(
        second,
        reorder(value, source, ffn_places(1, kind)),
        reorder(value, source, ffn_places(0, kind)),
    )


def from_ffn(value, kind, second):
    target = stream_places()
    return jnp.where(
        second,
        reorder(value, ffn_places(1, kind), target),
        reorder(value, ffn_places(0, kind), target),
    )


def crossed(blocks):
    rows = lax.axis_size("row")
    flags = [((lax.axis_index("row") & m) != 0, m) for m in bits_of("row")]
    flags += [((lax.axis_index("ctx") & m) != 0, m * rows) for m in bits_of("ctx")]
    for flag, mask in flags:
        blocks = [jnp.where(flag, blocks[i ^ mask], blocks[i]) for i in range(len(blocks))]
    return blocks


def natural_places():
    rows, ctxs = lax.axis_size("row"), lax.axis_size("ctx")
    return [(c, b, a) for a in range(rows) for c in range(2) for b in range(ctxs)]


def tied(*groups):
    return lax.optimization_barrier(groups)


def partner(value, axis, mask):
    count = lax.axis_size(axis)
    return lax.ppermute(value, axis, [(i, i ^ mask) for i in range(count)])


def swap_core(value):
    return partner(value, "core", 1)


def stages_of(axes):
    return [(axis, mask) for axis in axes for mask in bits_of(axis)]


A_AXES = ("row", "ctx")
B_AXES = ("ctx", "row")


def gather_first(weights):
    values = [w[None] for w in weights]
    rounds = [stages_of(axes)[:-1] for axes in (A_AXES, B_AXES)]
    for k in range(len(rounds[0])):
        values = join_pairs(values, [partner(v, *stages[k]) for v, stages in zip(values, rounds)])
    return values


def gather_last(values):
    far = [
        partner(values[0], *stages_of(A_AXES)[-1]),
        partner(values[1], *stages_of(B_AXES)[-1]),
    ]
    return [values[0], far[0], values[1], far[1]]


def ffn_weights(halves):
    other = [swap_core(h) for h in halves]
    return [*halves[:2], *other[:2]], [*halves[2:], *other[2:]]


def settle_open(chunks):
    near_a, far_a, near_b, far_b = chunks
    arrived = [
        partner(far_a, *stages_of(A_AXES)[-1]),
        partner(far_b, *stages_of(B_AXES)[-1]),
    ]
    return [near_a, near_b], arrived


def settle_close(own, far):
    halves = sum_halves(own, far)
    rounds = [stages_of(axes)[:-1][::-1] for axes in (A_AXES, B_AXES)]
    for k in range(len(rounds[0])):
        kept, sent = halves[:2], halves[2:]
        arrived = [partner(s, *stages[k]) for s, stages in zip(sent, rounds)]
        if k < len(rounds[0]) - 1:
            halves = sum_halves(kept, arrived)
    return kept, arrived


def ffn_halves(grads_in, grads_out):
    own = [*grads_in[:2], *grads_out[:2]]
    far = [swap_core(g) for g in (*grads_in[2:], *grads_out[2:])]
    return sum_pairs(own, far, BF16)


def tp_joined(own, arrived, mask, axis):
    upper = (lax.axis_index("tp") & mask) != 0
    return jnp.concatenate(
        [jnp.where(upper, arrived, own), jnp.where(upper, own, arrived)], axis
    )


def tp_first(value):
    steps = lax.axis_size("tp").bit_length() - 1
    value = value.reshape((2,) + (1,) * steps + value.shape[1:])
    mask = bits_of("tp")[-1]
    return tp_joined(value, partner(value, "tp", mask), mask, 1)


def tp_rest(value):
    for k, mask in enumerate(bits_of("tp")[:-1][::-1]):
        value = tp_joined(value, partner(value, "tp", mask), mask, 2 + k)
    return value.reshape((2, -1) + value.shape[-2:])


def core_finish(ids, kept, arrived, count):
    own, sent = tp_open(ids, kept, arrived)
    for mask in bits_of("tp")[::-1]:
        own, sent = tp_next(ids, own, partner(sent, "tp", mask))
    return core_last(ids, own, swap_core(sent), count)


def along(value, step):
    count = lax.axis_size("ctx") * lax.axis_size("tp")
    pairs = [(i, i + step) for i in range(count) if 0 <= i + step < count]
    return lax.ppermute(value, ("ctx", "tp"), pairs)


def widen_tp(rows):
    return lax.all_gather(rows, "tp", axis=0, tiled=True)


def exchange_tp(partial_value):
    count = lax.axis_size("tp")
    pieces = partial_value.reshape(
        count, partial_value.shape[0] // count, partial_value.shape[1]
    )
    return lax.all_to_all(pieces, "tp", 0, 0)


def widen_core(rows):
    return jnp.concatenate([rows, swap_core(rows)], 0)


def exchange_core(partial_value):
    half = partial_value.shape[0] // 2
    return [partial_value[:half], swap_core(partial_value[half:])]


PARAMS = pltpu.CompilerParams(vmem_limit_bytes=24 << 20)
SMEM = pl.BlockSpec(memory_space=pltpu.SMEM)


def whole(shape):
    return pl.BlockSpec(shape, lambda step: (0,) * len(shape))


def run(kernel, name, outs, *args, smem=0, scratch=()):
    return pl.pallas_call(
        kernel,
        grid=(1,),
        in_specs=[SMEM] * smem + [whole(a.shape) for a in args[smem:]],
        out_specs=[whole(shape) for shape, _ in outs],
        out_shape=[jax.ShapeDtypeStruct(shape, dtype) for shape, dtype in outs],
        scratch_shapes=list(scratch),
        compiler_params=PARAMS,
        name=name,
    )(*args)


def join_kernel(count, *refs):
    for own, far, out_ref in zip(refs[:count], refs[count : 2 * count], refs[2 * count :]):
        half = own.shape[0]
        out_ref[:half] = own[...]
        out_ref[half:] = far[...]


def join_pairs(own, far):
    outs = [((2 * v.shape[0], *v.shape[1:]), v.dtype) for v in own]
    return list(run(functools.partial(join_kernel, len(own)), "join_pairs", outs, *own, *far))


def sum_kernel(count, *refs):
    for own, far, out_ref in zip(refs[:count], refs[count : 2 * count], refs[2 * count :]):
        total = own[...].astype(F32) + far[...].astype(F32)
        out_ref[...] = total.reshape(out_ref.shape).astype(out_ref.dtype)


def sum_pairs(own, far, dtype, shape=None):
    outs = [(shape or v.shape, dtype) for v in own]
    return list(run(functools.partial(sum_kernel, len(own)), "sum_pairs", outs, *own, *far))


def halves_kernel(*refs):
    for k in range(2):
        own, far, kept_ref, sent_ref = refs[k::2]
        total = (own[...].astype(F32) + far[...].astype(F32)).astype(BF16)
        half = total.shape[0] // 2
        kept_ref[...] = total[:half]
        sent_ref[...] = total[half:]


def sum_halves(own, far):
    outs = [((v.shape[0] // 2, *v.shape[1:]), BF16) for v in own] * 2
    return list(run(halves_kernel, "sum_halves", outs, *own, *far))


def tp_open_kernel(ids_ref, *refs):
    own_ref, sent_ref = refs[4:]
    half = own_ref.shape[1]
    upper = lax.rem(ids_ref[3] // half, 2)
    for c in range(2):
        for ref, at in ((own_ref, upper), (sent_ref, 1 - upper)):
            rows = pl.ds(at * half, half)
            total = refs[c][0, rows].astype(F32) + refs[2 + c][0, rows].astype(F32)
            ref[c] = total.astype(BF16)


def tp_open(ids, kept, arrived):
    _, tp, rows, width = kept[0].shape
    outs = [((2, tp // 2, rows, width), BF16)] * 2
    return run(tp_open_kernel, "tp_open", outs, ids, *kept, *arrived, smem=1)


def tp_next_kernel(ids_ref, own_ref, far_ref, kept_ref, sent_ref):
    half = own_ref.shape[1] // 2
    if half:
        upper = lax.rem(ids_ref[3] // half, 2)
        for c in range(2):
            for ref, at in ((kept_ref, upper), (sent_ref, 1 - upper)):
                rows = pl.ds(at * half, half)
                total = own_ref[c, rows].astype(F32) + far_ref[c, rows].astype(F32)
                ref[c] = total.astype(BF16)
    else:
        for ref, at in ((kept_ref, ids_ref[0]), (sent_ref, 1 - ids_ref[0])):
            total = own_ref[at, 0].astype(F32) + far_ref[at, 0].astype(F32)
            ref[...] = total.astype(ref.dtype)


def tp_next(ids, own, far):
    _, tp, rows, width = own.shape
    outs = [((2, tp // 2, rows, width), BF16)] * 2
    if tp == 1:
        outs = [((rows, width), F32), ((rows, width), BF16)]
    return run(tp_next_kernel, "tp_next", outs, ids, own, far, smem=1)


def core_last_kernel(ids_ref, own_ref, far_ref, *outs):
    second = ids_ref[0] == 1
    half = own_ref.shape[1] // len(outs)
    for m, out_ref in enumerate(outs):
        lanes = slice(m * half, (m + 1) * half)
        own, far = own_ref[:, lanes], far_ref[:, lanes].astype(F32)
        out_ref[:, :half] = jnp.where(second, far, own)
        out_ref[:, half:] = jnp.where(second, own, far)


def core_last(ids, own, far, count):
    outs = [((own.shape[0], 2 * own.shape[1] // count), F32)] * count
    return run(core_last_kernel, "core_last", outs, ids, own, far, smem=1)


def stacked(refs):
    local = D // (4 * refs[0].shape[0])
    return jnp.concatenate([r[:, :local].reshape(-1, r.shape[-1]) for r in refs], 0)


def heads_of(refs, start, stop):
    return jnp.concatenate(
        [
            jnp.concatenate(
                [r[:, z, :, start:stop].reshape(-1, stop - start) for r in refs], 0
            )
            for z in range(refs[0].shape[1])
        ],
        1,
    )


def block_order(value, source, target, width):
    where = {place: k for k, place in enumerate(source)}
    return jnp.concatenate(
        [value[:, where[p] * width : (where[p] + 1) * width] for p in target], 1
    )


def by_core(value, kind, second, inverse=False):
    places, width = stream_places(), D // len(stream_places())
    options = []
    for core in range(2):
        other = ffn_places(core, kind)
        options.append(
            block_order(value, other, places, width)
            if inverse
            else block_order(value, places, other, width)
        )
    return jnp.where(second, options[1], options[0])


def grid_places():
    rows, ctxs = lax.axis_size("row"), lax.axis_size("ctx")
    return [(c, b, a) for c in range(2) for b in range(ctxs) for a in range(rows)]


def across(value, ids_ref, source, target):
    grid, rows = grid_places(), lax.axis_size("row")
    width = D // len(grid)
    value = block_order(value, source, grid, width)
    blocks = [value[:, k * width : (k + 1) * width] for k in range(len(grid))]
    flags = [((ids_ref[1] & m) != 0, m) for m in bits_of("row")]
    flags += [((ids_ref[2] & m) != 0, m * rows) for m in bits_of("ctx")]
    for flag, mask in flags:
        blocks = [jnp.where(flag, blocks[i ^ mask], blocks[i]) for i in range(len(blocks))]
    return block_order(jnp.concatenate(blocks, 1), grid, target, width)


def arrive_kernel(ids_ref, inputs_ref, near_ref, wide_ref):
    near = across(inputs_ref[0].astype(F32), ids_ref, natural_places(), stream_places())
    near_ref[...] = near.astype(BF16)
    wide_ref[...] = by_core(near, "in", ids_ref[0] == 1).astype(BF16)


def arrive(ids, inputs):
    shape = inputs.shape[1:]
    return run(arrive_kernel, "arrive", [(shape, BF16), (shape, BF16)], ids, inputs, smem=1)


SMALL = 64


def pack_kernel(count, weight_ref, *refs):
    out_ref, wide = refs[count:]
    local = weight_ref.shape[0]
    out_ref[:local] = weight_ref[...]
    wide[...] = jnp.zeros(wide.shape, F32)
    start = 0
    for ref in refs[:count]:
        rows, width = ref.shape
        wide[start : start + rows, :width] = ref[...].astype(F32)
        start += rows
    for k in range(out_ref.shape[1] // PAIR):
        lanes = slice(k * PAIR, (k + 1) * PAIR)
        out_ref[local:, lanes] = wide[8 * k : 8 * k + 8].astype(BF16)


def pack_below(weight, values):
    shape = (weight.shape[0] + 8, weight.shape[1])
    return run(
        functools.partial(pack_kernel, len(values)), "pack_below", [(shape, BF16)],
        weight, *values,
        scratch=[pltpu.VMEM((SMALL, PAIR), F32)],
    )[0]


def below(ids_ref, chunks, k, c):
    blocks = chunks[0].shape[0]
    own, other = chunks[2 * c + k // blocks], chunks[2 * (1 - c) + k // blocks]
    value = jnp.where(ids_ref[0] == 1, other[k % blocks], own[k % blocks])
    return jnp.concatenate(
        [value[:, m * PAIR : (m + 1) * PAIR] for m in range(SMALL // 8)], 0
    ).astype(F32)


def unpack_kernel(ids_ref, *refs):
    chunks, out_ref = refs[:4], refs[4]
    for k in range(out_ref.shape[0]):
        for c in range(2):
            out_ref[k, c] = below(ids_ref, chunks, k, c).astype(BF16)


def unpack_all_kernel(ids_ref, *refs):
    chunks, selector_ref, norm_refs, first_ref = refs[:4], refs[4], refs[5:10], refs[10]
    rel_ref, conv_ref, table, wide = refs[11:]
    rows, ctxs = lax.axis_size("row"), lax.axis_size("ctx")
    second = ids_ref[0] == 1
    near = [[below(ids_ref, chunks, k, c) for k in range(rows * ctxs)] for c in range(2)]
    for k, (c, b, a) in enumerate(stream_places()):
        value = near[c][b * rows + a]
        lanes = slice(k * PAIR, (k + 1) * PAIR)
        for m in range(5):
            norm_refs[m][0:1, lanes] = value[m : m + 1]
            norm_refs[m][1:2, lanes] = value[5 + m : 6 + m]
    first_ref[...] = by_core(norm_refs[0][...], "in", second)
    flags = [((ids_ref[1] & m) != 0, m) for m in bits_of("row")]
    flags += [((ids_ref[2] & m) != 0, m * rows) for m in bits_of("ctx")]
    for flag, mask in flags:
        near = [
            [jnp.where(flag, blocks[i ^ mask], blocks[i]) for i in range(len(blocks))]
            for blocks in near
        ]
    natural = [near[c][b * rows + a] for c, b, a in natural_places()]
    start, count = 10 + KERNEL + 2, HD // len(natural)
    for k, value in enumerate(natural):
        table[k * count : (k + 1) * count] = value[start : start + count]
    rel = product(table[...].astype(BF16), selector_ref[...]).astype(BF16)
    rel_ref[:HD] = rel
    rel_ref[HD:] = rel
    half = len(natural) // 2
    width = PAIR // half
    for k in range(half):
        wide[...] = jnp.where(second, natural[half + k], natural[k])
        conv_ref[:, k * width : (k + 1) * width] = wide[10:start, :width]


def unpack_specs(chunks, local):
    blocks, _, width = chunks[0].shape
    return [SMEM, *[pl.BlockSpec((blocks, 8, width), lambda step: (0, local // 8, 0))] * 4]


def unpack_all(ids, chunks, selector, local):
    shapes = [((2, D), F32)] * 6 + [((PAIR, PAIR), BF16), ((KERNEL + 2, PAIR), F32)]
    return pl.pallas_call(
        unpack_all_kernel,
        grid=(1,),
        in_specs=[*unpack_specs(chunks, local), whole(selector.shape)],
        out_specs=[whole(s) for s, _ in shapes],
        out_shape=[jax.ShapeDtypeStruct(s, d) for s, d in shapes],
        scratch_shapes=[pltpu.VMEM((HD, PAIR), F32), pltpu.VMEM((SMALL, PAIR), F32)],
        compiler_params=PARAMS,
        name="unpack_all",
    )(ids, *chunks, selector)


def unpack_below(ids, chunks, local):
    shape = (2 * chunks[0].shape[0], 2, SMALL, PAIR)
    return pl.pallas_call(
        unpack_kernel,
        grid=(1,),
        in_specs=unpack_specs(chunks, local),
        out_specs=whole(shape),
        out_shape=jax.ShapeDtypeStruct(shape, BF16),
        compiler_params=PARAMS,
        name="unpack_below",
    )(ids, *chunks)


def share_kernel(count, ids_ref, *refs):
    own_ref, other_ref = refs[-2:]
    second = ids_ref[0] == 1
    at = 0
    for ref in refs[:-2]:
        for m in range(ref.shape[1] // (2 * count)):
            low = ref[:, 2 * m * count : (2 * m + 1) * count]
            high = ref[:, (2 * m + 1) * count : (2 * m + 2) * count]
            own_ref[:, at : at + count] = jnp.where(second, high, low)
            other_ref[:, at : at + count] = jnp.where(second, low, high)
            at += count


def pair_kernel(ids_ref, own_ref, other_ref, out_ref):
    second = ids_ref[0] == 1
    out_ref[0] = jnp.where(second, other_ref[...], own_ref[...])
    out_ref[1] = jnp.where(second, own_ref[...], other_ref[...])


def core_shares(ids, matrices, half):
    rows, width = matrices[0].shape[0], sum(m.shape[1] for m in matrices) // 2
    own, other = run(
        functools.partial(share_kernel, half), "core_shares", [((rows, width), BF16)] * 2,
        ids, *matrices,
        smem=1,
    )
    outs = [((2, rows, width), BF16)]
    return run(pair_kernel, "core_pair", outs, ids, own, swap_core(other), smem=1)[0]


def normal_of(stream):
    centre = stream - jnp.mean(stream, axis=-1, keepdims=True)
    inverse = lax.rsqrt(jnp.mean(centre * centre, axis=-1, keepdims=True) + EPSILON)
    return centre * inverse, inverse


def summed(refs):
    total = None
    for ref in refs:
        value = ref[...].astype(F32)
        value = jnp.sum(value, axis=0) if value.ndim == 3 else value
        total = value if total is None else total + value
    return total


def back_through(upstream, normal, inverse, gain, ids_ref, grads_ref):
    scaled = upstream * gain
    grads = jnp.concatenate(
        [
            jnp.sum(upstream * normal, axis=0, keepdims=True),
            jnp.sum(upstream, axis=0, keepdims=True),
        ],
        0,
    )
    grads_ref[...] = across(grads, ids_ref, stream_places(), natural_places())
    return inverse * (
        scaled
        - jnp.mean(scaled, axis=-1, keepdims=True)
        - normal * jnp.mean(scaled * normal, axis=-1, keepdims=True)
    )


def onward_kernel(count, scale, source, target, core_ref, *refs):
    pieces, stream_ref, norm_ref = refs[:count], refs[count], refs[count + 1]
    next_ref, hidden_ref = refs[count + 2 :]
    second = core_ref[0] == 1
    total = summed(pieces)
    if source:
        total = by_core(total, source, second, inverse=True)
    stream = stream_ref[...] + scale * total
    next_ref[...] = stream
    hidden = normal_of(stream)[0] * norm_ref[0:1] + norm_ref[1:2]
    if target:
        hidden = by_core(hidden, target, second)
    hidden_ref[...] = hidden.astype(BF16)


def onward(core, pieces, stream, norm, scale, source, target):
    return run(
        functools.partial(onward_kernel, len(pieces), scale, source, target),
        "onward",
        [(stream.shape, F32), (stream.shape, BF16)],
        core,
        *pieces,
        stream,
        norm,
        smem=1,
    )


def turn_kernel(count, core_ref, *refs):
    pieces, stream_ref, up_ref, norm_ref = refs[:count], *refs[count : count + 3]
    result_ref, back_ref, branch_ref, grads_ref = refs[count + 3 :]
    second = core_ref[0] == 1
    upstream = across(up_ref[0].astype(F32), core_ref, natural_places(), stream_places())
    total = by_core(summed(pieces), "out", second, inverse=True)
    normal, inverse = normal_of(stream_ref[...] + 0.5 * total)
    result = normal * norm_ref[0:1] + norm_ref[1:2]
    result = across(result, core_ref, stream_places(), natural_places())
    result_ref[0] = result.astype(BF16)
    back = back_through(upstream, normal, inverse, norm_ref[0:1], core_ref, grads_ref)
    back_ref[...] = back
    branch_ref[...] = by_core(0.5 * back, "out", second).astype(BF16)


def turn(core, pieces, stream, upstream, norm):
    shape = stream.shape
    return run(
        functools.partial(turn_kernel, len(pieces)),
        "turn",
        [((1, *shape), BF16), (shape, F32), (shape, BF16), ((2, D), F32)],
        core,
        *pieces,
        stream,
        upstream,
        norm,
        smem=1,
    )


def return_kernel(count, scale, source, target, core_ref, *refs):
    pieces, stream_ref, up_ref, norm_ref = refs[:count], *refs[count : count + 3]
    back_ref, grads_ref = refs[count + 3 : count + 5]
    branch_ref = refs[-1]
    second = core_ref[0] == 1
    total = summed(pieces)
    if source:
        total = by_core(total, source, second, inverse=True)
    normal, inverse = normal_of(stream_ref[...].astype(F32))
    back = up_ref[...] + back_through(total, normal, inverse, norm_ref[0:1], core_ref, grads_ref)
    if scale is None:
        back_ref[0] = across(back, core_ref, stream_places(), natural_places())
        return
    back_ref[...] = back
    branch = scale * back
    if target:
        branch = by_core(branch, target, second)
    branch_ref[...] = branch.astype(BF16)


def returning(core, pieces, stream, upstream, norm, scale, source, target):
    shape = stream.shape
    outs = [(shape, F32), ((2, D), F32), (shape, BF16)]
    if scale is None:
        outs = [((1, *shape), F32), ((2, D), F32)]
    return run(
        functools.partial(return_kernel, len(pieces), scale, source, target),
        "returning",
        outs,
        core,
        *pieces,
        stream,
        upstream,
        norm,
        smem=1,
    )


def first_kernel(wide_ref, norm_ref, *refs):
    hidden_ref = refs[8]
    hidden = normal_of(wide_ref[...].astype(F32))[0] * norm_ref[0:1] + norm_ref[1:2]
    hidden_ref[...] = hidden.astype(BF16)
    ffn_forward_kernel(hidden_ref, *refs[:8], *refs[9:])


def ffn_forward_kernel(rows_ref, *refs):
    ins, outs = refs[:4], refs[4:8]
    before_ref, active_ref, branch_ref = refs[8:]
    before = product(rows_ref[...], stacked(ins))
    before_ref[...] = before.astype(BF16)
    active = (before * jax.nn.sigmoid(before)).astype(BF16)
    active_ref[...] = active
    branch_ref[...] = product_nt(active, stacked(outs)).astype(BF16)


def ffn_outs(height, width):
    return [((height, width), BF16), ((height, width), BF16), ((height, D), BF16)]


def ffn_first(wide, norm, ins, outs):
    height, width = wide.shape[0], ins[0].shape[-1]
    return run(
        first_kernel, "ffn_first", [((height, D), BF16), *ffn_outs(height, width)],
        wide, norm, *ins, *outs,
    )


def ffn_forward(hidden, ins, outs):
    height, width = hidden.shape[0], ins[0].shape[-1]
    return run(
        ffn_forward_kernel, "ffn_forward", ffn_outs(height, width), hidden, *ins, *outs
    )


def ffn_backward_kernel(rows_ref, before_ref, *refs):
    ins, outs = refs[:4], refs[4:8]
    d_before_ref, branch_ref = refs[8:]
    d_active = product(rows_ref[...], stacked(outs))
    d_before = (d_active * silu_slope(before_ref[...].astype(F32))).astype(BF16)
    d_before_ref[...] = d_before
    branch_ref[...] = product_nt(d_before, stacked(ins)).astype(BF16)


def ffn_backward(upstream, before, ins, outs):
    height, width = before.shape
    return run(
        ffn_backward_kernel, "ffn_backward", [((height, width), BF16), ((height, D), BF16)],
        upstream, before, *ins, *outs,
    )


def scatter_rows(value, refs):
    rows = value.shape[0] // len(refs)
    for j, ref in enumerate(refs):
        ref[...] = value[j * rows : (j + 1) * rows].reshape(ref.shape)


def ffn_grads_kernel(hidden_ref, d_before_ref, up_ref, active_ref, *outs):
    scatter_rows(product_tn(hidden_ref[...], d_before_ref[...]).astype(BF16), outs[:4])
    scatter_rows(product_tn(up_ref[...], active_ref[...]).astype(BF16), outs[4:])


def ffn_grads(hidden, d_before, upstream, active, like):
    grads = run(
        ffn_grads_kernel, "ffn_grads", [(like.shape, BF16)] * 8,
        hidden, d_before, upstream, active,
    )
    return grads[:4], grads[4:]


def project_kernel(rows_ref, *refs):
    chunks, outs = refs[:4], refs[4:]
    value = product(rows_ref[...], heads_of(chunks, 0, 3 * PAIR)).astype(BF16)
    for z in range(chunks[0].shape[1]):
        for m in range(3):
            outs[m][:, z * PAIR : (z + 1) * PAIR] = value[
                :, (3 * z + m) * PAIR : (3 * z + m + 1) * PAIR
            ]


def project_heads(hidden, chunks):
    shape = (hidden.shape[0], chunks[0].shape[1] * PAIR)
    return run(project_kernel, "project_heads", [(shape, BF16)] * 3, hidden, *chunks)


def core_grads_kernel(count, hidden_ref, up_ref, *refs):
    values, last_ref, outs = refs[:count], refs[count], refs[count + 1 :]
    tp = outs[0].shape[1]
    grads = [product_tn(hidden_ref[...], v[...]).astype(BF16) for v in values]
    grads.append(product_tn(up_ref[...], last_ref[...]).astype(BF16))
    for m, grad in enumerate(grads):
        rows = D // len(outs)
        for j, ref in enumerate(outs):
            for z in range(tp):
                piece = grad[j * rows : (j + 1) * rows, z * PAIR : (z + 1) * PAIR]
                ref[:, z, :, m * PAIR : (m + 1) * PAIR] = piece.reshape(
                    ref.shape[0], ref.shape[2], PAIR
                )


def core_grads(hidden, upstream, values, last, like):
    return run(
        functools.partial(core_grads_kernel, len(values)), "core_grads",
        [(like.shape, BF16)] * 4, hidden, upstream, *values, last,
    )


def interleaved(values):
    tp = values[0].shape[1] // PAIR
    return jnp.concatenate(
        [v[:, z * PAIR : (z + 1) * PAIR] for z in range(tp) for v in values], 1
    )


def window(first, length, height):
    rows = lax.broadcasted_iota(jnp.int32, (height, KEYS), 0)
    lanes = lax.broadcasted_iota(jnp.int32, (height, KEYS), 1)
    offset = lanes - rows
    frame = lanes + (first - LEFT)
    in_band = (offset >= 0) & (offset < SPAN)
    allowed = in_band & (frame >= 0) & (frame < length)
    return in_band, allowed


def both(mask):
    return jnp.concatenate([mask, mask], 0)


def window_of(left_ref, own_ref, right_ref, clip, z, side, height):
    channels = own_ref.shape[1]
    lanes = slice(z * PAIR, (z + 1) * PAIR)
    far = slice(side * channels + z * PAIR, side * channels + (z + 1) * PAIR)
    return jnp.concatenate(
        [
            left_ref[clip, :, far],
            own_ref[clip * height : (clip + 1) * height, lanes],
            right_ref[clip, :, far],
            jnp.zeros((KEYS - LEFT - RIGHT - height, PAIR), BF16),
        ],
        0,
    )


def split_heads(value, odd):
    zero = jnp.zeros_like(value)
    return jnp.concatenate([jnp.where(odd, zero, value), jnp.where(odd, value, zero)], 0)


def merge_heads(value, odd):
    height = value.shape[0] // 2
    return jnp.where(odd, value[height:], value[:height])


def attend_kernel(
    height, first_ref, lens_ref, q_ref, k_ref, v_ref, left_ref, right_ref, rel_ref,
    c0, c1, c2, c3, context_ref, chance_ref, branch_ref
):
    odd = lax.broadcasted_iota(jnp.int32, (1, PAIR), 1) >= HD
    for clip in range(2):
        rows = slice(clip * height, (clip + 1) * height)
        in_band, allowed = window(first_ref[0], lens_ref[clip], height)
        in_band, allowed = both(in_band), both(allowed)
        for z in range(c0.shape[1]):
            lanes = slice(z * PAIR, (z + 1) * PAIR)
            query = split_heads(q_ref[rows, lanes], odd)
            keys = window_of(left_ref, k_ref, right_ref, clip, z, 0, height)
            values = window_of(left_ref, v_ref, right_ref, clip, z, 1, height)
            relative = product(query, rel_ref[...])
            relative = jnp.concatenate([relative, jnp.zeros((2 * height, KEYS - PAIR), F32)], 1)
            relative = jnp.concatenate(
                [
                    pltpu.roll(relative[:height], 0, 1, stride=1, stride_axis=0),
                    pltpu.roll(relative[height:], 0, 1, stride=1, stride_axis=0),
                ],
                0,
            )
            score = (product_nt(query, keys) + relative) * SCALE
            masked = jnp.where(allowed, score, MASKED)
            ceiling = jnp.max(masked, axis=-1, keepdims=True)
            raised = jnp.where(in_band, jnp.exp(masked - ceiling), 0.0)
            chance = raised * (1.0 / jnp.sum(raised, axis=-1, keepdims=True))
            chance_ref[clip, z] = chance
            context = merge_heads(product(chance.astype(BF16), values), odd)
            context_ref[rows, lanes] = context.astype(BF16)
    weight = heads_of((c0, c1, c2, c3), 3 * PAIR, 4 * PAIR)
    branch_ref[...] = product_nt(context_ref[...], weight).astype(BF16)


def attend(first, lens, heads, left, right, rel, chunks):
    height, channels, tp = heads[0].shape[0] // 2, heads[0].shape[1], chunks[0].shape[1]
    return run(
        functools.partial(attend_kernel, height),
        "attend",
        [
            ((2 * height, channels), BF16),
            ((2, tp, 2 * height, KEYS), F32),
            ((2 * height, D), BF16),
        ],
        first, lens, *heads, left, right, rel, *chunks,
        smem=2,
    )


def attend_back_kernel(
    height, first_ref, lens_ref, up_ref, q_ref, k_ref, v_ref, left_ref, right_ref, rel_ref,
    c0, c1, c2, c3, chance_ref, dq_ref, own_ref, d_left_ref, d_right_ref, table_ref
):
    odd = lax.broadcasted_iota(jnp.int32, (1, PAIR), 1) >= HD
    weight = heads_of((c0, c1, c2, c3), 3 * PAIR, 4 * PAIR)
    d_context = product(up_ref[...], weight).astype(BF16)
    table = jnp.zeros((PAIR, PAIR), F32)
    flip = (
        lax.broadcasted_iota(jnp.int32, (height, height), 0)
        + lax.broadcasted_iota(jnp.int32, (height, height), 1)
        == height - 1
    ).astype(BF16)
    for clip in range(2):
        rows = slice(clip * height, (clip + 1) * height)
        allowed = both(window(first_ref[0], lens_ref[clip], height)[1])
        for z in range(c0.shape[1]):
            lanes = slice(z * PAIR, (z + 1) * PAIR)
            query = split_heads(q_ref[rows, lanes], odd)
            upstream = split_heads(d_context[rows, lanes], odd)
            keys = window_of(left_ref, k_ref, right_ref, clip, z, 0, height)
            values = window_of(left_ref, v_ref, right_ref, clip, z, 1, height)
            chance = chance_ref[clip, z]
            d_chance = product_nt(upstream, values)
            inner = jnp.sum(d_chance * chance, axis=-1, keepdims=True)
            d_score = jnp.where(allowed, chance * (d_chance - inner), 0.0).astype(BF16)
            d_values = product_tn(chance.astype(BF16), upstream)
            d_keys = product_tn(d_score, query) * SCALE
            relative = []
            for head in range(2):
                turned_rows = product(flip, d_score[head * height : (head + 1) * height])
                rolled = pltpu.roll(
                    turned_rows, KEYS - height + 1, 1, stride=1, stride_axis=0
                )[:, :PAIR].astype(BF16)
                relative.append(product(flip, rolled).astype(BF16))
            relative = jnp.concatenate(relative, 0)
            d_query = product(d_score, keys) + product_nt(relative, rel_ref[...])
            dq_ref[rows, lanes] = (merge_heads(d_query, odd) * SCALE).astype(BF16)
            table += product_tn(query, relative)
            for slot, value in ((0, d_keys), (1, d_values)):
                d_left_ref[slot, clip, :, lanes] = value[:LEFT].astype(BF16)
                own_ref[slot, rows, lanes] = value[LEFT : LEFT + height]
                d_right_ref[slot, clip, :, lanes] = value[
                    LEFT + height : LEFT + height + RIGHT
                ].astype(BF16)
    table_ref[...] = table * SCALE


def attend_back(first, lens, upstream, heads, left, right, rel, chunks, chance):
    height, channels = heads[0].shape[0] // 2, heads[0].shape[1]
    return run(
        functools.partial(attend_back_kernel, height),
        "attend_back",
        [
            ((2 * height, channels), BF16),
            ((2, 2 * height, channels), F32),
            ((2, 2, LEFT, channels), BF16),
            ((2, 2, RIGHT, channels), BF16),
            ((PAIR, PAIR), F32),
        ],
        first, lens, upstream, *heads, left, right, rel, *chunks, chance,
        smem=2,
    )


def heads_in_kernel(height, dq_ref, own_ref, left_ref, right_ref, *refs):
    chunks, dk_ref, dv_ref, branch_ref = refs[:4], *refs[4:]
    for slot, out_ref in ((0, dk_ref), (1, dv_ref)):
        for clip in range(2):
            start = clip * height
            own = own_ref[slot, start : start + height]
            top = own[:RIGHT] + right_ref[slot, clip].astype(F32)
            own = jnp.concatenate([top, own[RIGHT:]], 0)
            low = own[height - LEFT :] + left_ref[slot, clip].astype(F32)
            own = jnp.concatenate([own[: height - LEFT], low], 0)
            out_ref[start : start + height] = own.astype(BF16)
    value = interleaved([dq_ref[...], dk_ref[...], dv_ref[...]])
    branch_ref[...] = product_nt(value, heads_of(chunks, 0, 3 * PAIR)).astype(BF16)


def heads_in(d_query, own, from_next, from_last, chunks):
    shape = d_query.shape
    return run(
        functools.partial(heads_in_kernel, shape[0] // 2), "heads_in",
        [(shape, BF16), (shape, BF16), ((shape[0], D), BF16)],
        d_query, own, from_next, from_last, *chunks,
    )


REACH = 32


def gate_kernel(rows_ref, live_ref, *refs):
    chunks, value_ref, logistic_ref, gated_ref = refs[:4], *refs[4:]
    value = product(rows_ref[...], heads_of(chunks, 0, 2 * PAIR))
    for z in range(chunks[0].shape[1]):
        lanes = slice(z * PAIR, (z + 1) * PAIR)
        linear = value[:, 2 * z * PAIR : (2 * z + 1) * PAIR]
        logistic = jax.nn.sigmoid(value[:, (2 * z + 1) * PAIR : (2 * z + 2) * PAIR])
        value_ref[:, lanes] = linear
        logistic_ref[:, lanes] = logistic
        gated_ref[:, lanes] = (linear * logistic * live_ref[...]).astype(BF16)


def gate_channels(hidden, live, chunks):
    shape = (hidden.shape[0], chunks[0].shape[1] * PAIR)
    return run(
        gate_kernel, "gate_channels", [(shape, F32), (shape, F32), (shape, BF16)],
        hidden, live, *chunks,
    )


def extend(earlier_ref, own_ref, wide, height):
    for clip in range(2):
        wide[clip, :REACH] = earlier_ref[clip].astype(F32)
        wide[clip, REACH : REACH + height] = own_ref[
            clip * height : (clip + 1) * height
        ].astype(F32)


def mix_kernel(height, gated_ref, earlier_ref, taps_ref, mixed_ref, sums_ref, wide):
    extend(earlier_ref, gated_ref, wide, height)
    lead = REACH - (KERNEL - 1)
    for clip in range(2):
        rows = slice(clip * height, (clip + 1) * height)
        first = second = jnp.zeros((height, 1), F32)
        for z in range(gated_ref.shape[1] // PAIR):
            lanes = slice(z * PAIR, (z + 1) * PAIR)
            mixed = wide[clip, lead : lead + height, lanes] * taps_ref[0:1, lanes]
            for j in range(1, KERNEL):
                mixed += wide[clip, lead + j : lead + j + height, lanes] * taps_ref[j : j + 1, lanes]
            mixed_ref[rows, lanes] = mixed
            first += jnp.sum(mixed, axis=1, keepdims=True)
            second += jnp.sum(mixed * mixed, axis=1, keepdims=True)
        sums_ref[rows] = jnp.concatenate([first, second], 1)


def mix_channels(gated, earlier, taps):
    height, channels = gated.shape[0] // 2, gated.shape[1]
    return run(
        functools.partial(mix_kernel, height), "mix_channels",
        [((2 * height, channels), F32), ((2 * height, 2), F32)],
        gated, earlier, taps,
        scratch=[pltpu.VMEM((2, height + REACH, channels), F32)],
    )


def paired(own_ref, other_ref):
    half = own_ref.shape[0] // 2
    other = other_ref[...]
    return (own_ref[...] + jnp.concatenate([other[half:], other[:half]], 0)) * (1.0 / D)


def conv_norm(mixed_ref, sums_ref, other_ref):
    means = paired(sums_ref, other_ref)
    centre, square = means[:, 0:1], means[:, 1:2]
    inverse = lax.rsqrt(square - centre * centre + EPSILON)
    return (mixed_ref[...] - centre) * inverse, inverse


def conv_out_kernel(mixed_ref, sums_ref, other_ref, affine_ref, *refs):
    chunks, active_ref, branch_ref = refs[:4], *refs[4:]
    normal, _ = conv_norm(mixed_ref, sums_ref, other_ref)
    levels = normal * affine_ref[0:1] + affine_ref[1:2]
    active = (levels * jax.nn.sigmoid(levels)).astype(BF16)
    active_ref[...] = active
    weight = heads_of(chunks, 2 * PAIR, 3 * PAIR)
    branch_ref[...] = product_nt(active, weight).astype(BF16)


def conv_forward(mixed, sums, other, affine, chunks):
    return run(
        conv_out_kernel, "conv_forward", [(mixed.shape, BF16), ((mixed.shape[0], D), BF16)],
        mixed, sums, other, affine, *chunks,
    )


def conv_level_kernel(up_ref, mixed_ref, sums_ref, other_ref, affine_ref, *refs):
    chunks, scaled_ref, totals_ref, affine_grad_ref = refs[:4], *refs[4:]
    normal, _ = conv_norm(mixed_ref, sums_ref, other_ref)
    levels = normal * affine_ref[0:1] + affine_ref[1:2]
    weight = heads_of(chunks, 2 * PAIR, 3 * PAIR)
    d_levels = product(up_ref[...], weight) * silu_slope(levels)
    scaled = d_levels * affine_ref[0:1]
    scaled_ref[...] = scaled
    totals_ref[...] = jnp.concatenate(
        [
            jnp.sum(scaled, axis=1, keepdims=True),
            jnp.sum(scaled * normal, axis=1, keepdims=True),
        ],
        1,
    )
    affine_grad_ref[0:1] = jnp.sum(d_levels * normal, axis=0, keepdims=True)
    affine_grad_ref[1:2] = jnp.sum(d_levels, axis=0, keepdims=True)


def conv_levels_back(upstream, mixed, sums, other, affine, chunks):
    return run(
        conv_level_kernel, "conv_levels_back",
        [(mixed.shape, F32), (sums.shape, F32), ((2, mixed.shape[1]), F32)],
        upstream, mixed, sums, other, affine, *chunks,
    )


def unmix_kernel(
    height, scaled_ref, totals_ref, far_totals_ref, mixed_ref, sums_ref, other_ref, taps_ref,
    d_mixed_ref, own_ref, earlier_ref, wide
):
    normal, inverse = conv_norm(mixed_ref, sums_ref, other_ref)
    means = paired(totals_ref, far_totals_ref)
    d_mixed = inverse * (scaled_ref[...] - means[:, 0:1] - normal * means[:, 1:2])
    d_mixed_ref[...] = d_mixed
    for clip in range(2):
        rows = slice(clip * height, (clip + 1) * height)
        wide[clip, :REACH] = jnp.zeros((REACH, d_mixed.shape[1]), F32)
        wide[clip, REACH : REACH + height] = d_mixed[rows]
        wide[clip, REACH + height :] = jnp.zeros((REACH, d_mixed.shape[1]), F32)
        last = REACH + KERNEL - 1
        for z in range(d_mixed.shape[1] // PAIR):
            lanes = slice(z * PAIR, (z + 1) * PAIR)
            own = wide[clip, last : last + height, lanes] * taps_ref[0:1, lanes]
            for j in range(1, KERNEL):
                own += wide[clip, last - j : last - j + height, lanes] * taps_ref[j : j + 1, lanes]
            own_ref[rows, lanes] = own
            early = wide[clip, KERNEL - 1 : KERNEL - 1 + REACH, lanes] * taps_ref[0:1, lanes]
            for j in range(1, KERNEL):
                start = KERNEL - 1 - j
                early += wide[clip, start : start + REACH, lanes] * taps_ref[j : j + 1, lanes]
            earlier_ref[clip, :, lanes] = early


def unmix_channels(scaled, totals, far_totals, mixed, sums, other, taps):
    height, channels = mixed.shape[0] // 2, mixed.shape[1]
    return run(
        functools.partial(unmix_kernel, height), "unmix_channels",
        [(mixed.shape, F32), (mixed.shape, F32), ((2, REACH, channels), F32)],
        scaled, totals, far_totals, mixed, sums, other, taps,
        scratch=[pltpu.VMEM((2, height + 2 * REACH, channels), F32)],
    )


def gate_back_kernel(height, own_ref, later_ref, value_ref, logistic_ref, live_ref, *refs):
    chunks, d_value_ref, d_gate_ref, branch_ref = refs[:4], *refs[4:]
    for clip in range(2):
        rows = slice(clip * height, (clip + 1) * height)
        own = own_ref[rows]
        low = own[height - REACH :] + later_ref[clip]
        own = jnp.concatenate([own[: height - REACH], low], 0) * live_ref[rows]
        logistic = logistic_ref[rows]
        d_value_ref[rows] = (own * logistic).astype(BF16)
        d_gate_ref[rows] = (own * value_ref[rows] * logistic * (1.0 - logistic)).astype(BF16)
    value = interleaved([d_value_ref[...], d_gate_ref[...]])
    branch_ref[...] = product_nt(value, heads_of(chunks, 0, 2 * PAIR)).astype(BF16)


def gate_back(own, later, value_half, logistic, live, chunks):
    shape = own.shape
    return run(
        functools.partial(gate_back_kernel, shape[0] // 2), "gate_back",
        [(shape, BF16), (shape, BF16), ((shape[0], D), BF16)],
        own, later, value_half, logistic, live, *chunks,
    )


def tap_kernel(height, d_mixed_ref, gated_ref, earlier_ref, taps_ref, wide):
    extend(earlier_ref, gated_ref, wide, height)
    lead = REACH - (KERNEL - 1)
    for z in range(gated_ref.shape[1] // PAIR):
        lanes = slice(z * PAIR, (z + 1) * PAIR)
        for j in range(KERNEL):
            total = jnp.zeros((1, PAIR), F32)
            for clip in range(2):
                total += jnp.sum(
                    d_mixed_ref[clip * height : (clip + 1) * height, lanes]
                    * wide[clip, lead + j : lead + j + height, lanes],
                    axis=0,
                    keepdims=True,
                )
            taps_ref[j : j + 1, lanes] = total


def tap_grads_of(d_mixed, gated, earlier):
    height, channels = gated.shape[0] // 2, gated.shape[1]
    return run(
        functools.partial(tap_kernel, height), "tap_grads", [((KERNEL, channels), F32)],
        d_mixed, gated, earlier,
        scratch=[pltpu.VMEM((2, height + REACH, channels), F32)],
    )[0]


def body(
    inputs,
    cotangent,
    lengths,
    buckets,
    ffn1_in,
    ffn1_out,
    norm_gains,
    norm_biases,
    qkv_weight,
    attn_out,
    distance,
    glu_in,
    depthwise,
    conv_gain,
    conv_bias,
    conv_out,
    ffn2_in,
    ffn2_out,
):
    rows, ctxs, tp = lax.axis_size("row"), lax.axis_size("ctx"), lax.axis_size("tp")
    second = lax.axis_index("core") == 1
    core = jnp.stack([lax.axis_index(axis) for axis in ("core", "row", "ctx", "tp")])
    core = core.astype(jnp.int32)
    local = ffn1_in.shape[0]
    height = inputs.shape[1]
    first = (lax.axis_index("ctx") * tp + lax.axis_index("tp")) * height
    attn_shares = core_shares(
        core, [qkv_weight.reshape(local, -1), attn_out], attn_out.shape[1] // 2
    )
    near, rows_in = arrive(core, inputs)
    small = [norm_gains.T, norm_biases.T, depthwise.T, conv_gain[None], conv_bias[None], distance]
    joined = gather_first([pack_below(ffn1_in, small), ffn1_out])
    attn_half = tp_first(attn_shares)
    joined, attn_half, wide_inputs = tied(joined, attn_half, widen_tp(rows_in))
    halves = gather_last(joined)
    attn_rows = tp_rest(attn_half)
    conv_shares = core_shares(core, [glu_in.reshape(local, -1), conv_out], conv_out.shape[1] // 2)
    attn_rows, halves = tied(attn_rows, halves)
    one_in, one_out = ffn_weights(halves)
    w_attn = gather_last(gather_first(attn_rows))

    lens = widen_core(lengths)
    row_ids = lax.broadcasted_iota(jnp.int32, (2 * height, 1), 0)
    frame_ids = first + jnp.where(row_ids < height, row_ids, row_ids - height)
    live = (frame_ids < jnp.where(row_ids < height, lens[0], lens[1])).astype(F32)

    table_rows, width = distance.shape[0], conv_gain.shape[0]
    selector = (jnp.arange(SPAN, dtype=jnp.int32)[:, None] == buckets[None, :]).astype(BF16)
    selector_pad = jnp.pad(selector, ((0, PAIR - SPAN), (0, PAIR - SPAN)))
    width, table_rows = conv_gain.shape[0], distance.shape[0]
    half = conv_out.shape[1] // 2
    if local % PAIR == 0:
        *norm, first_norm, rel, conv_small = unpack_all(core, one_in, selector_pad, local)
    else:
        cube = unpack_below(core, one_in, local)
        take = lambda c, k: cube[k, c]
        norms = jnp.concatenate(
            [take(c, b * rows + a)[:10, :local] for c, b, a in stream_places()], 1
        ).astype(F32)
        norm = [jnp.stack([norms[k], norms[5 + k]], 0) for k in range(5)]
        blocks = [
            crossed([take(c, k)[10:] for k in range(rows * ctxs)]) for c in range(2)
        ]
        natural = [blocks[c][b * rows + a] for c, b, a in natural_places()]
        table_all = jnp.concatenate(
            [n[KERNEL + 2 : KERNEL + 2 + table_rows, :SPAN] for n in natural], 0
        )
        conv_small = jnp.concatenate([n[: KERNEL + 2, :width] for n in natural], 1)
        half = conv_small.shape[1] // 2
        conv_small = jnp.where(second, conv_small[:, half:], conv_small[:, :half])
        first_norm = to_ffn(norm[0], "in", second)
        rel = product(table_all, selector).astype(BF16)
        rel = jnp.pad(jnp.concatenate([rel, rel], 0), ((0, 0), (0, PAIR - SPAN)))
    for mask in bits_of("tp"):
        conv_small = tp_joined(conv_small, partner(conv_small, "tp", mask), mask, 1)
    conv_small = conv_small.astype(F32)
    taps, affine = conv_small[:KERNEL], conv_small[KERNEL:]


    hidden0, before0, active0, branch = ffn_first(
        wide_inputs, first_norm, one_in, one_out
    )
    branch, conv_shares = tied(branch, conv_shares)
    conv_half = tp_first(conv_shares)
    conv_rows, w_attn = tied(tp_rest(conv_half), w_attn)
    w_conv = gather_last(gather_first(conv_rows))
    two_rows, w_conv = tied([ffn2_in, ffn2_out], w_conv)
    two_in, two_out = ffn_weights(gather_last(gather_first(two_rows)))
    stream1, hidden1 = onward(
        core, [exchange_tp(branch)], near.astype(F32), norm[1], 0.5, "out", None
    )

    hidden1 = widen_core(hidden1)
    heads = project_heads(hidden1, w_attn)
    channels = heads[0].shape[1]
    key_value = [h.reshape(2, height, channels) for h in heads[1:]]
    left = along(jnp.concatenate([h[:, height - LEFT :] for h in key_value], 2), 1)
    right = along(jnp.concatenate([h[:, :RIGHT] for h in key_value], 2), -1)
    first_ref = first.reshape(1).astype(jnp.int32)
    context, chance, branch = attend(first_ref, lens, heads, left, right, rel, w_attn)
    stream2, hidden2 = onward(core, exchange_core(branch), stream1, norm[2], 1.0, None, None)

    hidden2 = widen_core(hidden2)
    value_half, logistic, gated = gate_channels(hidden2, live, w_conv)
    earlier = along(gated.reshape(2, height, channels)[:, height - REACH :], 1)
    mixed, sums = mix_channels(gated, earlier, taps)
    other = swap_core(sums)
    active_conv, branch = conv_forward(mixed, sums, other, affine, w_conv)
    stream3, hidden3 = onward(core, exchange_core(branch), stream2, norm[3], 1.0, None, "in")

    hidden3 = widen_tp(hidden3)
    before3, active3, branch = ffn_forward(hidden3, two_in, two_out)
    result, d_stream, d_branch, grads4 = turn(
        core, [exchange_tp(branch)], stream3, cotangent, norm[4]
    )

    d_branch = widen_tp(d_branch)
    d_before, branch = ffn_backward(d_branch, before3, two_in, two_out)
    two_own, two_far = settle_open(
        ffn_halves(*ffn_grads(hidden3, d_before, d_branch, active3, two_in[0]))
    )
    d_stream, grads3, d_branch = returning(
        core, [exchange_tp(branch)], stream3, d_stream, norm[3], 1.0, "in", None
    )

    d_branch = widen_core(d_branch)
    scaled, totals, affine_grads = conv_levels_back(d_branch, mixed, sums, other, affine, w_conv)
    d_mixed, d_own, d_earlier = unmix_channels(
        scaled, totals, swap_core(totals), mixed, sums, other, taps
    )
    two_own, two_far = settle_close(two_own, two_far)
    later = along(d_earlier, -1)
    d_value, d_gate, branch = gate_back(d_own, later, value_half, logistic, live, w_conv)
    conv_grads = core_grads(hidden2, d_branch, (d_value, d_gate), active_conv, w_conv[0])
    conv_own, conv_far = settle_open(conv_grads)
    d_stream, grads2, d_branch = returning(
        core, exchange_core(branch), stream2, d_stream, norm[2], 1.0, None, None
    )

    d_branch = widen_core(d_branch)
    grad_two_in, grad_two_out = sum_pairs(two_own, two_far, F32, ffn2_in.shape)
    d_query, d_own, d_left, d_right, d_table = attend_back(
        first_ref, lens, d_branch, heads, left, right, rel, w_attn, chance
    )
    from_next, conv_far = tied(along(d_left, -1), conv_far)
    d_key, d_val, branch = heads_in(d_query, d_own, from_next, along(d_right, 1), w_attn)
    conv_own, conv_far = settle_close(conv_own, conv_far)
    attn_grads = core_grads(hidden1, d_branch, (d_query, d_key, d_val), context, w_attn[0])
    d_stream, grads1, d_branch = returning(
        core, exchange_core(branch), stream1, d_stream, norm[1], 0.5, None, "out"
    )
    attn_own, attn_far = settle_open(attn_grads)

    d_branch, attn_far = tied(widen_tp(d_branch), attn_far)
    grad_value, grad_gate, grad_w_conv = core_finish(core, conv_own, conv_far, 3)
    d_before, branch = ffn_backward(d_branch, before0, one_in, one_out)
    one_grads = ffn_grads(hidden0, d_before, d_branch, active0, one_out[0])
    one_grads, attn_far = tied(one_grads, attn_far)
    attn_own, attn_far = settle_close(attn_own, attn_far)
    one_own, one_far = settle_open(ffn_halves(*one_grads))
    pieces = exchange_tp(branch)
    grad_q, grad_k, grad_v, grad_w_attn = core_finish(core, attn_own, attn_far, 4)
    input_grad, grads0 = returning(
        core, [pieces], near, d_stream, norm[0], None, "in", None
    )
    one_own, one_far = settle_close(one_own, one_far)
    grad_one_in, grad_one_out = sum_pairs(one_own, one_far, F32, ffn1_in.shape)

    d_rel = (d_table[:HD] + d_table[HD:])[:, :SPAN]
    grad_table = jnp.dot(d_rel, selector.astype(F32).T, precision=lax.Precision.HIGHEST)
    grad_table = jnp.pad(grad_table, ((0, 0), (0, PAIR - SPAN)))
    wide = tp * half
    fold_rows = lambda v: jnp.concatenate(
        [v[:, k : k + wide] for k in range(0, v.shape[1], wide)], 0
    )
    tap_grads = tap_grads_of(d_mixed, gated, earlier)
    packed = jnp.concatenate(
        [
            tap_grads,
            affine_grads,
            grad_table.reshape(-1, wide),
            *[fold_rows(g) for g in (grads4, grads3, grads2, grads1, grads0)],
        ],
        0,
    )
    for axis, mask in [*stages_of(A_AXES), *stages_of(("tp",))]:
        packed = packed + partner(packed, axis, mask)
    far_packed = swap_core(packed)
    total = (packed + far_packed)[KERNEL + 2 :]
    table_size = grad_table.size // wide
    grad_table = total[:table_size].reshape(HD, PAIR)[:, :SPAN]
    norm_grads = total[table_size:].reshape(5, D // wide, 2, wide)
    norm_grads = norm_grads.transpose(0, 2, 1, 3).reshape(10, D)[::-1]
    conv_cut = jnp.concatenate(
        [
            jnp.where(second, far_packed, packed)[: KERNEL + 2].reshape(-1, tp, half),
            jnp.where(second, packed, far_packed)[: KERNEL + 2].reshape(-1, tp, half),
        ],
        2,
    )
    place = (lax.axis_index("row") * 2 + lax.axis_index("core")) * ctxs + lax.axis_index("ctx")
    conv_cut = lax.dynamic_index_in_dim(conv_cut, lax.axis_index("tp"), 1, keepdims=False)
    conv_cut = lax.dynamic_slice_in_dim(conv_cut, place * width, width, 1)
    grad_table = lax.dynamic_slice_in_dim(grad_table, place * table_rows, table_rows, 0)
    norm_grads = lax.dynamic_slice_in_dim(norm_grads, place * local, local, 1)

    return (
        result,
        input_grad,
        grad_one_in,
        grad_one_out,
        norm_grads[1::2].T,
        norm_grads[::2].T,
        jnp.stack([grad_q, grad_k, grad_v], 1),
        grad_w_attn,
        grad_table,
        jnp.stack([grad_value, grad_gate], 1),
        conv_cut[:KERNEL].T,
        conv_cut[KERNEL],
        conv_cut[KERNEL + 1],
        grad_w_conv,
        grad_two_in,
        grad_two_out,
    )


def solution(mesh):
    shards, ctxs, tp = (mesh.shape[axis] for axis in ("shard", "ctx", "tp"))
    cut = Mesh(mesh.devices.reshape(shards // 2, 2, ctxs, tp), ("row", "core", "ctx", "tp"))
    shard = ("row", "core")
    block = ("row", "core", "ctx")
    every = ("tp", "row", "core", "ctx")
    weight = P(block, "tp")
    narrow = P(block, None)
    deep = P(block, None, "tp")
    frames = P(shard, ("ctx", "tp"), None)
    return jax.shard_map(
        body,
        mesh=cut,
        in_specs=(
            frames, frames, P(shard), P(), weight, weight, narrow, narrow, deep, weight, narrow,
            deep, P(every, None), P(every), P(every), weight, weight, weight,
        ),
        out_specs=(
            frames, frames, weight, weight, narrow, narrow, deep, weight, narrow, deep,
            P(every, None), P(every), P(every), weight, weight, weight,
        ),
        check_vma=False,
    )
```
